256 devices in a mesh: dp: 4 (over z_lo, core), fsdp: 16 (over x, z_hi), tensor: 4 (over y).
Axes of the slice: x: 4, y: 4, z: 8 (z_hi: 4, z_lo: 2; z = z_hi * 2 + z_lo), core: 2. Of those that a mesh axis runs over, the one named last changes fastest.
Arguments:
- candidates: bfloat16 [4, 128, 64, 4096], P('dp', 'fsdp', None, 'tensor'), may hold values from -40 to 40
- cand_lengths: int32 [4, 128], P('dp', 'fsdp'), may hold values from 1 to 64, 6144 in all within a row
- pairing: int32 [4, 64, 2], P('dp'), may hold values from 0 to 127, as said below
- attn_gain: float32 [4096], replicated, may hold values from 0.1 to 1.9
- w_query: bfloat16 [4096, 4096], P('fsdp', 'tensor'), may hold values from -2 to 2
- w_key: bfloat16 [4096, 512], P('fsdp', 'tensor'), may hold values from -1 to 1
- w_value: bfloat16 [4096, 512], P('fsdp', 'tensor'), may hold values from -0.09375 to 0.09375
- w_out: bfloat16 [4096, 4096], P('tensor', 'fsdp'), may hold values from -0.09375 to 0.09375
- ffn_gain: float32 [4096], replicated, may hold values from 0.1 to 1.9
Outputs:
- resid: bfloat16 [4, 64, 128, 4096], P('dp', 'fsdp', None, 'tensor')
- normed: bfloat16 [4, 64, 128, 4096], P('dp', 'fsdp')
The draws below stay inside these ranges and needn't reach their ends.
Inputs may be any that keep to these rules, and one draw needn't show every extreme that they name: pairing[p] names each of the 128 candidates of prompt p exactly once. Candidates come in blocks of 8 consecutive indices and pair rows in blocks of 4; each block of candidates sends exactly 1 of its candidates to each of 8 blocks of pair rows.
All inputs are finite; a program needn't handle non-finite values. No bound on the sum of `cand_lengths` on one device may be relied on, other than what follows from the above.
Results may differ from the reference program's by a relative error of at most 0.018.
Values may be sent and summed in bfloat16 or wider, within the bound.
No kernel may reach another device: no remote copies, remote signals or barrier semaphores. Data moves between devices by JAX's collectives and lax.ppermute only.
A program may use at most 192 MiB of HBM per device.

```python
import math
from functools import partial
import jax
import jax.numpy as jnp
import numpy as np
from jax import lax

D = 4096
QHEADS = 32
KVHEADS = 4
HEAD = 128
SAMPLE = 64
CAND_DEV = 8
CANDS = 128
PAIRS = 64
PROMPTS = 4
N_TENSOR = 4


def shared_base(key):
    return jnp.clip(jax.random.normal(key, (D, KVHEADS * HEAD), dtype=jnp.float32), -5.0, 5.0)


def draw_candidates(key, part):
    key = jax.random.fold_in(key, 21)
    keys = jax.random.split(key, 3)
    shape = (PROMPTS, CANDS, SAMPLE, D)
    row_scale = jnp.exp(jax.random.uniform(keys[1], (PROMPTS, CANDS, SAMPLE, 1), minval=-1.15, maxval=1.15))
    col_scale = jnp.exp(jax.random.uniform(keys[2], (D,), minval=-1.15, maxval=1.15))
    base = jnp.clip(jax.random.normal(keys[0], shape), -4.0, 4.0)
    values = jnp.clip(base * row_scale * col_scale, -40.0, 40.0)
    return values.astype(jnp.bfloat16)


def draw_w_key(key, part):
    base = shared_base(key)
    key = jax.random.fold_in(key, 31)
    extra = jnp.clip(jax.random.normal(key, (D, KVHEADS * HEAD)), -5.0, 5.0)
    values = (0.8 * base + 0.6 * extra) * D ** (-0.5)
    return jnp.clip(values, -1.0, 1.0).astype(jnp.bfloat16)


def draw_w_query(key, part):
    key = jax.random.fold_in(key, 32)
    keys = jax.random.split(key, 1)
    own = jnp.clip(jax.random.normal(keys[0], (D, QHEADS * HEAD)), -5.0, 5.0)
    values = own
    return jnp.clip(values * D ** (-0.5), -2.0, 2.0).astype(jnp.bfloat16)


def draw_pairing(key, part):
    key = jax.random.fold_in(key, 41)
    devices = CANDS // CAND_DEV
    reach = min(CAND_DEV, devices)

    def one_prompt(prompt_key):
        keys = jax.random.split(prompt_key, 3)
        offsets = jax.random.permutation(keys[0], devices)[:reach]
        order_keys = jax.random.split(keys[1], devices)
        local_order = jax.vmap(partial(jax.random.permutation, x=CAND_DEV))(order_keys)
        source = jnp.arange(devices, dtype=jnp.int32)[:, None]
        target = (source + offsets[local_order % reach]) % devices
        mixing = jax.random.permutation(keys[2], CANDS)
        scores = target.reshape(-1) * CANDS + mixing
        ordered = jnp.argsort(scores, stable=True)
        return ordered.astype(jnp.int32).reshape(PAIRS, 2)
    return jax.vmap(one_prompt)(jax.random.split(key, PROMPTS))


def level_of(key, dims, cuts, smallest, largest):
    def one(axis_at, blocks):
        draws = jax.random.uniform(jax.random.fold_in(jax.random.fold_in(key, 6), axis_at), (blocks,), jnp.float32, smallest / len(cuts), largest / len(cuts))
        return jnp.repeat(jnp.exp(draws), dims[axis_at] // blocks).reshape((-1,) + (1,) * (len(dims) - axis_at - 1))

    factor_of = one(*cuts[0])
    for cut in cuts[1:]:
        factor_of = factor_of * one(*cut)
    return factor_of


def length_profile(count, total, most, slope):
    weights = [(1 << 20) // math.isqrt(grade ** slope) + 1 for grade in range(2, count + 1)]
    rest, given = total - most - (count - 1), [1] * (count - 1)
    while rest > 0:
        free = [i for i in range(count - 1) if given[i] < most]
        whole, left = sum([weights[i] for i in free]), rest
        for i in free:
            addition = min(most - given[i], max(1, left * weights[i] // whole), rest)
            given[i] = given[i] + addition
            rest = rest - addition
    return np.array([most] + given)


def ragged_sizes(rng, number_of, total, bound, skew):
    if number_of == 2:
        one = jax.random.randint(rng, (), max(1, total - bound), min(bound, total - 1) + 1)
        return jnp.stack([one, total - one])
    sizes = jnp.asarray(length_profile(number_of, total, bound, skew), jnp.int32)
    pairs = (number_of - 1) // 2
    source_of, taker = sizes[1:1 + 2 * pairs:2], sizes[2:2 + 2 * pairs:2]
    margin = jnp.minimum(source_of - 1, bound - taker)
    shifted = jax.random.randint(jax.random.fold_in(rng, 1), (pairs,), 0, 1 << 20) % (margin + 1)
    sizes = sizes.at[1:1 + 2 * pairs:2].set(source_of - shifted).at[2:2 + 2 * pairs:2].set(taker + shifted)
    return sizes[jax.random.permutation(jax.random.fold_in(rng, 2), number_of)]


def bell_draw(rng, shape, scale, bound, cuts=(), kind=jnp.bfloat16):
    result = jax.random.normal(rng, shape, jnp.float32) * scale
    if len(cuts) > 0:
        result = level_of(rng, shape, cuts, -0.22, 0.18) * result
    return jnp.clip(result, min=-bound, max=bound).astype(kind)


def setup_inputs(seed: int = 0) -> dict:
    key_of = jax.random.split(jax.random.key(seed), 10)
    candidates = draw_candidates(jax.random.fold_in(key_of[9], 71), 0)
    cand_lengths = jax.vmap(lambda own: ragged_sizes(own, CANDS, CANDS * SAMPLE * 3 // 4, SAMPLE, 1))(jax.random.split(key_of[1], PROMPTS)).reshape((PROMPTS, CANDS)).astype(jnp.int32)
    pairing = draw_pairing(jax.random.fold_in(key_of[9], 71), 0)
    attn_gain = jnp.clip(1.0 + 0.18 * jax.random.normal(key_of[3], (D,), jnp.float32), 0.1, 1.9)
    w_query = draw_w_query(jax.random.fold_in(key_of[9], 71), 0)
    w_key = draw_w_key(jax.random.fold_in(key_of[9], 71), 0)
    w_value = bell_draw(key_of[6], (D, KVHEADS * HEAD), D ** -0.5, 0.09375, ((0, 16), (1, 4)))
    w_out = bell_draw(key_of[7], (QHEADS * HEAD, D), (QHEADS * HEAD) ** -0.5, 0.09375, ((0, 4), (1, 16)))
    ffn_gain = jnp.clip(1.0 + 0.18 * jax.random.normal(key_of[8], (D,), jnp.float32), 0.1, 1.9)
    return {"candidates": candidates, "cand_lengths": cand_lengths, "pairing": pairing, "attn_gain": attn_gain, "w_query": w_query, "w_key": w_key, "w_value": w_value, "w_out": w_out, "ffn_gain": ffn_gain}


epsilon = 1e-05
rope_base = 500000.0

def rms_scale(values, gain):
    mean_square = lax.optimization_barrier(jnp.mean(values * values, axis=-1, keepdims=True))
    return values * lax.rsqrt(mean_square + epsilon) * gain

def positions_of(lengths, sample):
    slot_steps = jnp.arange(2 * sample, dtype=jnp.int32)
    return jnp.where(slot_steps < sample, slot_steps, lengths[..., :1] + slot_steps - sample)

def key_mask(lengths, sample):
    slot_steps = jnp.arange(2 * sample, dtype=jnp.int32)
    local_step = jnp.where(slot_steps < sample, slot_steps, slot_steps - sample)
    limit = jnp.where(slot_steps < sample, lengths[..., :1], lengths[..., 1:])
    valid = local_step < limit
    causal = slot_steps[None, :] <= slot_steps[:, None]
    return causal[None] & valid[:, None, :]

def rotate(values, positions, head_size):
    half = head_size // 2
    inv_freq = rope_base ** (-jnp.arange(half, dtype=jnp.float32) * 2.0 / head_size)
    angles = positions.astype(jnp.float32)[..., None] * inv_freq
    cosine = jnp.cos(angles)[..., None, :]
    sine_table = jnp.sin(angles)[..., None, :]
    lower = values[..., :half]
    upper = values[..., half:]
    return jnp.concatenate([lower * cosine - upper * sine_table, upper * cosine + lower * sine_table], axis=-1)

def attend(query, key_rows, value_rows, allowed):
    pair_rows, row_count, kv_count, group_size, head_size = query.shape
    scores = jnp.einsum('bqkgd,bskd->bkgqs', query.astype(jnp.float32), key_rows.astype(jnp.float32)) * head_size ** (-0.5)
    scores = jnp.where(allowed[:, None, None], scores, -1e+30)
    row_peak = lax.optimization_barrier(jnp.max(scores, axis=-1, keepdims=True))
    weights = jnp.exp(scores - row_peak)
    prob_rows = (weights / lax.optimization_barrier(jnp.sum(weights, axis=-1, keepdims=True))).astype(jnp.bfloat16)
    mixed_rows = jnp.einsum('bkgqs,bskd->bqkgd', prob_rows.astype(jnp.float32), value_rows.astype(jnp.float32))
    return mixed_rows.astype(jnp.bfloat16).reshape(pair_rows, row_count, kv_count * group_size * head_size)

def reference(candidates, cand_lengths, pairing, attn_gain, w_query, w_key, w_value, w_out, ffn_gain):

    def one_prompt(packed):
        cand_rows, lengths, pair_table = packed
        pair_count = pair_table.shape[0]
        sample = cand_rows.shape[1]
        width = cand_rows.shape[2]
        chosen = pair_table.reshape(-1).astype(jnp.int32)
        joined = jnp.take(cand_rows, chosen, axis=0).reshape(pair_count, 2 * sample, width)
        row_lengths = jnp.take(lengths, chosen, axis=0).reshape(pair_count, 2)
        inputs = joined.astype(jnp.float32).reshape(-1, width)
        normal_rows = rms_scale(inputs, attn_gain).astype(jnp.bfloat16)
        query = jnp.dot(normal_rows, w_query, preferred_element_type=jnp.float32)
        key_rows = jnp.dot(normal_rows, w_key, preferred_element_type=jnp.float32)
        value_rows = jnp.dot(normal_rows, w_value, preferred_element_type=jnp.float32)
        positions = positions_of(row_lengths, sample)
        query = rotate(query.reshape(pair_count, 2 * sample, QHEADS, HEAD), positions, HEAD).astype(jnp.bfloat16)
        key_rows = rotate(key_rows.reshape(pair_count, 2 * sample, KVHEADS, HEAD), positions, HEAD).astype(jnp.bfloat16)
        value_rows = value_rows.astype(jnp.bfloat16).reshape(pair_count, 2 * sample, KVHEADS, HEAD)
        query = query.reshape(pair_count, 2 * sample, KVHEADS, QHEADS // KVHEADS, HEAD)
        mixed = attend(query, key_rows, value_rows, key_mask(row_lengths, sample)).reshape(-1, QHEADS * HEAD)
        group_cols = QHEADS * HEAD // N_TENSOR
        branch = jnp.zeros((mixed.shape[0], width), jnp.float32)
        for group in range(N_TENSOR):
            term = jnp.dot(mixed[:, group * group_cols:(group + 1) * group_cols], w_out[group * group_cols:(group + 1) * group_cols], preferred_element_type=jnp.float32)
            rounded = lax.optimization_barrier(term.astype(jnp.bfloat16))
            branch = branch + rounded.astype(jnp.float32)
        stream = inputs + branch
        resid = stream.astype(jnp.bfloat16).reshape(pair_count, 2 * sample, width)
        normed = rms_scale(stream, ffn_gain).astype(jnp.bfloat16).reshape(pair_count, 2 * sample, width)
        return (resid, normed)
    resid, normed = lax.map(one_prompt, (candidates, cand_lengths, pairing))
    return (resid, normed)
```

```python
import jax
import jax.numpy as jnp
from jax import lax
from jax.experimental import pallas as pl
from jax.experimental.pallas import tpu as pltpu
from jax.sharding import PartitionSpec as P

HEAD = 128
SAMPLE = 64
TENSOR = 4
RING = 4
LANES = 1024
PIECE = 256
epsilon = 1e-05
rope_base = 500000.0
BF = jnp.bfloat16
F32 = jnp.float32
VMEM_LIMIT = 40 * 1024 * 1024


def wrap(value):
    return lax.rem(value + 2 * RING, RING)


def in_vmem():
    return pl.BlockSpec(memory_space=pltpu.VMEM)


def in_smem():
    return pl.BlockSpec(memory_space=pltpu.SMEM)


def params(**kw):
    return pltpu.CompilerParams(vmem_limit_bytes=VMEM_LIMIT, **kw)


def pack_kernel(pick_ref, cand_ref, first_ref, second_ref):
    half = SAMPLE // 2
    for slot in range(first_ref.shape[0]):
        own = pick_ref[slot]
        first_ref[slot] = cand_ref[own, :half, :]
        second_ref[slot] = cand_ref[own, half:, :]


def pack(pick, cands, slots):
    shape = jax.ShapeDtypeStruct((slots, SAMPLE // 2, cands.shape[2]), BF)
    return pl.pallas_call(
        pack_kernel,
        out_shape=(shape, shape),
        in_specs=[in_smem(), in_vmem()],
        out_specs=(in_vmem(), in_vmem()),
        compiler_params=params(),
        name="pack",
    )(pick, cands)


def unpack_kernel(source_ref, slots_ref, rows_ref):
    half = slots_ref.shape[1]
    for cand in range(source_ref.shape[0]):
        rows_ref[cand * half : (cand + 1) * half, :] = slots_ref[source_ref[cand]]


def unpack(source, slots):
    return pl.pallas_call(
        unpack_kernel,
        out_shape=jax.ShapeDtypeStruct((source.shape[0] * slots.shape[1], slots.shape[2]), BF),
        in_specs=[in_smem(), in_vmem()],
        out_specs=in_vmem(),
        compiler_params=params(),
        name="unpack",
    )(source, slots)


def place_of(place_ref):
    x, z, y, core = place_ref[0], place_ref[1], place_ref[2], place_ref[3]
    return x, z, y, core, 1 - 2 * core


def lane_block(index, width):
    return pl.ds(pl.multiple_of(index * width, width), width)


def project_kernel(place_ref, *refs):
    rows_refs = refs[:4]
    gain_ref, cos_ref, sin_ref = refs[4:7]
    own_refs, other_refs = refs[7:15], refs[15:23]
    query_ref, key_ref, value_ref = refs[23:26]
    own_rows, other_rows, result = refs[26:29]
    x, z, y, core, way = place_of(place_ref)
    squares = jnp.zeros((rows_refs[0].shape[0], 1), F32)
    for r in range(RING):
        block = wrap(y - r * way)
        s = wrap((x - block) * way)
        for m in range(RING):
            part = wrap(z - m * way)
            piece = rows_refs[r][:, lane_block(part, PIECE)].astype(F32)
            squares = squares + jnp.sum(piece * piece, axis=-1, keepdims=True)
            gain = gain_ref[:, lane_block(block * RING + part, PIECE)]
            own_rows[:, lane_block(s * RING + m, PIECE)] = (piece * gain).astype(BF)
    for s in range(RING):
        for m in range(RING):
            at = (s * RING + m) * PIECE
            back = ((RING - s) % RING * RING + (RING - m) % RING) * PIECE
            other_rows[:, at : at + PIECE] = own_rows[:, back : back + PIECE]
    wide = own_refs[0].shape[2]
    depth = 2 * PIECE
    for rows, weights, side in ((own_rows, own_refs, core), (other_rows, other_refs, 1 - core)):
        total = None
        for g in range(2 * RING):
            term = jnp.dot(
                rows[:, g * depth : (g + 1) * depth],
                weights[g][...].reshape(depth, wide),
                preferred_element_type=F32,
            )
            total = term if total is None else total + term
        result[:, pl.ds(pl.multiple_of(side * wide, HEAD), wide)] = total
    scale = lax.rsqrt(squares * (1.0 / (TENSOR * LANES)) + epsilon)
    cosine, sine = cos_ref[...], sin_ref[...]
    heads = query_ref.shape[1] // HEAD
    for h in range(heads + 1):
        values = result[:, h * HEAD : (h + 1) * HEAD] * scale
        turned = (values * cosine + pltpu.roll(values, HEAD // 2, 1) * sine).astype(BF)
        if h < heads:
            query_ref[:, h * HEAD : (h + 1) * HEAD] = turned
        else:
            key_ref[...] = turned
    value_ref[...] = (result[:, (heads + 1) * HEAD :] * scale).astype(BF)


def project(place, rows, gain, cosine, sine, own, other):
    count = rows[0].shape[0]
    width = rows[0].shape[1]
    return pl.pallas_call(
        project_kernel,
        out_shape=(
            jax.ShapeDtypeStruct((count, width), BF),
            jax.ShapeDtypeStruct((count, HEAD), BF),
            jax.ShapeDtypeStruct((count, HEAD), BF),
        ),
        in_specs=[in_smem()] + [in_vmem()] * 23,
        out_specs=(in_vmem(),) * 3,
        scratch_shapes=[
            pltpu.VMEM((count, TENSOR * width), BF),
            pltpu.VMEM((count, TENSOR * width), BF),
            pltpu.VMEM((count, width + 2 * HEAD), F32),
        ],
        compiler_params=params(),
        name="project",
    )(place, *rows, gain, cosine, sine, *own, *other)


def attend_kernel(first_pair, pairs, place_ref, lens_ref, *refs):
    q0, q1, k0, k1, v0, v1 = refs[:6]
    own_refs, other_refs = refs[6:14], refs[14:22]
    out_refs = refs[22:26]
    mixed, terms = refs[26:28]
    x, z, y, core, way = place_of(place_ref)
    half = SAMPLE // 2
    slots = 2 * SAMPLE
    heads = q0.shape[1] // HEAD
    step_t = lax.broadcasted_iota(jnp.int32, (slots, slots), 0)
    step_u = lax.broadcasted_iota(jnp.int32, (slots, slots), 1)
    for p in range(pairs):
        at = (first_pair + p) * SAMPLE

        def joined(lo, hi):
            return jnp.concatenate(
                [
                    lo[at : at + half, :],
                    hi[at : at + half, :],
                    lo[at + half : at + SAMPLE, :],
                    hi[at + half : at + SAMPLE, :],
                ],
                axis=0,
            )

        query, key, value = joined(q0, q1), joined(k0, k1), joined(v0, v1)
        stacked = jnp.concatenate(
            [query[:, h * HEAD : (h + 1) * HEAD] for h in range(heads)], axis=0
        )
        scores = lax.dot_general(
            stacked, key, (((1,), (1,)), ((), ())), preferred_element_type=F32
        ) * (HEAD**-0.5)
        len_a = lens_ref[2 * (first_pair + p)]
        len_b = lens_ref[2 * (first_pair + p) + 1]
        limit = jnp.where(step_u < SAMPLE, len_a, len_b + SAMPLE)
        limit = jnp.minimum(limit, step_t + 1)
        closed = jnp.where(step_u < limit, 0.0, -1e30).astype(F32)
        scores = scores.reshape(heads, slots, slots) + closed[None]
        peak = jnp.max(scores, axis=-1, keepdims=True)
        weights = jnp.exp(scores - peak)
        probs = weights / jnp.sum(weights, axis=-1, keepdims=True)
        out = jnp.dot(
            probs.astype(BF).reshape(heads * slots, slots), value, preferred_element_type=F32
        ).astype(BF)
        for h in range(heads):
            mixed[p * slots : (p + 1) * slots, h * HEAD : (h + 1) * HEAD] = out[
                h * slots : (h + 1) * slots
            ]
    depth = own_refs[0].shape[1]
    mine = mixed[:, lane_block(core, depth)]
    theirs = mixed[:, lane_block(1 - core, depth)]
    for s in range(RING):
        owner = wrap(x - s * way)
        r = wrap((y - owner) * way)
        for m in range(RING):
            part = wrap(z - m * way)
            s2, m2 = (RING - s) % RING, (RING - m) % RING
            term = jnp.dot(mine, own_refs[2 * s + m // 2][m % 2], preferred_element_type=F32)
            term = term + jnp.dot(
                theirs, other_refs[2 * s2 + m2 // 2][m2 % 2], preferred_element_type=F32
            )
            terms[r, :, lane_block(part, PIECE)] = term.astype(BF)
    for r in range(RING):
        out_refs[r][...] = terms[r]


def attend(first_pair, pairs, place, lens, chunks, own, other):
    count = pairs * 2 * SAMPLE
    width = chunks[0].shape[1]

    def kernel(*refs):
        attend_kernel(first_pair, pairs, *refs)

    return pl.pallas_call(
        kernel,
        out_shape=(jax.ShapeDtypeStruct((count, width), BF),) * RING,
        in_specs=[in_smem(), in_smem()] + [in_vmem()] * 22,
        out_specs=(in_vmem(),) * RING,
        scratch_shapes=[
            pltpu.VMEM((count, width), BF),
            pltpu.VMEM((RING, count, width), BF),
        ],
        compiler_params=params(),
        name="attend",
    )(place, lens, *chunks, *own, *other)


def finish_kernel(place_ref, gain_ref, b0, b1, b2, b3, *rest):
    out_ref = rest[-1]
    _, _, y, _, way = place_of(place_ref)
    values = [b[...].astype(F32) for b in (b0, b1, b2, b3)]
    squares = sum(jnp.sum(v * v, axis=-1, keepdims=True) for v in values)
    scale = lax.rsqrt(squares * (1.0 / (TENSOR * LANES)) + epsilon)
    for r in range(RING):
        lanes = lane_block(wrap(y - r * way), LANES)
        out_ref[:, lanes] = (values[r] * scale * gain_ref[:, lanes]).astype(BF)


def finish(place, gain, blocks, before, chunk, total):
    count, width = blocks[0].shape
    tile = 2 * SAMPLE
    steps = count // tile
    specs = [
        in_smem(),
        pl.BlockSpec((1, TENSOR * width), lambda i: (0, 0)),
    ] + [pl.BlockSpec((tile, width), lambda i: (i, 0))] * RING
    args = [place, gain, *blocks]
    aliases = {}
    if before is not None:
        specs.append(pl.BlockSpec(memory_space=pl.ANY))
        aliases = {len(args): 0}
        args.append(before)
    return pl.pallas_call(
        finish_kernel,
        grid=(steps,),
        out_shape=jax.ShapeDtypeStruct((total, TENSOR * width), BF),
        in_specs=specs,
        out_specs=pl.BlockSpec((tile, TENSOR * width), lambda i: (i + chunk * steps, 0)),
        input_output_aliases=aliases,
        compiler_params=params(),
        name="finish",
    )(*args)


def way_of(dp):
    return 1 - 2 * (dp % 2)


def along_y(values):
    pairs = [
        (dp * TENSOR + y, dp * TENSOR + (y + way_of(dp)) % TENSOR)
        for dp in range(4)
        for y in range(TENSOR)
    ]
    return lax.ppermute(values, ("dp", "tensor"), pairs)


def along_x(values):
    pairs = [
        (dp * 16 + x * 4 + z, dp * 16 + (x + way_of(dp)) % 4 * 4 + z)
        for dp in range(4)
        for x in range(4)
        for z in range(4)
    ]
    return lax.ppermute(values, ("dp", "fsdp"), pairs)


def along_z(values):
    pairs = [
        (dp * 16 + x * 4 + z, dp * 16 + x * 4 + (z + way_of(dp)) % 4)
        for dp in range(4)
        for x in range(4)
        for z in range(4)
    ]
    return lax.ppermute(values, ("dp", "fsdp"), pairs)


def other_core(values):
    return lax.ppermute(values, "dp", [(dp, dp ^ 1) for dp in range(4)])


def gather_weight(piece):
    rounds = [piece]
    for _ in range(3):
        rounds.append(along_z(rounds[-1]))
    own = [None] * 8
    for g in range(2):
        block = jnp.stack(rounds[2 * g : 2 * g + 2])
        for s in range(4):
            own[2 * s + g] = block
            if s < 3:
                block = along_x(block)
    return own, [other_core(block) for block in own]


def on_device(
    candidates, cand_lengths, pairing, attn_gain, w_query, w_key, w_value, w_out, ffn_gain
):
    me = lax.axis_index("fsdp")
    y = lax.axis_index("tensor")
    core = lax.rem(lax.axis_index("dp"), 2)
    place = jnp.stack([me // 4, lax.rem(me, 4), y, core]).astype(jnp.int32)
    cand_dev = candidates.shape[1]
    devices = lax.axis_size("fsdp")
    flat = pairing[0].reshape(devices, cand_dev)
    pick = jnp.sum(jnp.where(flat // cand_dev == me, lax.rem(flat, cand_dev), 0), axis=1)
    wanted = lax.dynamic_index_in_dim(flat, me, 0, keepdims=False)
    source = wanted // cand_dev

    lens_all = lax.all_gather(cand_lengths[0], "fsdp", axis=0, tiled=True)
    every = jnp.arange(devices * cand_dev, dtype=jnp.int32)
    lens = jnp.sum(jnp.where(wanted[:, None] == every[None, :], lens_all[None, :], 0), axis=1)

    packed = pack(pick, candidates[0], devices)

    half_cols = (w_query.shape[1] + w_key.shape[1] + w_value.shape[1]) // 2
    first = w_query[:, :half_cols]
    second = jnp.concatenate([w_query[:, half_cols:], w_key, w_value], axis=1)
    qkv_piece = jnp.where(core == 0, first, second)
    depth = w_out.shape[0] // 2
    out_piece = lax.dynamic_slice_in_dim(w_out, core * depth, depth, 0)
    qkv_own, qkv_other = gather_weight(qkv_piece)
    out_own, out_other = gather_weight(out_piece)

    gain_in = attn_gain.reshape(1, -1)
    gain_out = ffn_gain.reshape(1, -1)
    half = SAMPLE // 2
    freq = rope_base ** (-jnp.arange(HEAD // 2, dtype=F32) * 2.0 / HEAD)
    before = jnp.where(
        jnp.arange(cand_dev) % 2 == 0, 0, jnp.roll(lens, 1)
    )
    chunks = []
    local = []
    for c in range(2):
        incoming = lax.all_to_all(packed[c], "fsdp", split_axis=0, concat_axis=0, tiled=True)
        rows = unpack(source, incoming)
        local.append(rows)
        ring = [rows]
        for _ in range(3):
            ring.append(along_y(ring[-1]))
        positions = before[:, None] + c * half + jnp.arange(half, dtype=jnp.int32)[None, :]
        angles = positions.reshape(-1, 1).astype(F32) * freq[None, :]
        cosine, sine = jnp.cos(angles), jnp.sin(angles)
        cosine = jnp.concatenate([cosine, cosine], axis=1)
        sine = jnp.concatenate([-sine, sine], axis=1)
        chunks.append(project(place, ring, gain_in, cosine, sine, qkv_own, qkv_other))
    flat_chunks = [chunks[c][i] for i in range(3) for c in range(2)]
    width = candidates.shape[3]
    total = cand_dev * SAMPLE
    rows_all = jnp.concatenate(
        [r.reshape(cand_dev, half, width) for r in local], axis=1
    ).reshape(total, width)

    parts = 2
    pairs = cand_dev // 2 // parts
    size = total // parts
    normed = None
    resids = []
    for c in range(parts):
        terms = attend(c * pairs, pairs, place, lens, flat_chunks, out_own, out_other)
        moving = along_y(terms[1])
        for r in (2, 3):
            moving = along_y((moving.astype(F32) + terms[r].astype(F32)).astype(BF))
        stream = (
            rows_all[c * size : (c + 1) * size].astype(F32)
            + terms[0].astype(F32)
            + moving.astype(F32)
        )
        blocks = [stream.astype(BF)]
        for _ in range(3):
            blocks.append(along_y(blocks[-1]))
        resids.append(blocks[0])
        normed = finish(place, gain_out, blocks, normed, c, total)
    resid = jnp.concatenate(resids, axis=0)
    pair_dev = cand_dev // 2
    return (
        resid.reshape(1, pair_dev, 2 * SAMPLE, width),
        normed.reshape(1, pair_dev, 2 * SAMPLE, TENSOR * width),
    )


def solution(mesh):
    return jax.shard_map(
        on_device,
        mesh=mesh,
        in_specs=(
            P("dp", "fsdp", None, "tensor"),
            P("dp", "fsdp"),
            P("dp", None, None),
            P(),
            P("fsdp", "tensor"),
            P("fsdp", "tensor"),
            P("fsdp", "tensor"),
            P("tensor", "fsdp"),
            P(),
        ),
        out_specs=(P("dp", "fsdp", None, "tensor"), P("dp", "fsdp", None, None)),
        check_vma=False,
    )
```

```python
import jax
import jax.numpy as jnp
from jax import lax
from jax.experimental import pallas as pl
from jax.experimental.pallas import tpu as pltpu
from jax.sharding import PartitionSpec as P

HEAD = 128
SAMPLE = 64
TENSOR = 4
RING = 4
LANES = 1024
PIECE = 256
EXTRA = 16
epsilon = 1e-05
rope_base = 500000.0
BF = jnp.bfloat16
F32 = jnp.float32
VMEM_LIMIT = 40 * 1024 * 1024


def wrap(value):
    return lax.rem(value + 2 * RING, RING)


def in_vmem():
    return pl.BlockSpec(memory_space=pltpu.VMEM)


def in_smem():
    return pl.BlockSpec(memory_space=pltpu.SMEM)


def params(**kw):
    return pltpu.CompilerParams(vmem_limit_bytes=VMEM_LIMIT, **kw)


def pack_kernel(pick_ref, lens_ref, cand_ref, _, slots_ref):
    blocks = cand_ref.shape[2] // HEAD
    for slot in range(slots_ref.shape[0]):
        own = pick_ref[slot]
        for b in range(blocks):
            slots_ref[slot, b * SAMPLE : (b + 1) * SAMPLE, :] = cand_ref[
                own, :, b * HEAD : (b + 1) * HEAD
            ]
        length = jnp.full((EXTRA, HEAD), lens_ref[own], jnp.int32).astype(F32)
        slots_ref[slot, blocks * SAMPLE :, :] = length.astype(BF)


def pack(pick, lens, cands, earlier, slots):
    rows = cands.shape[2] // HEAD * SAMPLE + EXTRA
    return pl.pallas_call(
        pack_kernel,
        out_shape=jax.ShapeDtypeStruct((slots, rows, HEAD), BF),
        in_specs=[in_smem(), in_smem(), in_vmem(), pl.BlockSpec(memory_space=pl.ANY)],
        out_specs=in_vmem(),
        compiler_params=params(),
        name="pack",
    )(pick, lens, cands, earlier)


def unpack_kernel(source_ref, slots_ref, *rows_refs):
    blocks = rows_refs[0].shape[1] // HEAD
    per = source_ref.shape[0] // len(rows_refs)
    for cand in range(source_ref.shape[0]):
        at = cand % per * SAMPLE
        for b in range(blocks):
            rows_refs[cand // per][at : at + SAMPLE, b * HEAD : (b + 1) * HEAD] = slots_ref[
                source_ref[cand], b * SAMPLE : (b + 1) * SAMPLE, :
            ]


def unpack(source, slots, parts):
    width = (slots.shape[1] - EXTRA) // SAMPLE * HEAD
    rows = source.shape[0] * SAMPLE // parts
    return pl.pallas_call(
        unpack_kernel,
        out_shape=(jax.ShapeDtypeStruct((rows, width), BF),) * parts,
        in_specs=[in_smem(), in_vmem()],
        out_specs=(in_vmem(),) * parts,
        compiler_params=params(),
        name="unpack",
    )(source, slots)


def place_of(place_ref):
    x, z, y, core = place_ref[0], place_ref[1], place_ref[2], place_ref[3]
    return x, z, y, core, 1 - 2 * core


def lane_block(index, width):
    return pl.ds(pl.multiple_of(index * width, width), width)


def project_kernel(place_ref, *refs):
    rows_refs = refs[:4]
    gain_ref, cos_ref, sin_ref = refs[4:7]
    own_refs, other_refs = refs[7:15], refs[15:23]
    query_ref, key_ref, value_ref = refs[23:26]
    own_rows, other_rows, result = refs[26:29]
    x, z, y, core, way = place_of(place_ref)
    squares = jnp.zeros((rows_refs[0].shape[0], 1), F32)
    for r in range(RING):
        block = wrap(y - r * way)
        s = wrap((x - block) * way)
        for m in range(RING):
            part = wrap(z - m * way)
            piece = rows_refs[r][:, lane_block(part, PIECE)].astype(F32)
            squares = squares + jnp.sum(piece * piece, axis=-1, keepdims=True)
            gain = gain_ref[:, lane_block(block * RING + part, PIECE)]
            own_rows[:, lane_block(s * RING + m, PIECE)] = (piece * gain).astype(BF)
    for s in range(RING):
        for m in range(RING):
            at = (s * RING + m) * PIECE
            back = ((RING - s) % RING * RING + (RING - m) % RING) * PIECE
            other_rows[:, at : at + PIECE] = own_rows[:, back : back + PIECE]
    wide = own_refs[0].shape[2]
    depth = 2 * PIECE
    for rows, weights, side in ((own_rows, own_refs, core), (other_rows, other_refs, 1 - core)):
        total = None
        for g in range(2 * RING):
            term = jnp.dot(
                rows[:, g * depth : (g + 1) * depth],
                weights[g][...].reshape(depth, wide),
                preferred_element_type=F32,
            )
            total = term if total is None else total + term
        result[:, pl.ds(pl.multiple_of(side * wide, HEAD), wide)] = total
    scale = lax.rsqrt(squares * (1.0 / (TENSOR * LANES)) + epsilon)
    cosine, sine = cos_ref[...], sin_ref[...]
    heads = query_ref.shape[1] // HEAD
    for h in range(heads + 1):
        values = result[:, h * HEAD : (h + 1) * HEAD] * scale
        turned = (values * cosine + pltpu.roll(values, HEAD // 2, 1) * sine).astype(BF)
        if h < heads:
            query_ref[:, h * HEAD : (h + 1) * HEAD] = turned
        else:
            key_ref[...] = turned
    value_ref[...] = (result[:, (heads + 1) * HEAD :] * scale).astype(BF)


def project(place, rows, gain, cosine, sine, own, other):
    count = rows[0].shape[0]
    width = rows[0].shape[1]
    return pl.pallas_call(
        project_kernel,
        out_shape=(
            jax.ShapeDtypeStruct((count, width), BF),
            jax.ShapeDtypeStruct((count, HEAD), BF),
            jax.ShapeDtypeStruct((count, HEAD), BF),
        ),
        in_specs=[in_smem()] + [in_vmem()] * 23,
        out_specs=(in_vmem(),) * 3,
        scratch_shapes=[
            pltpu.VMEM((count, TENSOR * width), BF),
            pltpu.VMEM((count, TENSOR * width), BF),
            pltpu.VMEM((count, width + 2 * HEAD), F32),
        ],
        compiler_params=params(),
        name="project",
    )(place, *rows, gain, cosine, sine, *own, *other)


def attend_kernel(first_pair, pairs, place_ref, lens_ref, q_ref, k_ref, v_ref, *refs):
    own_ref, other_ref = refs[:2]
    out_refs = refs[2:6]
    mixed, terms = refs[6:8]
    _, _, y, core, way = place_of(place_ref)
    slots = 2 * SAMPLE
    heads = q_ref.shape[1] // HEAD
    step_t = lax.broadcasted_iota(jnp.int32, (slots, slots), 0)
    step_u = lax.broadcasted_iota(jnp.int32, (slots, slots), 1)
    for p in range(pairs):
        at = slice(p * slots, (p + 1) * slots)
        stacked = jnp.concatenate(
            [q_ref[at, h * HEAD : (h + 1) * HEAD] for h in range(heads)], axis=0
        )
        scores = lax.dot_general(
            stacked, k_ref[at, :], (((1,), (1,)), ((), ())), preferred_element_type=F32
        ) * (HEAD**-0.5)
        len_a = lens_ref[2 * (first_pair + p)]
        len_b = lens_ref[2 * (first_pair + p) + 1]
        limit = jnp.where(step_u < SAMPLE, len_a, len_b + SAMPLE)
        limit = jnp.minimum(limit, step_t + 1)
        closed = jnp.where(step_u < limit, 0.0, -1e30).astype(F32)
        scores = scores.reshape(heads, slots, slots) + closed[None]
        peak = jnp.max(scores, axis=-1, keepdims=True)
        weights = jnp.exp(scores - peak)
        probs = weights / jnp.sum(weights, axis=-1, keepdims=True)
        out = jnp.dot(
            probs.astype(BF).reshape(heads * slots, slots),
            v_ref[at, :],
            preferred_element_type=F32,
        ).astype(BF)
        for h in range(heads):
            mixed[at, h * HEAD : (h + 1) * HEAD] = out[h * slots : (h + 1) * slots]
    count, depth, wide = own_ref.shape
    mine = mixed[:, lane_block(core, depth)]
    theirs = mixed[:, lane_block(1 - core, depth)]
    for f in range(count):
        r = wrap((y - f // RING) * way)
        term = jnp.dot(mine, own_ref[f], preferred_element_type=F32)
        term = term + jnp.dot(theirs, other_ref[f], preferred_element_type=F32)
        part = f % RING * wide
        terms[r, :, part : part + wide] = term.astype(BF)
    for r in range(RING):
        out_refs[r][...] = terms[r]


def attend(first_pair, pairs, place, lens, qkv, own, other):
    count = pairs * 2 * SAMPLE
    width = qkv[0].shape[1]

    def kernel(*refs):
        attend_kernel(first_pair, pairs, *refs)

    return pl.pallas_call(
        kernel,
        out_shape=(jax.ShapeDtypeStruct((count, width), BF),) * RING,
        in_specs=[in_smem(), in_smem()] + [in_vmem()] * 5,
        out_specs=(in_vmem(),) * RING,
        scratch_shapes=[
            pltpu.VMEM((count, width), BF),
            pltpu.VMEM((RING, count, width), BF),
        ],
        compiler_params=params(),
        name="attend",
    )(place, lens, *qkv, own, other)


def finish_kernel(place_ref, gain_ref, b0, b1, b2, b3, *rest):
    out_ref = rest[-1]
    _, _, y, _, way = place_of(place_ref)
    values = [b[...].astype(F32) for b in (b0, b1, b2, b3)]
    squares = sum(jnp.sum(v * v, axis=-1, keepdims=True) for v in values)
    scale = lax.rsqrt(squares * (1.0 / (TENSOR * LANES)) + epsilon)
    for r in range(RING):
        lanes = lane_block(wrap(y - r * way), LANES)
        out_ref[:, lanes] = (values[r] * scale * gain_ref[:, lanes]).astype(BF)


def finish(place, gain, blocks, before, chunk, total):
    count, width = blocks[0].shape
    tile = 2 * SAMPLE
    steps = count // tile
    specs = [
        in_smem(),
        pl.BlockSpec((1, TENSOR * width), lambda i: (0, 0)),
    ] + [pl.BlockSpec((tile, width), lambda i: (i, 0))] * RING
    args = [place, gain, *blocks]
    aliases = {}
    if before is not None:
        specs.append(pl.BlockSpec(memory_space=pl.ANY))
        aliases = {len(args): 0}
        args.append(before)
    return pl.pallas_call(
        finish_kernel,
        grid=(steps,),
        out_shape=jax.ShapeDtypeStruct((total, TENSOR * width), BF),
        in_specs=specs,
        out_specs=pl.BlockSpec((tile, TENSOR * width), lambda i: (i + chunk * steps, 0)),
        input_output_aliases=aliases,
        compiler_params=params(),
        name="finish",
    )(*args)


def after(value, *others):
    anywhere = pl.BlockSpec(memory_space=pl.ANY)
    return pl.pallas_call(
        lambda *refs: None,
        out_shape=jax.ShapeDtypeStruct(value.shape, value.dtype),
        in_specs=[anywhere] * (1 + len(others)),
        out_specs=anywhere,
        input_output_aliases={0: 0},
        name="after",
    )(value, *others)


def way_of(dp):
    return 1 - 2 * (dp % 2)


def along_y(values):
    pairs = [
        (dp * TENSOR + y, dp * TENSOR + (y + way_of(dp)) % TENSOR)
        for dp in range(4)
        for y in range(TENSOR)
    ]
    return lax.ppermute(values, ("dp", "tensor"), pairs)


def along_x(values):
    pairs = [
        (dp * 16 + x * 4 + z, dp * 16 + (x + way_of(dp)) % 4 * 4 + z)
        for dp in range(4)
        for x in range(4)
        for z in range(4)
    ]
    return lax.ppermute(values, ("dp", "fsdp"), pairs)


def along_z(values):
    pairs = [
        (dp * 16 + x * 4 + z, dp * 16 + x * 4 + (z + way_of(dp)) % 4)
        for dp in range(4)
        for x in range(4)
        for z in range(4)
    ]
    return lax.ppermute(values, ("dp", "fsdp"), pairs)


def other_core(values):
    return lax.ppermute(values, "dp", [(dp, dp ^ 1) for dp in range(4)])


def spread_x(rounds):
    own = [None] * 8
    for g in range(2):
        block = jnp.stack(rounds[2 * g : 2 * g + 2])
        for s in range(4):
            own[2 * s + g] = block
            if s < 3:
                block = along_x(block)
    return own, [other_core(block) for block in own]


def on_device(
    candidates, cand_lengths, pairing, attn_gain, w_query, w_key, w_value, w_out, ffn_gain
):
    me = lax.axis_index("fsdp")
    y = lax.axis_index("tensor")
    core = lax.rem(lax.axis_index("dp"), 2)
    place = jnp.stack([me // 4, lax.rem(me, 4), y, core]).astype(jnp.int32)
    cand_dev = candidates.shape[1]
    devices = lax.axis_size("fsdp")
    flat = pairing[0].reshape(devices, cand_dev)
    pick = jnp.sum(jnp.where(flat // cand_dev == me, lax.rem(flat, cand_dev), 0), axis=1)
    wanted = lax.dynamic_index_in_dim(flat, me, 0, keepdims=False)
    source = wanted // cand_dev

    half_cols = (w_query.shape[1] + w_key.shape[1] + w_value.shape[1]) // 2
    first = w_query[:, :half_cols]
    second = jnp.concatenate([w_query[:, half_cols:], w_key, w_value], axis=1)
    rounds = [jnp.where(core == 0, first, second)]
    for _ in range(3):
        rounds.append(along_z(rounds[-1]))
    depth = w_out.shape[0] // 2
    out_piece = lax.dynamic_slice_in_dim(w_out, core * depth, depth, 0)
    out_own = lax.all_gather(out_piece, "fsdp", axis=0, tiled=False)

    packed = pack(pick, cand_lengths[0], candidates[0], rounds[1], devices)
    incoming = lax.all_to_all(packed, "fsdp", split_axis=0, concat_axis=0, tiled=True)
    qkv_own, qkv_other = spread_x(rounds)
    incoming = after(incoming, qkv_own[3], qkv_own[6])
    parts = 2
    pairs = cand_dev // 2 // parts
    local = unpack(source, incoming, parts)
    sent = incoming[:, -1, 0].astype(F32)
    slots = jnp.arange(devices, dtype=jnp.int32)
    lens = jnp.sum(
        jnp.where(source[:, None] == slots[None, :], sent[None, :], 0.0), axis=1
    ).astype(jnp.int32)


    gain_in = attn_gain.reshape(1, -1)
    gain_out = ffn_gain.reshape(1, -1)
    freq = rope_base ** (-jnp.arange(HEAD // 2, dtype=F32) * 2.0 / HEAD)
    starts = jnp.where(jnp.arange(cand_dev) % 2 == 0, 0, jnp.roll(lens, 1))
    positions = starts[:, None] + jnp.arange(SAMPLE, dtype=jnp.int32)[None, :]
    angles = positions.reshape(parts, -1, 1).astype(F32) * freq
    cosine, sine = jnp.cos(angles), jnp.sin(angles)
    cosine = jnp.concatenate([cosine, cosine], axis=2)
    sine = jnp.concatenate([-sine, sine], axis=2)

    width = candidates.shape[3]
    total = cand_dev * SAMPLE
    normed = None
    resids = []
    for c in range(parts):
        ring = [local[c]]
        for _ in range(3):
            ring.append(along_y(ring[-1]))
        if c == 0:
            out_own = after(out_own, ring[3], qkv_own[6], qkv_own[7])
            out_other = other_core(out_own)
        qkv = project(place, ring, gain_in, cosine[c], sine[c], qkv_own, qkv_other)
        terms = attend(c * pairs, pairs, place, lens, qkv, out_own, out_other)
        moving = along_y(terms[1])
        for r in (2, 3):
            moving = along_y((moving.astype(F32) + terms[r].astype(F32)).astype(BF))
        stream = local[c].astype(F32) + terms[0].astype(F32) + moving.astype(F32)
        blocks = [stream.astype(BF)]
        for _ in range(3):
            blocks.append(along_y(blocks[-1]))
        resids.append(blocks[0])
        normed = finish(place, gain_out, blocks, normed, c, total)
    resid = jnp.concatenate(resids, axis=0)
    pair_dev = cand_dev // 2
    return (
        resid.reshape(1, pair_dev, 2 * SAMPLE, width),
        normed.reshape(1, pair_dev, 2 * SAMPLE, TENSOR * width),
    )


def solution(mesh):
    return jax.shard_map(
        on_device,
        mesh=mesh,
        in_specs=(
            P("dp", "fsdp", None, "tensor"),
            P("dp", "fsdp"),
            P("dp", None, None),
            P(),
            P("fsdp", "tensor"),
            P("fsdp", "tensor"),
            P("fsdp", "tensor"),
            P("tensor", "fsdp"),
            P(),
        ),
        out_specs=(P("dp", "fsdp", None, "tensor"), P("dp", "fsdp", None, None)),
        check_vma=False,
    )
```

```python
import jax
import jax.numpy as jnp
from jax import lax
from jax.experimental import pallas as pl
from jax.experimental.pallas import tpu as pltpu
from jax.sharding import PartitionSpec as P

HEAD = 128
SAMPLE = 64
TENSOR = 4
RING = 4
LANES = 1024
PIECE = 256
EXTRA = 16
epsilon = 1e-05
rope_base = 500000.0
BF = jnp.bfloat16
F32 = jnp.float32
VMEM_LIMIT = 40 * 1024 * 1024


def wrap(value):
    return lax.rem(value + 2 * RING, RING)


def in_vmem():
    return pl.BlockSpec(memory_space=pltpu.VMEM)


def in_smem():
    return pl.BlockSpec(memory_space=pltpu.SMEM)


def params(**kw):
    return pltpu.CompilerParams(vmem_limit_bytes=VMEM_LIMIT, **kw)


def pack_kernel(pick_ref, lens_ref, cand_ref, _, slots_ref):
    blocks = cand_ref.shape[2] // HEAD
    for slot in range(slots_ref.shape[0]):
        own = pick_ref[slot]
        for b in range(blocks):
            slots_ref[slot, b * SAMPLE : (b + 1) * SAMPLE, :] = cand_ref[
                own, :, b * HEAD : (b + 1) * HEAD
            ]
        length = jnp.full((EXTRA, HEAD), lens_ref[own], jnp.int32).astype(F32)
        slots_ref[slot, blocks * SAMPLE :, :] = length.astype(BF)


def pack(pick, lens, cands, earlier, slots):
    rows = cands.shape[2] // HEAD * SAMPLE + EXTRA
    return pl.pallas_call(
        pack_kernel,
        out_shape=jax.ShapeDtypeStruct((slots, rows, HEAD), BF),
        in_specs=[in_smem(), in_smem(), in_vmem(), pl.BlockSpec(memory_space=pl.ANY)],
        out_specs=in_vmem(),
        compiler_params=params(),
        name="pack",
    )(pick, lens, cands, earlier)


def unpack_kernel(source_ref, slots_ref, *rows_refs):
    blocks = rows_refs[0].shape[1] // HEAD
    per = source_ref.shape[0] // len(rows_refs)
    for cand in range(source_ref.shape[0]):
        at = cand % per * SAMPLE
        for b in range(blocks):
            rows_refs[cand // per][at : at + SAMPLE, b * HEAD : (b + 1) * HEAD] = slots_ref[
                source_ref[cand], b * SAMPLE : (b + 1) * SAMPLE, :
            ]


def unpack(source, slots, parts):
    width = (slots.shape[1] - EXTRA) // SAMPLE * HEAD
    rows = source.shape[0] * SAMPLE // parts
    return pl.pallas_call(
        unpack_kernel,
        out_shape=(jax.ShapeDtypeStruct((rows, width), BF),) * parts,
        in_specs=[in_smem(), in_vmem()],
        out_specs=(in_vmem(),) * parts,
        compiler_params=params(),
        name="unpack",
    )(source, slots)


def place_of(place_ref):
    x, z, y, core = place_ref[0], place_ref[1], place_ref[2], place_ref[3]
    return x, z, y, core, 1 - 2 * core


def lane_block(index, width):
    return pl.ds(pl.multiple_of(index * width, width), width)


def project_kernel(place_ref, *refs):
    rows_refs = refs[:4]
    gain_ref, cos_ref, sin_ref = refs[4:7]
    own_refs, other_refs = refs[7:15], refs[15:23]
    query_ref, key_ref, value_ref = refs[23:26]
    own_rows, other_rows, result = refs[26:29]
    x, z, y, core, way = place_of(place_ref)
    squares = jnp.zeros((rows_refs[0].shape[0], 1), F32)
    for r in range(RING):
        block = wrap(y - r * way)
        s = wrap((x - block) * way)
        for m in range(RING):
            part = wrap(z - m * way)
            piece = rows_refs[r][:, lane_block(part, PIECE)].astype(F32)
            squares = squares + jnp.sum(piece * piece, axis=-1, keepdims=True)
            gain = gain_ref[:, lane_block(block * RING + part, PIECE)]
            own_rows[:, lane_block(s * RING + m, PIECE)] = (piece * gain).astype(BF)
    for s in range(RING):
        for m in range(RING):
            at = (s * RING + m) * PIECE
            back = ((RING - s) % RING * RING + (RING - m) % RING) * PIECE
            other_rows[:, at : at + PIECE] = own_rows[:, back : back + PIECE]
    wide = own_refs[0].shape[2]
    depth = 2 * PIECE
    for rows, weights, side in ((own_rows, own_refs, core), (other_rows, other_refs, 1 - core)):
        total = None
        for g in range(2 * RING):
            term = jnp.dot(
                rows[:, g * depth : (g + 1) * depth],
                weights[g][...].reshape(depth, wide),
                preferred_element_type=F32,
            )
            total = term if total is None else total + term
        result[:, pl.ds(pl.multiple_of(side * wide, HEAD), wide)] = total
    scale = lax.rsqrt(squares * (1.0 / (TENSOR * LANES)) + epsilon)
    cosine, sine = cos_ref[...], sin_ref[...]
    heads = query_ref.shape[1] // HEAD
    for h in range(heads + 1):
        values = result[:, h * HEAD : (h + 1) * HEAD] * scale
        turned = (values * cosine + pltpu.roll(values, HEAD // 2, 1) * sine).astype(BF)
        if h < heads:
            query_ref[:, h * HEAD : (h + 1) * HEAD] = turned
        else:
            key_ref[...] = turned
    value_ref[...] = (result[:, (heads + 1) * HEAD :] * scale).astype(BF)


def project(place, rows, gain, cosine, sine, own, other):
    count = rows[0].shape[0]
    width = rows[0].shape[1]
    return pl.pallas_call(
        project_kernel,
        out_shape=(
            jax.ShapeDtypeStruct((count, width), BF),
            jax.ShapeDtypeStruct((count, HEAD), BF),
            jax.ShapeDtypeStruct((count, HEAD), BF),
        ),
        in_specs=[in_smem()] + [in_vmem()] * 23,
        out_specs=(in_vmem(),) * 3,
        scratch_shapes=[
            pltpu.VMEM((count, TENSOR * width), BF),
            pltpu.VMEM((count, TENSOR * width), BF),
            pltpu.VMEM((count, width + 2 * HEAD), F32),
        ],
        compiler_params=params(),
        name="project",
    )(place, *rows, gain, cosine, sine, *own, *other)


def attend_kernel(first_pair, pairs, place_ref, lens_ref, q_ref, k_ref, v_ref, *refs):
    own_refs, other_refs = refs[:4], refs[4:8]
    out_refs = refs[8:12]
    mixed, terms = refs[12:14]
    x, z, y, core, way = place_of(place_ref)
    slots = 2 * SAMPLE
    heads = q_ref.shape[1] // HEAD
    step_t = lax.broadcasted_iota(jnp.int32, (slots, slots), 0)
    step_u = lax.broadcasted_iota(jnp.int32, (slots, slots), 1)
    for p in range(pairs):
        at = slice(p * slots, (p + 1) * slots)
        stacked = jnp.concatenate(
            [q_ref[at, h * HEAD : (h + 1) * HEAD] for h in range(heads)], axis=0
        )
        scores = lax.dot_general(
            stacked, k_ref[at, :], (((1,), (1,)), ((), ())), preferred_element_type=F32
        ) * (HEAD**-0.5)
        len_a = lens_ref[2 * (first_pair + p)]
        len_b = lens_ref[2 * (first_pair + p) + 1]
        limit = jnp.where(step_u < SAMPLE, len_a, len_b + SAMPLE)
        limit = jnp.minimum(limit, step_t + 1)
        closed = jnp.where(step_u < limit, 0.0, -1e30).astype(F32)
        scores = scores.reshape(heads, slots, slots) + closed[None]
        peak = jnp.max(scores, axis=-1, keepdims=True)
        weights = jnp.exp(scores - peak)
        probs = weights / jnp.sum(weights, axis=-1, keepdims=True)
        out = jnp.dot(
            probs.astype(BF).reshape(heads * slots, slots),
            v_ref[at, :],
            preferred_element_type=F32,
        ).astype(BF)
        for h in range(heads):
            mixed[at, h * HEAD : (h + 1) * HEAD] = out[h * slots : (h + 1) * slots]
    depth = own_refs[0].shape[1]
    mine = mixed[:, lane_block(core, depth)]
    theirs = mixed[:, lane_block(1 - core, depth)]
    for s in range(RING):
        r = wrap((y - wrap(x - s * way)) * way)
        for m in range(RING):
            part = wrap(z - m * way)
            term = jnp.dot(mine, own_refs[m][s], preferred_element_type=F32)
            term = term + jnp.dot(
                theirs, other_refs[(RING - m) % RING][(RING - s) % RING], preferred_element_type=F32
            )
            terms[r, :, lane_block(part, PIECE)] = term.astype(BF)
    for r in range(RING):
        out_refs[r][...] = terms[r]


def attend(first_pair, pairs, place, lens, qkv, own, other):
    count = pairs * 2 * SAMPLE
    width = qkv[0].shape[1]

    def kernel(*refs):
        attend_kernel(first_pair, pairs, *refs)

    return pl.pallas_call(
        kernel,
        out_shape=(jax.ShapeDtypeStruct((count, width), BF),) * RING,
        in_specs=[in_smem(), in_smem()] + [in_vmem()] * 11,
        out_specs=(in_vmem(),) * RING,
        scratch_shapes=[
            pltpu.VMEM((count, width), BF),
            pltpu.VMEM((RING, count, width), BF),
        ],
        compiler_params=params(),
        name="attend",
    )(place, lens, *qkv, *own, *other)


def finish_kernel(place_ref, gain_ref, b0, b1, b2, b3, *rest):
    out_ref = rest[-1]
    _, _, y, _, way = place_of(place_ref)
    values = [b[...].astype(F32) for b in (b0, b1, b2, b3)]
    squares = sum(jnp.sum(v * v, axis=-1, keepdims=True) for v in values)
    scale = lax.rsqrt(squares * (1.0 / (TENSOR * LANES)) + epsilon)
    for r in range(RING):
        lanes = lane_block(wrap(y - r * way), LANES)
        out_ref[:, lanes] = (values[r] * scale * gain_ref[:, lanes]).astype(BF)


def finish(place, gain, blocks, before, chunk, total):
    count, width = blocks[0].shape
    tile = 2 * SAMPLE
    steps = count // tile
    specs = [
        in_smem(),
        pl.BlockSpec((1, TENSOR * width), lambda i: (0, 0)),
    ] + [pl.BlockSpec((tile, width), lambda i: (i, 0))] * RING
    args = [place, gain, *blocks]
    aliases = {}
    if before is not None:
        specs.append(pl.BlockSpec(memory_space=pl.ANY))
        aliases = {len(args): 0}
        args.append(before)
    return pl.pallas_call(
        finish_kernel,
        grid=(steps,),
        out_shape=jax.ShapeDtypeStruct((total, TENSOR * width), BF),
        in_specs=specs,
        out_specs=pl.BlockSpec((tile, TENSOR * width), lambda i: (i + chunk * steps, 0)),
        input_output_aliases=aliases,
        compiler_params=params(),
        name="finish",
    )(*args)


def after(value, *others):
    anywhere = pl.BlockSpec(memory_space=pl.ANY)
    return pl.pallas_call(
        lambda *refs: None,
        out_shape=jax.ShapeDtypeStruct(value.shape, value.dtype),
        in_specs=[anywhere] * (1 + len(others)),
        out_specs=anywhere,
        input_output_aliases={0: 0},
        name="after",
    )(value, *others)


def way_of(dp):
    return 1 - 2 * (dp % 2)


def along_y(values):
    pairs = [
        (dp * TENSOR + y, dp * TENSOR + (y + way_of(dp)) % TENSOR)
        for dp in range(4)
        for y in range(TENSOR)
    ]
    return lax.ppermute(values, ("dp", "tensor"), pairs)


def along_x(values):
    pairs = [
        (dp * 16 + x * 4 + z, dp * 16 + (x + way_of(dp)) % 4 * 4 + z)
        for dp in range(4)
        for x in range(4)
        for z in range(4)
    ]
    return lax.ppermute(values, ("dp", "fsdp"), pairs)


def along_z(values):
    pairs = [
        (dp * 16 + x * 4 + z, dp * 16 + x * 4 + (z + way_of(dp)) % 4)
        for dp in range(4)
        for x in range(4)
        for z in range(4)
    ]
    return lax.ppermute(values, ("dp", "fsdp"), pairs)


def other_core(values):
    return lax.ppermute(values, "dp", [(dp, dp ^ 1) for dp in range(4)])


def spread_x(rounds):
    own = [None] * 8
    for g in range(2):
        block = jnp.stack(rounds[2 * g : 2 * g + 2])
        for s in range(4):
            own[2 * s + g] = block
            if s < 3:
                block = along_x(block)
    return own, [other_core(block) for block in own]


def ring_x(piece):
    rounds = [piece]
    for _ in range(3):
        rounds.append(along_x(rounds[-1]))
    return jnp.stack(rounds)


def on_device(
    candidates, cand_lengths, pairing, attn_gain, w_query, w_key, w_value, w_out, ffn_gain
):
    me = lax.axis_index("fsdp")
    y = lax.axis_index("tensor")
    core = lax.rem(lax.axis_index("dp"), 2)
    place = jnp.stack([me // 4, lax.rem(me, 4), y, core]).astype(jnp.int32)
    cand_dev = candidates.shape[1]
    devices = lax.axis_size("fsdp")
    flat = pairing[0].reshape(devices, cand_dev)
    pick = jnp.sum(jnp.where(flat // cand_dev == me, lax.rem(flat, cand_dev), 0), axis=1)
    wanted = lax.dynamic_index_in_dim(flat, me, 0, keepdims=False)
    source = wanted // cand_dev

    half_cols = (w_query.shape[1] + w_key.shape[1] + w_value.shape[1]) // 2
    first = w_query[:, :half_cols]
    second = jnp.concatenate([w_query[:, half_cols:], w_key, w_value], axis=1)
    rounds = [jnp.where(core == 0, first, second)]
    for _ in range(3):
        rounds.append(along_z(rounds[-1]))
    depth = w_out.shape[0] // 2
    out_piece = lax.dynamic_slice_in_dim(w_out, core * depth, depth, 0)
    out_first = along_z(after(out_piece, rounds[2]))
    out_own = [ring_x(out_piece)]

    packed = pack(pick, cand_lengths[0], candidates[0], rounds[2], devices)
    incoming = lax.all_to_all(packed, "fsdp", split_axis=0, concat_axis=0, tiled=True)
    qkv_own, qkv_other = spread_x(rounds)
    incoming = after(incoming, qkv_own[3], qkv_own[6])
    parts = 2
    pairs = cand_dev // 2 // parts
    local = unpack(source, incoming, parts)
    out_rounds = [out_first]
    for m in range(3):
        out_own.append(ring_x(out_rounds[-1]))
        if m == 0:
            out_rounds.append(along_z(after(out_first, local[0])))
        elif m == 1:
            out_rounds.append(along_z(out_rounds[-1]))
    out_other = [other_core(block) for block in out_own]
    sent = incoming[:, -1, 0].astype(F32)
    slots = jnp.arange(devices, dtype=jnp.int32)
    lens = jnp.sum(
        jnp.where(source[:, None] == slots[None, :], sent[None, :], 0.0), axis=1
    ).astype(jnp.int32)


    gain_in = attn_gain.reshape(1, -1)
    gain_out = ffn_gain.reshape(1, -1)
    freq = rope_base ** (-jnp.arange(HEAD // 2, dtype=F32) * 2.0 / HEAD)
    starts = jnp.where(jnp.arange(cand_dev) % 2 == 0, 0, jnp.roll(lens, 1))
    positions = starts[:, None] + jnp.arange(SAMPLE, dtype=jnp.int32)[None, :]
    angles = positions.reshape(parts, -1, 1).astype(F32) * freq
    cosine, sine = jnp.cos(angles), jnp.sin(angles)
    cosine = jnp.concatenate([cosine, cosine], axis=2)
    sine = jnp.concatenate([-sine, sine], axis=2)

    width = candidates.shape[3]
    total = cand_dev * SAMPLE
    normed = None
    resids = []
    for c in range(parts):
        ring = [local[c]]
        for _ in range(3):
            ring.append(along_y(ring[-1]))
        qkv = project(place, ring, gain_in, cosine[c], sine[c], qkv_own, qkv_other)
        terms = attend(c * pairs, pairs, place, lens, qkv, out_own, out_other)
        moving = along_y(terms[1])
        for r in (2, 3):
            moving = along_y((moving.astype(F32) + terms[r].astype(F32)).astype(BF))
        stream = local[c].astype(F32) + terms[0].astype(F32) + moving.astype(F32)
        blocks = [stream.astype(BF)]
        for _ in range(3):
            blocks.append(along_y(blocks[-1]))
        resids.append(blocks[0])
        normed = finish(place, gain_out, blocks, normed, c, total)
    resid = jnp.concatenate(resids, axis=0)
    pair_dev = cand_dev // 2
    return (
        resid.reshape(1, pair_dev, 2 * SAMPLE, width),
        normed.reshape(1, pair_dev, 2 * SAMPLE, TENSOR * width),
    )


def solution(mesh):
    return jax.shard_map(
        on_device,
        mesh=mesh,
        in_specs=(
            P("dp", "fsdp", None, "tensor"),
            P("dp", "fsdp"),
            P("dp", None, None),
            P(),
            P("fsdp", "tensor"),
            P("fsdp", "tensor"),
            P("fsdp", "tensor"),
            P("tensor", "fsdp"),
            P(),
        ),
        out_specs=(P("dp", "fsdp", None, "tensor"), P("dp", "fsdp", None, None)),
        check_vma=False,
    )
```

```python
import jax
import jax.numpy as jnp
from jax import lax
from jax.experimental import pallas as pl
from jax.experimental.pallas import tpu as pltpu
from jax.sharding import PartitionSpec as P

HEAD = 128
SAMPLE = 64
TENSOR = 4
RING = 4
LANES = 1024
PIECE = 256
EXTRA = 16
GROUPS = ((0, 1), (1, 2), (2, 4))
GROUP_OF = (0, 1, 2, 2)
SLOT_OF = (0, 0, 0, 1)
epsilon = 1e-05
rope_base = 500000.0
BF = jnp.bfloat16
F32 = jnp.float32
VMEM_LIMIT = 40 * 1024 * 1024


def wrap(value):
    return lax.rem(value + 2 * RING, RING)


def in_vmem():
    return pl.BlockSpec(memory_space=pltpu.VMEM)


def in_smem():
    return pl.BlockSpec(memory_space=pltpu.SMEM)


def params(**kw):
    return pltpu.CompilerParams(vmem_limit_bytes=VMEM_LIMIT, **kw)


def pack_kernel(pick_ref, lens_ref, cand_ref, *refs):
    slots_ref = refs[-1]
    blocks = cand_ref.shape[2] // HEAD
    for slot in range(slots_ref.shape[0]):
        own = pick_ref[slot]
        for b in range(blocks):
            slots_ref[slot, b * SAMPLE : (b + 1) * SAMPLE, :] = cand_ref[
                own, :, b * HEAD : (b + 1) * HEAD
            ]
        length = jnp.full((EXTRA, HEAD), lens_ref[own], jnp.int32).astype(F32)
        slots_ref[slot, blocks * SAMPLE :, :] = length.astype(BF)


def pack(pick, lens, cands, earlier, slots):
    rows = cands.shape[2] // HEAD * SAMPLE + EXTRA
    return pl.pallas_call(
        pack_kernel,
        out_shape=jax.ShapeDtypeStruct((slots, rows, HEAD), BF),
        in_specs=[in_smem(), in_smem(), in_vmem()]
        + [pl.BlockSpec(memory_space=pl.ANY)] * len(earlier),
        out_specs=in_vmem(),
        compiler_params=params(),
        name="pack",
    )(pick, lens, cands, *earlier)


def unpack_kernel(source_ref, slots_ref, *rows_refs):
    blocks = rows_refs[0].shape[1] // HEAD
    per = source_ref.shape[0] // len(rows_refs)
    for cand in range(source_ref.shape[0]):
        at = cand % per * SAMPLE
        for b in range(blocks):
            rows_refs[cand // per][at : at + SAMPLE, b * HEAD : (b + 1) * HEAD] = slots_ref[
                source_ref[cand], b * SAMPLE : (b + 1) * SAMPLE, :
            ]


def unpack(source, slots, parts):
    width = (slots.shape[1] - EXTRA) // SAMPLE * HEAD
    rows = source.shape[0] * SAMPLE // parts
    return pl.pallas_call(
        unpack_kernel,
        out_shape=(jax.ShapeDtypeStruct((rows, width), BF),) * parts,
        in_specs=[in_smem(), in_vmem()],
        out_specs=(in_vmem(),) * parts,
        compiler_params=params(),
        name="unpack",
    )(source, slots)


def place_of(place_ref):
    x, z, y, core = place_ref[0], place_ref[1], place_ref[2], place_ref[3]
    return x, z, y, core, 1 - 2 * core


def lane_block(index, width):
    return pl.ds(pl.multiple_of(index * width, width), width)


def project_kernel(place_ref, *refs):
    rows_refs = refs[:4]
    gain_ref, cos_ref, sin_ref = refs[4:7]
    own_refs, other_refs = refs[7:19], refs[19:31]
    query_ref, key_ref, value_ref = refs[31:34]
    own_rows, other_rows, result = refs[34:37]
    x, z, y, core, way = place_of(place_ref)
    squares = jnp.zeros((rows_refs[0].shape[0], 1), F32)
    for r in range(RING):
        block = wrap(y - r * way)
        s = wrap((x - block) * way)
        for m in range(RING):
            part = wrap(z - m * way)
            piece = rows_refs[r][:, lane_block(part, PIECE)].astype(F32)
            squares = squares + jnp.sum(piece * piece, axis=-1, keepdims=True)
            gain = gain_ref[:, lane_block(block * RING + part, PIECE)]
            own_rows[:, lane_block(s * RING + m, PIECE)] = (piece * gain).astype(BF)
    for s in range(RING):
        for m in range(RING):
            at = (s * RING + m) * PIECE
            back = ((RING - s) % RING * RING + (RING - m) % RING) * PIECE
            other_rows[:, at : at + PIECE] = own_rows[:, back : back + PIECE]
    wide = result.shape[1] // 2
    for rows, weights, side in ((own_rows, own_refs, core), (other_rows, other_refs, 1 - core)):
        total = None
        for s in range(RING):
            at = s * RING * PIECE
            for g, (start, stop) in enumerate(GROUPS):
                depth = (stop - start) * PIECE
                term = jnp.dot(
                    rows[:, at + start * PIECE : at + stop * PIECE],
                    weights[3 * s + g][:, :, :wide].reshape(depth, wide),
                    preferred_element_type=F32,
                )
                total = term if total is None else total + term
        result[:, pl.ds(pl.multiple_of(side * wide, HEAD), wide)] = total
    scale = lax.rsqrt(squares * (1.0 / (TENSOR * LANES)) + epsilon)
    cosine, sine = cos_ref[...], sin_ref[...]
    heads = query_ref.shape[1] // HEAD
    for h in range(heads + 1):
        values = result[:, h * HEAD : (h + 1) * HEAD] * scale
        turned = (values * cosine + pltpu.roll(values, HEAD // 2, 1) * sine).astype(BF)
        if h < heads:
            query_ref[:, h * HEAD : (h + 1) * HEAD] = turned
        else:
            key_ref[...] = turned
    value_ref[...] = (result[:, (heads + 1) * HEAD :] * scale).astype(BF)


def project(place, rows, gain, cosine, sine, own, other):
    count = rows[0].shape[0]
    width = rows[0].shape[1]
    return pl.pallas_call(
        project_kernel,
        out_shape=(
            jax.ShapeDtypeStruct((count, width), BF),
            jax.ShapeDtypeStruct((count, HEAD), BF),
            jax.ShapeDtypeStruct((count, HEAD), BF),
        ),
        in_specs=[in_smem()] + [in_vmem()] * 31,
        out_specs=(in_vmem(),) * 3,
        scratch_shapes=[
            pltpu.VMEM((count, TENSOR * width), BF),
            pltpu.VMEM((count, TENSOR * width), BF),
            pltpu.VMEM((count, width + 2 * HEAD), F32),
        ],
        compiler_params=params(),
        name="project",
    )(place, *rows, gain, cosine, sine, *own, *other)


def attend_kernel(first_pair, pairs, place_ref, lens_ref, q_ref, k_ref, v_ref, *refs):
    own_refs, other_refs = refs[:12], refs[12:24]
    out_refs = refs[24:28]
    mixed, terms = refs[28:30]
    x, z, y, core, way = place_of(place_ref)
    slots = 2 * SAMPLE
    heads = q_ref.shape[1] // HEAD
    step_t = lax.broadcasted_iota(jnp.int32, (slots, slots), 0)
    step_u = lax.broadcasted_iota(jnp.int32, (slots, slots), 1)
    for p in range(pairs):
        at = slice(p * slots, (p + 1) * slots)
        stacked = jnp.concatenate(
            [q_ref[at, h * HEAD : (h + 1) * HEAD] for h in range(heads)], axis=0
        )
        scores = lax.dot_general(
            stacked, k_ref[at, :], (((1,), (1,)), ((), ())), preferred_element_type=F32
        ) * (HEAD**-0.5)
        len_a = lens_ref[2 * (first_pair + p)]
        len_b = lens_ref[2 * (first_pair + p) + 1]
        limit = jnp.where(step_u < SAMPLE, len_a, len_b + SAMPLE)
        limit = jnp.minimum(limit, step_t + 1)
        closed = jnp.where(step_u < limit, 0.0, -1e30).astype(F32)
        scores = scores.reshape(heads, slots, slots) + closed[None]
        peak = jnp.max(scores, axis=-1, keepdims=True)
        weights = jnp.exp(scores - peak)
        probs = weights / jnp.sum(weights, axis=-1, keepdims=True)
        out = jnp.dot(
            probs.astype(BF).reshape(heads * slots, slots),
            v_ref[at, :],
            preferred_element_type=F32,
        ).astype(BF)
        for h in range(heads):
            mixed[at, h * HEAD : (h + 1) * HEAD] = out[h * slots : (h + 1) * slots]
    depth = 2 * PIECE
    wide = own_refs[0].shape[2] - depth
    mine = mixed[:, lane_block(core, depth)]
    theirs = mixed[:, lane_block(1 - core, depth)]

    def product(values, weights, s, m):
        block = weights[3 * s + GROUP_OF[m]]
        low = block[SLOT_OF[m], :, wide : wide + PIECE]
        high = block[SLOT_OF[m], :, wide + PIECE :]
        return jnp.dot(values[:, :PIECE], low, preferred_element_type=F32) + jnp.dot(
            values[:, PIECE:], high, preferred_element_type=F32
        )

    for s in range(RING):
        r = wrap((y - wrap(x - s * way)) * way)
        for m in range(RING):
            part = wrap(z - m * way)
            term = product(mine, own_refs, s, m) + product(
                theirs, other_refs, (RING - s) % RING, (RING - m) % RING
            )
            terms[r, :, lane_block(part, PIECE)] = term.astype(BF)
    for r in range(RING):
        out_refs[r][...] = terms[r]


def attend(first_pair, pairs, place, lens, qkv, own, other):
    count = pairs * 2 * SAMPLE
    width = qkv[0].shape[1]

    def kernel(*refs):
        attend_kernel(first_pair, pairs, *refs)

    return pl.pallas_call(
        kernel,
        out_shape=(jax.ShapeDtypeStruct((count, width), BF),) * RING,
        in_specs=[in_smem(), in_smem()] + [in_vmem()] * 27,
        out_specs=(in_vmem(),) * RING,
        scratch_shapes=[
            pltpu.VMEM((count, width), BF),
            pltpu.VMEM((RING, count, width), BF),
        ],
        compiler_params=params(),
        name="attend",
    )(place, lens, *qkv, *own, *other)


def finish_kernel(place_ref, gain_ref, b0, b1, b2, b3, *rest):
    out_ref = rest[-1]
    _, _, y, _, way = place_of(place_ref)
    values = [b[...].astype(F32) for b in (b0, b1, b2, b3)]
    squares = sum(jnp.sum(v * v, axis=-1, keepdims=True) for v in values)
    scale = lax.rsqrt(squares * (1.0 / (TENSOR * LANES)) + epsilon)
    for r in range(RING):
        lanes = lane_block(wrap(y - r * way), LANES)
        out_ref[:, lanes] = (values[r] * scale * gain_ref[:, lanes]).astype(BF)


def finish(place, gain, blocks, before, chunk, total):
    count, width = blocks[0].shape
    tile = 2 * SAMPLE
    steps = count // tile
    specs = [
        in_smem(),
        pl.BlockSpec((1, TENSOR * width), lambda i: (0, 0)),
    ] + [pl.BlockSpec((tile, width), lambda i: (i, 0))] * RING
    args = [place, gain, *blocks]
    aliases = {}
    if before is not None:
        specs.append(pl.BlockSpec(memory_space=pl.ANY))
        aliases = {len(args): 0}
        args.append(before)
    return pl.pallas_call(
        finish_kernel,
        grid=(steps,),
        out_shape=jax.ShapeDtypeStruct((total, TENSOR * width), BF),
        in_specs=specs,
        out_specs=pl.BlockSpec((tile, TENSOR * width), lambda i: (i + chunk * steps, 0)),
        input_output_aliases=aliases,
        compiler_params=params(),
        name="finish",
    )(*args)


def after(value, *others):
    anywhere = pl.BlockSpec(memory_space=pl.ANY)
    return pl.pallas_call(
        lambda *refs: None,
        out_shape=jax.ShapeDtypeStruct(value.shape, value.dtype),
        in_specs=[anywhere] * (1 + len(others)),
        out_specs=anywhere,
        input_output_aliases={0: 0},
        name="after",
    )(value, *others)


def way_of(dp):
    return 1 - 2 * (dp % 2)


def along_y(values):
    pairs = [
        (dp * TENSOR + y, dp * TENSOR + (y + way_of(dp)) % TENSOR)
        for dp in range(4)
        for y in range(TENSOR)
    ]
    return lax.ppermute(values, ("dp", "tensor"), pairs)


def along_x(values):
    pairs = [
        (dp * 16 + x * 4 + z, dp * 16 + (x + way_of(dp)) % 4 * 4 + z)
        for dp in range(4)
        for x in range(4)
        for z in range(4)
    ]
    return lax.ppermute(values, ("dp", "fsdp"), pairs)


def along_z(values):
    pairs = [
        (dp * 16 + x * 4 + z, dp * 16 + x * 4 + (z + way_of(dp)) % 4)
        for dp in range(4)
        for x in range(4)
        for z in range(4)
    ]
    return lax.ppermute(values, ("dp", "fsdp"), pairs)


def other_core(values):
    return lax.ppermute(values, "dp", [(dp, dp ^ 1) for dp in range(4)])


def spread_x(rounds):
    own = [None] * 12
    for g, (start, stop) in enumerate(GROUPS):
        block = jnp.stack(rounds[start:stop])
        for s in range(4):
            own[3 * s + g] = block
            if s < 3:
                block = along_x(block)
    return own, [other_core(block) for block in own]


def on_device(
    candidates, cand_lengths, pairing, attn_gain, w_query, w_key, w_value, w_out, ffn_gain
):
    me = lax.axis_index("fsdp")
    y = lax.axis_index("tensor")
    core = lax.rem(lax.axis_index("dp"), 2)
    place = jnp.stack([me // 4, lax.rem(me, 4), y, core]).astype(jnp.int32)
    cand_dev = candidates.shape[1]
    devices = lax.axis_size("fsdp")
    flat = pairing[0].reshape(devices, cand_dev)
    pick = jnp.sum(jnp.where(flat // cand_dev == me, lax.rem(flat, cand_dev), 0), axis=1)
    wanted = lax.dynamic_index_in_dim(flat, me, 0, keepdims=False)
    source = wanted // cand_dev

    half_cols = (w_query.shape[1] + w_key.shape[1] + w_value.shape[1]) // 2
    first = w_query[:, :half_cols]
    second = jnp.concatenate([w_query[:, half_cols:], w_key, w_value], axis=1)
    depth = w_out.shape[0] // 2
    third = jnp.where(core == 0, w_out[:depth], w_out[depth:])
    piece = jnp.concatenate(
        [jnp.where(core == 0, first, second), third[: depth // 2], third[depth // 2 :]], axis=1
    )
    rounds = [piece]
    for _ in range(3):
        rounds.append(along_z(rounds[-1]))
    own, other = spread_x(rounds)

    packed = pack(pick, cand_lengths[0], candidates[0], (rounds[3], own[7], own[9]), devices)
    incoming = lax.all_to_all(packed, "fsdp", split_axis=0, concat_axis=0, tiled=True)
    parts = 2
    pairs = cand_dev // 2 // parts
    local = unpack(source, incoming, parts)
    sent = incoming[:, -1, 0].astype(F32)
    slots = jnp.arange(devices, dtype=jnp.int32)
    lens = jnp.sum(
        jnp.where(source[:, None] == slots[None, :], sent[None, :], 0.0), axis=1
    ).astype(jnp.int32)


    gain_in = attn_gain.reshape(1, -1)
    gain_out = ffn_gain.reshape(1, -1)
    freq = rope_base ** (-jnp.arange(HEAD // 2, dtype=F32) * 2.0 / HEAD)
    starts = jnp.where(jnp.arange(cand_dev) % 2 == 0, 0, jnp.roll(lens, 1))
    positions = starts[:, None] + jnp.arange(SAMPLE, dtype=jnp.int32)[None, :]
    angles = positions.reshape(parts, -1, 1).astype(F32) * freq
    cosine, sine = jnp.cos(angles), jnp.sin(angles)
    cosine = jnp.concatenate([cosine, cosine], axis=2)
    sine = jnp.concatenate([-sine, sine], axis=2)

    width = candidates.shape[3]
    total = cand_dev * SAMPLE
    normed = None
    resids = []
    for c in range(parts):
        ring = [local[c]]
        for _ in range(3):
            ring.append(along_y(ring[-1]))
        qkv = project(place, ring, gain_in, cosine[c], sine[c], own, other)
        terms = attend(c * pairs, pairs, place, lens, qkv, own, other)
        moving = along_y(terms[1])
        for r in (2, 3):
            moving = along_y((moving.astype(F32) + terms[r].astype(F32)).astype(BF))
        stream = local[c].astype(F32) + terms[0].astype(F32) + moving.astype(F32)
        blocks = [stream.astype(BF)]
        for _ in range(3):
            blocks.append(along_y(blocks[-1]))
        resids.append(blocks[0])
        normed = finish(place, gain_out, blocks, normed, c, total)
    resid = jnp.concatenate(resids, axis=0)
    pair_dev = cand_dev // 2
    return (
        resid.reshape(1, pair_dev, 2 * SAMPLE, width),
        normed.reshape(1, pair_dev, 2 * SAMPLE, TENSOR * width),
    )


def solution(mesh):
    return jax.shard_map(
        on_device,
        mesh=mesh,
        in_specs=(
            P("dp", "fsdp", None, "tensor"),
            P("dp", "fsdp"),
            P("dp", None, None),
            P(),
            P("fsdp", "tensor"),
            P("fsdp", "tensor"),
            P("fsdp", "tensor"),
            P("tensor", "fsdp"),
            P(),
        ),
        out_specs=(P("dp", "fsdp", None, "tensor"), P("dp", "fsdp", None, None)),
        check_vma=False,
    )
```

```python
import jax
import jax.numpy as jnp
from jax import lax
from jax.experimental import pallas as pl
from jax.experimental.pallas import tpu as pltpu
from jax.sharding import PartitionSpec as P

HEAD = 128
SAMPLE = 64
TENSOR = 4
RING = 4
LANES = 1024
PIECE = 256
EXTRA = 16
GROUPS = ((0, 1), (1, 2), (2, 4))
epsilon = 1e-05
rope_base = 500000.0
BF = jnp.bfloat16
F32 = jnp.float32
VMEM_LIMIT = 40 * 1024 * 1024


def wrap(value):
    return lax.rem(value + 2 * RING, RING)


def in_vmem():
    return pl.BlockSpec(memory_space=pltpu.VMEM)


def in_smem():
    return pl.BlockSpec(memory_space=pltpu.SMEM)


def params(**kw):
    return pltpu.CompilerParams(vmem_limit_bytes=VMEM_LIMIT, **kw)


def pack_kernel(pick_ref, lens_ref, cand_ref, *refs):
    slots_ref = refs[-1]
    blocks = cand_ref.shape[2] // HEAD
    for slot in range(slots_ref.shape[0]):
        own = pick_ref[slot]
        for b in range(blocks):
            slots_ref[slot, b * SAMPLE : (b + 1) * SAMPLE, :] = cand_ref[
                own, :, b * HEAD : (b + 1) * HEAD
            ]
        length = jnp.full((EXTRA, HEAD), lens_ref[own], jnp.int32).astype(F32)
        slots_ref[slot, blocks * SAMPLE :, :] = length.astype(BF)


def pack(pick, lens, cands, earlier, slots):
    rows = cands.shape[2] // HEAD * SAMPLE + EXTRA
    return pl.pallas_call(
        pack_kernel,
        out_shape=jax.ShapeDtypeStruct((slots, rows, HEAD), BF),
        in_specs=[in_smem(), in_smem(), in_vmem()]
        + [pl.BlockSpec(memory_space=pl.ANY)] * len(earlier),
        out_specs=in_vmem(),
        compiler_params=params(),
        name="pack",
    )(pick, lens, cands, *earlier)


def unpack_kernel(earlier, source_ref, slots_ref, *refs):
    rows_refs = refs[earlier:]
    blocks = rows_refs[0].shape[1] // HEAD
    per = source_ref.shape[0] // len(rows_refs)
    for cand in range(source_ref.shape[0]):
        at = cand % per * SAMPLE
        for b in range(blocks):
            rows_refs[cand // per][at : at + SAMPLE, b * HEAD : (b + 1) * HEAD] = slots_ref[
                source_ref[cand], b * SAMPLE : (b + 1) * SAMPLE, :
            ]


def unpack(source, slots, earlier, parts):
    width = (slots.shape[1] - EXTRA) // SAMPLE * HEAD
    rows = source.shape[0] * SAMPLE // parts

    def kernel(*refs):
        unpack_kernel(len(earlier), *refs)

    return pl.pallas_call(
        kernel,
        out_shape=(jax.ShapeDtypeStruct((rows, width), BF),) * parts,
        in_specs=[in_smem(), in_vmem()] + [anywhere()] * len(earlier),
        out_specs=(in_vmem(),) * parts,
        compiler_params=params(),
        name="unpack",
    )(source, slots, *earlier)


def place_of(place_ref):
    x, z, y, core = place_ref[0], place_ref[1], place_ref[2], place_ref[3]
    return x, z, y, core, 1 - 2 * core


def lane_block(index, width):
    return pl.ds(pl.multiple_of(index * width, width), width)


def fetch(own_refs, other_refs, start, weights, sems):
    width = weights.shape[4]
    copies = []
    for side, blocks in enumerate((own_refs, other_refs)):
        copies.append([])
        for s in range(RING):
            copies[side].append([])
            for g, (lo, hi) in enumerate(GROUPS):
                copy = pltpu.make_async_copy(
                    blocks[3 * s + g].at[:, :, start : start + width],
                    weights.at[side, s, 2 * lo : 2 * hi],
                    sems.at[side, s, g],
                )
                copy.start()
                copies[side][s].append(copy)
    return copies


def weight_space(width):
    return [
        pltpu.VMEM((2, RING, 2 * RING, PIECE // 2, width), BF),
        pltpu.SemaphoreType.DMA((2, RING, len(GROUPS))),
    ]


def anywhere():
    return pl.BlockSpec(memory_space=pl.ANY)


def project_kernel(place_ref, *refs):
    rows_refs = refs[:4]
    gain_ref, cos_ref, sin_ref = refs[4:7]
    own_refs, other_refs = refs[7:19], refs[19:31]
    query_ref, key_ref, value_ref = refs[31:34]
    own_rows, other_rows, result, weights, sems = refs[34:39]
    wide = weights.shape[4]
    copies = fetch(own_refs, other_refs, 0, weights, sems)
    x, z, y, core, way = place_of(place_ref)
    squares = jnp.zeros((rows_refs[0].shape[0], 1), F32)
    for r in range(RING):
        block = wrap(y - r * way)
        s = wrap((x - block) * way)
        for m in range(RING):
            part = wrap(z - m * way)
            piece = rows_refs[r][:, lane_block(part, PIECE)].astype(F32)
            squares = squares + jnp.sum(piece * piece, axis=-1, keepdims=True)
            gain = gain_ref[:, lane_block(block * RING + part, PIECE)]
            own_rows[:, lane_block(s * RING + m, PIECE)] = (piece * gain).astype(BF)
    for s in range(RING):
        for m in range(RING):
            at = (s * RING + m) * PIECE
            back = ((RING - s) % RING * RING + (RING - m) % RING) * PIECE
            other_rows[:, at : at + PIECE] = own_rows[:, back : back + PIECE]
    for side, (rows, at) in enumerate(((own_rows, core), (other_rows, 1 - core))):
        total = None
        for s in range(RING):
            for copy in copies[side][s]:
                copy.wait()
            term = jnp.dot(
                rows[:, s * LANES : (s + 1) * LANES],
                weights[side, s].reshape(LANES, wide),
                preferred_element_type=F32,
            )
            total = term if total is None else total + term
        result[:, pl.ds(pl.multiple_of(at * wide, HEAD), wide)] = total
    scale = lax.rsqrt(squares * (1.0 / (TENSOR * LANES)) + epsilon)
    cosine, sine = cos_ref[...], sin_ref[...]
    heads = query_ref.shape[1] // HEAD
    for h in range(heads + 1):
        values = result[:, h * HEAD : (h + 1) * HEAD] * scale
        turned = (values * cosine + pltpu.roll(values, HEAD // 2, 1) * sine).astype(BF)
        if h < heads:
            query_ref[:, h * HEAD : (h + 1) * HEAD] = turned
        else:
            key_ref[...] = turned
    value_ref[...] = (result[:, (heads + 1) * HEAD :] * scale).astype(BF)


def project(place, rows, gain, cosine, sine, own, other):
    count = rows[0].shape[0]
    width = rows[0].shape[1]
    return pl.pallas_call(
        project_kernel,
        out_shape=(
            jax.ShapeDtypeStruct((count, width), BF),
            jax.ShapeDtypeStruct((count, HEAD), BF),
            jax.ShapeDtypeStruct((count, HEAD), BF),
        ),
        in_specs=[in_smem()] + [in_vmem()] * 7 + [anywhere()] * 24,
        out_specs=(in_vmem(),) * 3,
        scratch_shapes=[
            pltpu.VMEM((count, TENSOR * width), BF),
            pltpu.VMEM((count, TENSOR * width), BF),
            pltpu.VMEM((count, width + 2 * HEAD), F32),
        ]
        + weight_space((width + 2 * HEAD) // 2),
        compiler_params=params(),
        name="project",
    )(place, *rows, gain, cosine, sine, *own, *other)


def attend_kernel(first_pair, pairs, place_ref, lens_ref, q_ref, k_ref, v_ref, *refs):
    own_refs, other_refs = refs[:12], refs[12:24]
    out_refs = refs[24:28]
    mixed, terms, weights, sems = refs[28:32]
    copies = fetch(own_refs, other_refs, (q_ref.shape[1] + 2 * HEAD) // 2, weights, sems)
    x, z, y, core, way = place_of(place_ref)
    slots = 2 * SAMPLE
    heads = q_ref.shape[1] // HEAD
    step_t = lax.broadcasted_iota(jnp.int32, (slots, slots), 0)
    step_u = lax.broadcasted_iota(jnp.int32, (slots, slots), 1)
    for p in range(pairs):
        at = slice(p * slots, (p + 1) * slots)
        stacked = jnp.concatenate(
            [q_ref[at, h * HEAD : (h + 1) * HEAD] for h in range(heads)], axis=0
        )
        scores = lax.dot_general(
            stacked, k_ref[at, :], (((1,), (1,)), ((), ())), preferred_element_type=F32
        ) * (HEAD**-0.5)
        len_a = lens_ref[2 * (first_pair + p)]
        len_b = lens_ref[2 * (first_pair + p) + 1]
        limit = jnp.where(step_u < SAMPLE, len_a, len_b + SAMPLE)
        limit = jnp.minimum(limit, step_t + 1)
        closed = jnp.where(step_u < limit, 0.0, -1e30).astype(F32)
        scores = scores.reshape(heads, slots, slots) + closed[None]
        peak = jnp.max(scores, axis=-1, keepdims=True)
        raised = jnp.exp(scores - peak)
        probs = raised / jnp.sum(raised, axis=-1, keepdims=True)
        out = jnp.dot(
            probs.astype(BF).reshape(heads * slots, slots),
            v_ref[at, :],
            preferred_element_type=F32,
        ).astype(BF)
        for h in range(heads):
            mixed[at, h * HEAD : (h + 1) * HEAD] = out[h * slots : (h + 1) * slots]
    depth = 2 * PIECE
    mine = mixed[:, lane_block(core, depth)]
    theirs = mixed[:, lane_block(1 - core, depth)]
    for side in copies:
        for step in side:
            for copy in step:
                copy.wait()

    def product(values, side, s, m):
        block = weights[side, s, 2 * m : 2 * m + 2].reshape(PIECE, depth)
        return jnp.dot(values[:, :PIECE], block[:, :PIECE], preferred_element_type=F32) + jnp.dot(
            values[:, PIECE:], block[:, PIECE:], preferred_element_type=F32
        )

    for s in range(RING):
        r = wrap((y - wrap(x - s * way)) * way)
        for m in range(RING):
            part = wrap(z - m * way)
            term = product(mine, 0, s, m) + product(
                theirs, 1, (RING - s) % RING, (RING - m) % RING
            )
            terms[r, :, lane_block(part, PIECE)] = term.astype(BF)
    for r in range(RING):
        out_refs[r][...] = terms[r]


def attend(first_pair, pairs, place, lens, qkv, own, other):
    count = pairs * 2 * SAMPLE
    width = qkv[0].shape[1]

    def kernel(*refs):
        attend_kernel(first_pair, pairs, *refs)

    return pl.pallas_call(
        kernel,
        out_shape=(jax.ShapeDtypeStruct((count, width), BF),) * RING,
        in_specs=[in_smem(), in_smem()] + [in_vmem()] * 3 + [anywhere()] * 24,
        out_specs=(in_vmem(),) * RING,
        scratch_shapes=[
            pltpu.VMEM((count, width), BF),
            pltpu.VMEM((RING, count, width), BF),
        ]
        + weight_space(2 * PIECE),
        compiler_params=params(),
        name="attend",
    )(place, lens, *qkv, *own, *other)


def finish_kernel(place_ref, gain_ref, b0, b1, b2, b3, *rest):
    out_ref = rest[-1]
    _, _, y, _, way = place_of(place_ref)
    values = [b[...].astype(F32) for b in (b0, b1, b2, b3)]
    squares = sum(jnp.sum(v * v, axis=-1, keepdims=True) for v in values)
    scale = lax.rsqrt(squares * (1.0 / (TENSOR * LANES)) + epsilon)
    for r in range(RING):
        lanes = lane_block(wrap(y - r * way), LANES)
        out_ref[:, lanes] = (values[r] * scale * gain_ref[:, lanes]).astype(BF)


def finish(place, gain, blocks, before, chunk, total):
    count, width = blocks[0].shape
    tile = 2 * SAMPLE
    steps = count // tile
    specs = [
        in_smem(),
        pl.BlockSpec((1, TENSOR * width), lambda i: (0, 0)),
    ] + [pl.BlockSpec((tile, width), lambda i: (i, 0))] * RING
    args = [place, gain, *blocks]
    aliases = {}
    if before is not None:
        specs.append(pl.BlockSpec(memory_space=pl.ANY))
        aliases = {len(args): 0}
        args.append(before)
    return pl.pallas_call(
        finish_kernel,
        grid=(steps,),
        out_shape=jax.ShapeDtypeStruct((total, TENSOR * width), BF),
        in_specs=specs,
        out_specs=pl.BlockSpec((tile, TENSOR * width), lambda i: (i + chunk * steps, 0)),
        input_output_aliases=aliases,
        compiler_params=params(),
        name="finish",
    )(*args)


def after(value, *others):
    return pl.pallas_call(
        lambda *refs: None,
        out_shape=jax.ShapeDtypeStruct(value.shape, value.dtype),
        in_specs=[anywhere()] * (1 + len(others)),
        out_specs=anywhere(),
        input_output_aliases={0: 0},
        name="after",
    )(value, *others)


def way_of(dp):
    return 1 - 2 * (dp % 2)


def along_y(values):
    pairs = [
        (dp * TENSOR + y, dp * TENSOR + (y + way_of(dp)) % TENSOR)
        for dp in range(4)
        for y in range(TENSOR)
    ]
    return lax.ppermute(values, ("dp", "tensor"), pairs)


def along_x(values):
    pairs = [
        (dp * 16 + x * 4 + z, dp * 16 + (x + way_of(dp)) % 4 * 4 + z)
        for dp in range(4)
        for x in range(4)
        for z in range(4)
    ]
    return lax.ppermute(values, ("dp", "fsdp"), pairs)


def along_z(values):
    pairs = [
        (dp * 16 + x * 4 + z, dp * 16 + x * 4 + (z + way_of(dp)) % 4)
        for dp in range(4)
        for x in range(4)
        for z in range(4)
    ]
    return lax.ppermute(values, ("dp", "fsdp"), pairs)


def other_core(values):
    return lax.ppermute(values, "dp", [(dp, dp ^ 1) for dp in range(4)])


def spread_x(rounds):
    own = [None] * 12
    for g, (start, stop) in enumerate(GROUPS):
        block = jnp.stack([half for step in rounds[start:stop] for half in step])
        for s in range(4):
            own[3 * s + g] = block
            if s < 3 and (s < 2 or g < 2):
                block = along_x(block)
    return own


def on_device(
    candidates, cand_lengths, pairing, attn_gain, w_query, w_key, w_value, w_out, ffn_gain
):
    me = lax.axis_index("fsdp")
    y = lax.axis_index("tensor")
    core = lax.rem(lax.axis_index("dp"), 2)
    place = jnp.stack([me // 4, lax.rem(me, 4), y, core]).astype(jnp.int32)
    cand_dev = candidates.shape[1]
    devices = lax.axis_size("fsdp")
    flat = pairing[0].reshape(devices, cand_dev)
    pick = jnp.sum(jnp.where(flat // cand_dev == me, lax.rem(flat, cand_dev), 0), axis=1)
    wanted = lax.dynamic_index_in_dim(flat, me, 0, keepdims=False)
    source = wanted // cand_dev

    half_cols = (w_query.shape[1] + w_key.shape[1] + w_value.shape[1]) // 2
    first = w_query[:, :half_cols]
    second = jnp.concatenate([w_query[:, half_cols:], w_key, w_value], axis=1)
    depth = w_out.shape[0] // 2
    third = jnp.where(core == 0, w_out[:depth], w_out[depth:])
    piece = jnp.concatenate(
        [jnp.where(core == 0, first, second), third[: depth // 2], third[depth // 2 :]], axis=1
    )
    rounds = [[piece[: PIECE // 2], piece[PIECE // 2 :]]]
    for _ in range(3):
        rounds.append([along_z(half) for half in rounds[-1]])
    own = spread_x(rounds)

    packed = pack(pick, cand_lengths[0], candidates[0], (*rounds[3], own[7], own[9]), devices)
    incoming = lax.all_to_all(packed, "fsdp", split_axis=0, concat_axis=0, tiled=True)
    parts = 2
    pairs = cand_dev // 2 // parts
    local = unpack(source, incoming, (own[10],), parts)
    own[11] = along_x(after(own[8], local[0]))
    other = [other_core(block) for block in own]
    sent = incoming[:, -1, 0].astype(F32)
    slots = jnp.arange(devices, dtype=jnp.int32)
    lens = jnp.sum(
        jnp.where(source[:, None] == slots[None, :], sent[None, :], 0.0), axis=1
    ).astype(jnp.int32)


    gain_in = attn_gain.reshape(1, -1)
    gain_out = ffn_gain.reshape(1, -1)
    freq = rope_base ** (-jnp.arange(HEAD // 2, dtype=F32) * 2.0 / HEAD)
    starts = jnp.where(jnp.arange(cand_dev) % 2 == 0, 0, jnp.roll(lens, 1))
    positions = starts[:, None] + jnp.arange(SAMPLE, dtype=jnp.int32)[None, :]
    angles = positions.reshape(parts, -1, 1).astype(F32) * freq
    cosine, sine = jnp.cos(angles), jnp.sin(angles)
    cosine = jnp.concatenate([cosine, cosine], axis=2)
    sine = jnp.concatenate([-sine, sine], axis=2)

    width = candidates.shape[3]
    total = cand_dev * SAMPLE
    normed = None
    resids = []
    for c in range(parts):
        ring = [local[c] if c == 0 else after(local[c], ring[3])]
        for _ in range(3):
            ring.append(along_y(ring[-1]))
        qkv = project(place, ring, gain_in, cosine[c], sine[c], own, other)
        terms = attend(c * pairs, pairs, place, lens, qkv, own, other)
        moving = along_y(terms[1])
        for r in (2, 3):
            moving = along_y((moving.astype(F32) + terms[r].astype(F32)).astype(BF))
        stream = local[c].astype(F32) + terms[0].astype(F32) + moving.astype(F32)
        blocks = [stream.astype(BF)]
        for _ in range(3):
            blocks.append(along_y(blocks[-1]))
        resids.append(blocks[0])
        normed = finish(place, gain_out, blocks, normed, c, total)
    resid = jnp.concatenate(resids, axis=0)
    pair_dev = cand_dev // 2
    return (
        resid.reshape(1, pair_dev, 2 * SAMPLE, width),
        normed.reshape(1, pair_dev, 2 * SAMPLE, TENSOR * width),
    )


def solution(mesh):
    return jax.shard_map(
        on_device,
        mesh=mesh,
        in_specs=(
            P("dp", "fsdp", None, "tensor"),
            P("dp", "fsdp"),
            P("dp", None, None),
            P(),
            P("fsdp", "tensor"),
            P("fsdp", "tensor"),
            P("fsdp", "tensor"),
            P("tensor", "fsdp"),
            P(),
        ),
        out_specs=(P("dp", "fsdp", None, "tensor"), P("dp", "fsdp", None, None)),
        check_vma=False,
    )
```

```python
import jax
import jax.numpy as jnp
from jax import lax
from jax.experimental import pallas as pl
from jax.experimental.pallas import tpu as pltpu
from jax.sharding import PartitionSpec as P

HEAD = 128
SAMPLE = 64
TENSOR = 4
RING = 4
LANES = 1024
PIECE = 256
EXTRA = 16
epsilon = 1e-05
rope_base = 500000.0
BF = jnp.bfloat16
F32 = jnp.float32
VMEM_LIMIT = 40 * 1024 * 1024


def wrap(value):
    return lax.rem(value + 2 * RING, RING)


def in_vmem():
    return pl.BlockSpec(memory_space=pltpu.VMEM)


def in_smem():
    return pl.BlockSpec(memory_space=pltpu.SMEM)


def params(**kw):
    return pltpu.CompilerParams(vmem_limit_bytes=VMEM_LIMIT, **kw)


def pack_kernel(pick_ref, lens_ref, cand_ref, *refs):
    slots_ref = refs[-1]
    blocks = cand_ref.shape[2] // HEAD
    for slot in range(slots_ref.shape[0]):
        own = pick_ref[slot]
        for b in range(blocks):
            slots_ref[slot, b * SAMPLE : (b + 1) * SAMPLE, :] = cand_ref[
                own, :, b * HEAD : (b + 1) * HEAD
            ]
        length = jnp.full((EXTRA, HEAD), lens_ref[own], jnp.int32).astype(F32)
        slots_ref[slot, blocks * SAMPLE :, :] = length.astype(BF)


def pack(pick, lens, cands, earlier, slots):
    rows = cands.shape[2] // HEAD * SAMPLE + EXTRA
    return pl.pallas_call(
        pack_kernel,
        out_shape=jax.ShapeDtypeStruct((slots, rows, HEAD), BF),
        in_specs=[in_smem(), in_smem(), in_vmem()]
        + [pl.BlockSpec(memory_space=pl.ANY)] * len(earlier),
        out_specs=in_vmem(),
        compiler_params=params(),
        name="pack",
    )(pick, lens, cands, *earlier)


def unpack_kernel(earlier, source_ref, slots_ref, *refs):
    rows_refs = refs[earlier:]
    blocks = rows_refs[0].shape[1] // HEAD
    per = source_ref.shape[0] // len(rows_refs)
    for cand in range(source_ref.shape[0]):
        at = cand % per * SAMPLE
        for b in range(blocks):
            rows_refs[cand // per][at : at + SAMPLE, b * HEAD : (b + 1) * HEAD] = slots_ref[
                source_ref[cand], b * SAMPLE : (b + 1) * SAMPLE, :
            ]


def unpack(source, slots, earlier, parts):
    width = (slots.shape[1] - EXTRA) // SAMPLE * HEAD
    rows = source.shape[0] * SAMPLE // parts

    def kernel(*refs):
        unpack_kernel(len(earlier), *refs)

    return pl.pallas_call(
        kernel,
        out_shape=(jax.ShapeDtypeStruct((rows, width), BF),) * parts,
        in_specs=[in_smem(), in_vmem()] + [anywhere()] * len(earlier),
        out_specs=(in_vmem(),) * parts,
        compiler_params=params(),
        name="unpack",
    )(source, slots, *earlier)


def place_of(place_ref):
    x, z, y, core = place_ref[0], place_ref[1], place_ref[2], place_ref[3]
    return x, z, y, core, 1 - 2 * core


def lane_block(index, width):
    return pl.ds(pl.multiple_of(index * width, width), width)


def fetch(own_refs, other_refs, start, weights, sems):
    width = weights.shape[4]
    copies = []
    for side, blocks in enumerate((own_refs, other_refs)):
        copies.append([])
        for s in range(RING):
            copies[side].append([])
            for m in range(RING):
                copy = pltpu.make_async_copy(
                    blocks[RING * s + m].at[:, start : start + width],
                    weights.at[side, s, m],
                    sems.at[side, s, m],
                )
                copy.start()
                copies[side][s].append(copy)
    return copies


def weight_space(width):
    return [
        pltpu.VMEM((2, RING, RING, PIECE, width), BF),
        pltpu.SemaphoreType.DMA((2, RING, RING)),
    ]


def anywhere():
    return pl.BlockSpec(memory_space=pl.ANY)


def project_kernel(parts, place_ref, *refs):
    rows_refs = [refs[RING * c : RING * c + RING] for c in range(parts)]
    refs = refs[RING * parts :]
    gain_ref, cos_ref, sin_ref = refs[:3]
    own_refs, other_refs = refs[3:19], refs[19:35]
    query_ref, key_ref, value_ref = refs[35:38]
    own_rows, other_rows, result, weights, sems = refs[38:43]
    wide = weights.shape[4]
    copies = fetch(own_refs, other_refs, 0, weights, sems)
    x, z, y, core, way = place_of(place_ref)
    count = rows_refs[0][0].shape[0]
    squares = [jnp.zeros((count, 1), F32) for _ in range(parts)]
    for r in range(RING):
        block = wrap(y - r * way)
        s = wrap((x - block) * way)
        for m in range(RING):
            part = wrap(z - m * way)
            gain = gain_ref[:, lane_block(block * RING + part, PIECE)]
            for c in range(parts):
                piece = rows_refs[c][r][:, lane_block(part, PIECE)].astype(F32)
                squares[c] = squares[c] + jnp.sum(piece * piece, axis=-1, keepdims=True)
                own_rows[c * count : (c + 1) * count, lane_block(s * RING + m, PIECE)] = (
                    piece * gain
                ).astype(BF)
    squares = jnp.concatenate(squares, axis=0)
    for s in range(RING):
        for m in range(RING):
            at = (s * RING + m) * PIECE
            back = ((RING - s) % RING * RING + (RING - m) % RING) * PIECE
            other_rows[:, at : at + PIECE] = own_rows[:, back : back + PIECE]
    for side, (rows, at) in enumerate(((own_rows, core), (other_rows, 1 - core))):
        total = None
        for s in range(RING):
            for copy in copies[side][s]:
                copy.wait()
            term = jnp.dot(
                rows[:, s * LANES : (s + 1) * LANES],
                weights[side, s].reshape(LANES, wide),
                preferred_element_type=F32,
            )
            total = term if total is None else total + term
        result[:, pl.ds(pl.multiple_of(at * wide, HEAD), wide)] = total
    scale = lax.rsqrt(squares * (1.0 / (TENSOR * LANES)) + epsilon)
    cosine, sine = cos_ref[...], sin_ref[...]
    heads = query_ref.shape[1] // HEAD
    for h in range(heads + 1):
        values = result[:, h * HEAD : (h + 1) * HEAD] * scale
        turned = (values * cosine + pltpu.roll(values, HEAD // 2, 1) * sine).astype(BF)
        if h < heads:
            query_ref[:, h * HEAD : (h + 1) * HEAD] = turned
        else:
            key_ref[...] = turned
    value_ref[...] = (result[:, (heads + 1) * HEAD :] * scale).astype(BF)


def project(place, rings, gain, cosine, sine, own, other):
    width = rings[0][0].shape[1]
    count = rings[0][0].shape[0] * len(rings)

    def kernel(*refs):
        project_kernel(len(rings), *refs)

    return pl.pallas_call(
        kernel,
        out_shape=(
            jax.ShapeDtypeStruct((count, width), BF),
            jax.ShapeDtypeStruct((count, HEAD), BF),
            jax.ShapeDtypeStruct((count, HEAD), BF),
        ),
        in_specs=[in_smem()] + [in_vmem()] * (RING * len(rings) + 3) + [anywhere()] * 32,
        out_specs=(in_vmem(),) * 3,
        scratch_shapes=[
            pltpu.VMEM((count, TENSOR * width), BF),
            pltpu.VMEM((count, TENSOR * width), BF),
            pltpu.VMEM((count, width + 2 * HEAD), F32),
        ]
        + weight_space((width + 2 * HEAD) // 2),
        compiler_params=params(),
        name="project",
    )(place, *[row for ring in rings for row in ring], gain, cosine, sine, *own, *other)


def attend_kernel(pairs, parts, place_ref, lens_ref, q_ref, k_ref, v_ref, *refs):
    own_refs, other_refs = refs[:16], refs[16:32]
    out_refs = refs[32 : 32 + RING * parts]
    mixed, terms, weights, sems = refs[32 + RING * parts :]
    copies = fetch(own_refs, other_refs, (q_ref.shape[1] + 2 * HEAD) // 2, weights, sems)
    x, z, y, core, way = place_of(place_ref)
    slots = 2 * SAMPLE
    heads = q_ref.shape[1] // HEAD
    step_t = lax.broadcasted_iota(jnp.int32, (slots, slots), 0)
    step_u = lax.broadcasted_iota(jnp.int32, (slots, slots), 1)
    for p in range(pairs):
        at = slice(p * slots, (p + 1) * slots)
        stacked = jnp.concatenate(
            [q_ref[at, h * HEAD : (h + 1) * HEAD] for h in range(heads)], axis=0
        )
        scores = lax.dot_general(
            stacked, k_ref[at, :], (((1,), (1,)), ((), ())), preferred_element_type=F32
        ) * (HEAD**-0.5)
        len_a = lens_ref[2 * p]
        len_b = lens_ref[2 * p + 1]
        limit = jnp.where(step_u < SAMPLE, len_a, len_b + SAMPLE)
        limit = jnp.minimum(limit, step_t + 1)
        closed = jnp.where(step_u < limit, 0.0, -1e30).astype(F32)
        scores = scores.reshape(heads, slots, slots) + closed[None]
        peak = jnp.max(scores, axis=-1, keepdims=True)
        raised = jnp.exp(scores - peak)
        probs = raised / jnp.sum(raised, axis=-1, keepdims=True)
        out = jnp.dot(
            probs.astype(BF).reshape(heads * slots, slots),
            v_ref[at, :],
            preferred_element_type=F32,
        ).astype(BF)
        for h in range(heads):
            mixed[at, h * HEAD : (h + 1) * HEAD] = out[h * slots : (h + 1) * slots]
    depth = 2 * PIECE
    mine = mixed[:, lane_block(core, depth)]
    theirs = mixed[:, lane_block(1 - core, depth)]
    for side in copies:
        for step in side:
            for copy in step:
                copy.wait()

    def product(values, side, s, m):
        block = weights[side, s, m]
        return jnp.dot(values[:, :PIECE], block[:, :PIECE], preferred_element_type=F32) + jnp.dot(
            values[:, PIECE:], block[:, PIECE:], preferred_element_type=F32
        )

    for s in range(RING):
        r = wrap((y - wrap(x - s * way)) * way)
        for m in range(RING):
            part = wrap(z - m * way)
            term = product(mine, 0, s, m) + product(
                theirs, 1, (RING - s) % RING, (RING - m) % RING
            )
            terms[r, :, lane_block(part, PIECE)] = term.astype(BF)
    count = pairs * slots // parts
    for r in range(RING):
        for c in range(parts):
            out_refs[r * parts + c][...] = terms[r, c * count : (c + 1) * count, :]


def attend(parts, place, lens, qkv, own, other):
    count, width = qkv[0].shape

    def kernel(*refs):
        attend_kernel(count // (2 * SAMPLE), parts, *refs)

    return pl.pallas_call(
        kernel,
        out_shape=(jax.ShapeDtypeStruct((count // parts, width), BF),) * (RING * parts),
        in_specs=[in_smem(), in_smem()] + [in_vmem()] * 3 + [anywhere()] * 32,
        out_specs=(in_vmem(),) * (RING * parts),
        scratch_shapes=[
            pltpu.VMEM((count, width), BF),
            pltpu.VMEM((RING, count, width), BF),
        ]
        + weight_space(2 * PIECE),
        compiler_params=params(),
        name="attend",
    )(place, lens, *qkv, *own, *other)


def finish_kernel(place_ref, gain_ref, b0, b1, b2, b3, *rest):
    out_ref = rest[-1]
    _, _, y, _, way = place_of(place_ref)
    values = [b[...].astype(F32) for b in (b0, b1, b2, b3)]
    squares = sum(jnp.sum(v * v, axis=-1, keepdims=True) for v in values)
    scale = lax.rsqrt(squares * (1.0 / (TENSOR * LANES)) + epsilon)
    for r in range(RING):
        lanes = lane_block(wrap(y - r * way), LANES)
        out_ref[:, lanes] = (values[r] * scale * gain_ref[:, lanes]).astype(BF)


def finish(place, gain, blocks, before, chunk, total):
    count, width = blocks[0].shape
    tile = 2 * SAMPLE
    steps = count // tile
    specs = [
        in_smem(),
        pl.BlockSpec((1, TENSOR * width), lambda i: (0, 0)),
    ] + [pl.BlockSpec((tile, width), lambda i: (i, 0))] * RING
    args = [place, gain, *blocks]
    aliases = {}
    if before is not None:
        specs.append(pl.BlockSpec(memory_space=pl.ANY))
        aliases = {len(args): 0}
        args.append(before)
    return pl.pallas_call(
        finish_kernel,
        grid=(steps,),
        out_shape=jax.ShapeDtypeStruct((total, TENSOR * width), BF),
        in_specs=specs,
        out_specs=pl.BlockSpec((tile, TENSOR * width), lambda i: (i + chunk * steps, 0)),
        input_output_aliases=aliases,
        compiler_params=params(),
        name="finish",
    )(*args)


def after(value, *others):
    return pl.pallas_call(
        lambda *refs: None,
        out_shape=jax.ShapeDtypeStruct(value.shape, value.dtype),
        in_specs=[anywhere()] * (1 + len(others)),
        out_specs=anywhere(),
        input_output_aliases={0: 0},
        name="after",
    )(value, *others)


def way_of(dp):
    return 1 - 2 * (dp % 2)


def along_y(values):
    pairs = [
        (dp * TENSOR + y, dp * TENSOR + (y + way_of(dp)) % TENSOR)
        for dp in range(4)
        for y in range(TENSOR)
    ]
    return lax.ppermute(values, ("dp", "tensor"), pairs)


def along_x(values):
    pairs = [
        (dp * 16 + x * 4 + z, dp * 16 + (x + way_of(dp)) % 4 * 4 + z)
        for dp in range(4)
        for x in range(4)
        for z in range(4)
    ]
    return lax.ppermute(values, ("dp", "fsdp"), pairs)


def along_z(values):
    pairs = [
        (dp * 16 + x * 4 + z, dp * 16 + x * 4 + (z + way_of(dp)) % 4)
        for dp in range(4)
        for x in range(4)
        for z in range(4)
    ]
    return lax.ppermute(values, ("dp", "fsdp"), pairs)


def other_core(values):
    return lax.ppermute(values, "dp", [(dp, dp ^ 1) for dp in range(4)])


def spread_x(rounds):
    own = [None] * 16
    for m in range(RING):
        block = rounds[m]
        for s in range(RING):
            own[RING * s + m] = block
            if s < 3:
                block = along_x(block)
    return own


def on_device(
    candidates, cand_lengths, pairing, attn_gain, w_query, w_key, w_value, w_out, ffn_gain
):
    me = lax.axis_index("fsdp")
    y = lax.axis_index("tensor")
    core = lax.rem(lax.axis_index("dp"), 2)
    place = jnp.stack([me // 4, lax.rem(me, 4), y, core]).astype(jnp.int32)
    cand_dev = candidates.shape[1]
    devices = lax.axis_size("fsdp")
    flat = pairing[0].reshape(devices, cand_dev)
    pick = jnp.sum(jnp.where(flat // cand_dev == me, lax.rem(flat, cand_dev), 0), axis=1)
    wanted = lax.dynamic_index_in_dim(flat, me, 0, keepdims=False)
    source = wanted // cand_dev

    half_cols = (w_query.shape[1] + w_key.shape[1] + w_value.shape[1]) // 2
    first = w_query[:, :half_cols]
    second = jnp.concatenate([w_query[:, half_cols:], w_key, w_value], axis=1)
    depth = w_out.shape[0] // 2
    third = jnp.where(core == 0, w_out[:depth], w_out[depth:])
    piece = jnp.concatenate(
        [jnp.where(core == 0, first, second), third[: depth // 2], third[depth // 2 :]], axis=1
    )
    rounds = [piece]
    for _ in range(3):
        rounds.append(along_z(rounds[-1]))
    own = spread_x(rounds)
    other = [other_core(block) for block in own]

    packed = pack(pick, cand_lengths[0], candidates[0], (), devices)
    incoming = lax.all_to_all(packed, "fsdp", split_axis=0, concat_axis=0, tiled=True)
    parts = 2
    local = unpack(source, incoming, (rounds[3],), parts)
    sent = incoming[:, -1, 0].astype(F32)
    slots = jnp.arange(devices, dtype=jnp.int32)
    lens = jnp.sum(
        jnp.where(source[:, None] == slots[None, :], sent[None, :], 0.0), axis=1
    ).astype(jnp.int32)


    gain_in = attn_gain.reshape(1, -1)
    gain_out = ffn_gain.reshape(1, -1)
    freq = rope_base ** (-jnp.arange(HEAD // 2, dtype=F32) * 2.0 / HEAD)
    starts = jnp.where(jnp.arange(cand_dev) % 2 == 0, 0, jnp.roll(lens, 1))
    positions = starts[:, None] + jnp.arange(SAMPLE, dtype=jnp.int32)[None, :]
    angles = positions.reshape(-1, 1).astype(F32) * freq[None, :]
    cosine, sine = jnp.cos(angles), jnp.sin(angles)
    cosine = jnp.concatenate([cosine, cosine], axis=1)
    sine = jnp.concatenate([-sine, sine], axis=1)

    width = candidates.shape[3]
    total = cand_dev * SAMPLE
    rings = [[rows] for rows in local]
    for _ in range(3):
        for ring in rings:
            ring.append(along_y(ring[-1]))
    qkv = project(place, rings, gain_in, cosine, sine, own, other)
    terms = attend(parts, place, lens, qkv, own, other)
    normed = None
    resids = []
    for c in range(parts):
        term = terms[c::parts]
        moving = along_y(term[1])
        for r in (2, 3):
            moving = along_y((moving.astype(F32) + term[r].astype(F32)).astype(BF))
        stream = local[c].astype(F32) + term[0].astype(F32) + moving.astype(F32)
        blocks = [stream.astype(BF)]
        for _ in range(3):
            blocks.append(along_y(blocks[-1]))
        resids.append(blocks[0])
        normed = finish(place, gain_out, blocks, normed, c, total)
    resid = jnp.concatenate(resids, axis=0)
    pair_dev = cand_dev // 2
    return (
        resid.reshape(1, pair_dev, 2 * SAMPLE, width),
        normed.reshape(1, pair_dev, 2 * SAMPLE, TENSOR * width),
    )


def solution(mesh):
    return jax.shard_map(
        on_device,
        mesh=mesh,
        in_specs=(
            P("dp", "fsdp", None, "tensor"),
            P("dp", "fsdp"),
            P("dp", None, None),
            P(),
            P("fsdp", "tensor"),
            P("fsdp", "tensor"),
            P("fsdp", "tensor"),
            P("tensor", "fsdp"),
            P(),
        ),
        out_specs=(P("dp", "fsdp", None, "tensor"), P("dp", "fsdp", None, None)),
        check_vma=False,
    )
```

```python
import jax
import jax.numpy as jnp
from jax import lax
from jax.experimental import pallas as pl
from jax.experimental.pallas import tpu as pltpu
from jax.sharding import PartitionSpec as P

HEAD = 128
SAMPLE = 64
TENSOR = 4
RING = 4
LANES = 1024
PIECE = 256
EXTRA = 16
epsilon = 1e-05
rope_base = 500000.0
BF = jnp.bfloat16
F32 = jnp.float32
VMEM_LIMIT = 40 * 1024 * 1024


def wrap(value):
    return lax.rem(value + 2 * RING, RING)


def in_vmem():
    return pl.BlockSpec(memory_space=pltpu.VMEM)


def in_smem():
    return pl.BlockSpec(memory_space=pltpu.SMEM)


def params(**kw):
    return pltpu.CompilerParams(vmem_limit_bytes=VMEM_LIMIT, **kw)


def pack_kernel(pick_ref, lens_ref, cand_ref, *refs):
    slots_ref = refs[-1]
    blocks = cand_ref.shape[2] // HEAD
    for slot in range(slots_ref.shape[0]):
        own = pick_ref[slot]
        for b in range(blocks):
            slots_ref[slot, b * SAMPLE : (b + 1) * SAMPLE, :] = cand_ref[
                own, :, b * HEAD : (b + 1) * HEAD
            ]
        length = jnp.full((EXTRA, HEAD), lens_ref[own], jnp.int32).astype(F32)
        slots_ref[slot, blocks * SAMPLE :, :] = length.astype(BF)


def pack(pick, lens, cands, earlier, slots):
    rows = cands.shape[2] // HEAD * SAMPLE + EXTRA
    return pl.pallas_call(
        pack_kernel,
        out_shape=jax.ShapeDtypeStruct((slots, rows, HEAD), BF),
        in_specs=[in_smem(), in_smem(), in_vmem()]
        + [pl.BlockSpec(memory_space=pl.ANY)] * len(earlier),
        out_specs=in_vmem(),
        compiler_params=params(),
        name="pack",
    )(pick, lens, cands, *earlier)


def unpack_kernel(earlier, source_ref, slots_ref, *refs):
    rows_refs = refs[earlier:]
    blocks = rows_refs[0].shape[1] // HEAD
    per = source_ref.shape[0] // len(rows_refs)
    for cand in range(source_ref.shape[0]):
        at = cand % per * SAMPLE
        for b in range(blocks):
            rows_refs[cand // per][at : at + SAMPLE, b * HEAD : (b + 1) * HEAD] = slots_ref[
                source_ref[cand], b * SAMPLE : (b + 1) * SAMPLE, :
            ]


def unpack(source, slots, earlier, parts):
    width = (slots.shape[1] - EXTRA) // SAMPLE * HEAD
    rows = source.shape[0] * SAMPLE // parts

    def kernel(*refs):
        unpack_kernel(len(earlier), *refs)

    return pl.pallas_call(
        kernel,
        out_shape=(jax.ShapeDtypeStruct((rows, width), BF),) * parts,
        in_specs=[in_smem(), in_vmem()] + [anywhere()] * len(earlier),
        out_specs=(in_vmem(),) * parts,
        compiler_params=params(),
        name="unpack",
    )(source, slots, *earlier)


def place_of(place_ref):
    x, z, y, core = place_ref[0], place_ref[1], place_ref[2], place_ref[3]
    return x, z, y, core, 1 - 2 * core


def lane_block(index, width):
    return pl.ds(pl.multiple_of(index * width, width), width)


def fetch(own_refs, other_refs, start, weights, sems):
    width = weights.shape[4]
    copies = []
    for side, blocks in enumerate((own_refs, other_refs)):
        copies.append([])
        for m, block in enumerate(blocks):
            copy = pltpu.make_async_copy(
                block.at[:, :, start : start + width], weights.at[side, m], sems.at[side, m]
            )
            copy.start()
            copies[side].append(copy)
    return copies


def weight_space(pieces, width):
    return [
        pltpu.VMEM((2, pieces, RING, PIECE, width), BF),
        pltpu.SemaphoreType.DMA((2, pieces)),
    ]


def anywhere():
    return pl.BlockSpec(memory_space=pl.ANY)


def prepare_kernel(parts, place_ref, gain_ref, *refs):
    rows_refs = [refs[RING * c : RING * c + RING] for c in range(parts)]
    own_main, own_last, other_main, other_last, scale_ref = refs[RING * parts :]
    x, z, y, _, way = place_of(place_ref)
    count = rows_refs[0][0].shape[0]
    squares = [jnp.zeros((count, 1), F32) for _ in range(parts)]
    for r in range(RING):
        block = wrap(y - r * way)
        s = wrap((x - block) * way)
        for m in range(RING):
            part = wrap(z - m * way)
            gain = gain_ref[:, lane_block(block * RING + part, PIECE)]
            target, base = (own_main, m * RING) if m < RING - 1 else (own_last, 0)
            for c in range(parts):
                piece = rows_refs[c][r][:, lane_block(part, PIECE)].astype(F32)
                squares[c] = squares[c] + jnp.sum(piece * piece, axis=-1, keepdims=True)
                target[c * count : (c + 1) * count, lane_block(base + s, PIECE)] = (
                    piece * gain
                ).astype(BF)

    def spot(m, s, main, last):
        if m < RING - 1:
            return main, slice((m * RING + s) * PIECE, (m * RING + s + 1) * PIECE)
        return last, slice(s * PIECE, (s + 1) * PIECE)

    for m in range(RING):
        for s in range(RING):
            to, lanes = spot(m, s, other_main, other_last)
            source, back = spot((RING - m) % RING, (RING - s) % RING, own_main, own_last)
            to[:, lanes] = source[:, back]
    mean = jnp.concatenate(squares, axis=0) * (1.0 / (TENSOR * LANES))
    scale_ref[...] = jnp.broadcast_to(lax.rsqrt(mean + epsilon), scale_ref.shape)


def prepare(place, gain, rings):
    width = rings[0][0].shape[1]
    count = rings[0][0].shape[0] * len(rings)

    def kernel(*refs):
        prepare_kernel(len(rings), *refs)

    main = jax.ShapeDtypeStruct((count, (RING - 1) * width), BF)
    last = jax.ShapeDtypeStruct((count, width), BF)
    return pl.pallas_call(
        kernel,
        out_shape=(main, last, main, last, jax.ShapeDtypeStruct((count, HEAD), F32)),
        in_specs=[in_smem()] + [in_vmem()] * (1 + RING * len(rings)),
        out_specs=(in_vmem(),) * 5,
        compiler_params=params(),
        name="prepare",
    )(place, gain, *[row for ring in rings for row in ring])


def partial_kernel(pieces, own_rows, other_rows, *refs):
    own_refs, other_refs = refs[:pieces], refs[pieces : 2 * pieces]
    own_out, other_out, weights, sems = refs[2 * pieces :]
    copies = fetch(own_refs, other_refs, 0, weights, sems)
    for side, (rows, out) in enumerate(((own_rows, own_out), (other_rows, other_out))):
        out[...] = sum_over(pieces, side, rows, weights, copies)


def sum_over(pieces, side, rows, weights, copies):
    total = None
    for m in range(pieces):
        copies[side][m].wait()
        term = jnp.dot(
            rows[:, m * LANES : (m + 1) * LANES],
            weights[side, m].reshape(LANES, weights.shape[4]),
            preferred_element_type=F32,
        )
        total = term if total is None else total + term
    return total


def partial(own_rows, other_rows, own, other, wide):
    count = own_rows.shape[0]
    pieces = len(own)

    def kernel(*refs):
        partial_kernel(pieces, *refs)

    return pl.pallas_call(
        kernel,
        out_shape=(jax.ShapeDtypeStruct((count, wide), F32),) * 2,
        in_specs=[in_vmem()] * 2 + [anywhere()] * (2 * pieces),
        out_specs=(in_vmem(),) * 2,
        scratch_shapes=weight_space(pieces, wide),
        compiler_params=params(),
        name="partial",
    )(own_rows, other_rows, *own, *other)


def project_kernel(place_ref, scale_ref, cos_ref, sin_ref, *refs):
    rows_refs, sums_refs = refs[:2], refs[2:4]
    own_ref, other_ref = refs[4:6]
    query_ref, key_ref, value_ref = refs[6:9]
    result, weights, sems = refs[9:12]
    core = place_ref[3]
    wide = weights.shape[4]
    copies = fetch((own_ref,), (other_ref,), 0, weights, sems)
    for side, at in enumerate((core, 1 - core)):
        term = sum_over(1, side, rows_refs[side], weights, copies)
        lanes = pl.ds(pl.multiple_of(at * wide, HEAD), wide)
        result[:, lanes] = sums_refs[side][...] + term
    scale, cosine, sine = scale_ref[...], cos_ref[...], sin_ref[...]
    cosine, sine = cosine * scale, sine * scale
    heads = query_ref.shape[1] // HEAD
    for h in range(heads + 1):
        values = result[:, h * HEAD : (h + 1) * HEAD]
        turned = (values * cosine + pltpu.roll(values, HEAD // 2, 1) * sine).astype(BF)
        if h < heads:
            query_ref[:, h * HEAD : (h + 1) * HEAD] = turned
        else:
            key_ref[...] = turned
    value_ref[...] = (result[:, (heads + 1) * HEAD :] * scale).astype(BF)


def project(place, scale, cosine, sine, rows, sums, own, other):
    count, width = rows[0].shape
    wide = sums[0].shape[1]
    return pl.pallas_call(
        project_kernel,
        out_shape=(
            jax.ShapeDtypeStruct((count, width), BF),
            jax.ShapeDtypeStruct((count, HEAD), BF),
            jax.ShapeDtypeStruct((count, HEAD), BF),
        ),
        in_specs=[in_smem()] + [in_vmem()] * 7 + [anywhere()] * 2,
        out_specs=(in_vmem(),) * 3,
        scratch_shapes=[pltpu.VMEM((count, 2 * wide), F32)] + weight_space(1, wide),
        compiler_params=params(),
        name="project",
    )(place, scale, cosine, sine, *rows, *sums, own, other)


def attend_kernel(pairs, parts, place_ref, lens_ref, q_ref, k_ref, v_ref, *refs):
    own_refs, other_refs = refs[:RING], refs[RING : 2 * RING]
    out_refs = refs[2 * RING : 2 * RING + RING * parts]
    mixed, terms, weights, sems = refs[2 * RING + RING * parts :]
    copies = fetch(own_refs, other_refs, (q_ref.shape[1] + 2 * HEAD) // 2, weights, sems)
    x, z, y, core, way = place_of(place_ref)
    slots = 2 * SAMPLE
    heads = q_ref.shape[1] // HEAD
    step_t = lax.broadcasted_iota(jnp.int32, (slots, slots), 0)
    step_u = lax.broadcasted_iota(jnp.int32, (slots, slots), 1)
    for p in range(pairs):
        at = slice(p * slots, (p + 1) * slots)
        stacked = jnp.concatenate(
            [q_ref[at, h * HEAD : (h + 1) * HEAD] for h in range(heads)], axis=0
        )
        scores = lax.dot_general(
            stacked, k_ref[at, :], (((1,), (1,)), ((), ())), preferred_element_type=F32
        ) * (HEAD**-0.5)
        len_a = lens_ref[2 * p]
        len_b = lens_ref[2 * p + 1]
        limit = jnp.where(step_u < SAMPLE, len_a, len_b + SAMPLE)
        limit = jnp.minimum(limit, step_t + 1)
        closed = jnp.where(step_u < limit, 0.0, -1e30).astype(F32)
        scores = scores.reshape(heads, slots, slots) + closed[None]
        peak = jnp.max(scores, axis=-1, keepdims=True)
        raised = jnp.exp(scores - peak)
        probs = raised / jnp.sum(raised, axis=-1, keepdims=True)
        out = jnp.dot(
            probs.astype(BF).reshape(heads * slots, slots),
            v_ref[at, :],
            preferred_element_type=F32,
        ).astype(BF)
        for h in range(heads):
            mixed[at, h * HEAD : (h + 1) * HEAD] = out[h * slots : (h + 1) * slots]
    depth = 2 * PIECE
    mine = mixed[:, lane_block(core, depth)]
    theirs = mixed[:, lane_block(1 - core, depth)]
    for side in copies:
        for copy in side:
            copy.wait()

    def product(values, side, s, m):
        block = weights[side, m, s]
        return jnp.dot(values[:, :PIECE], block[:, :PIECE], preferred_element_type=F32) + jnp.dot(
            values[:, PIECE:], block[:, PIECE:], preferred_element_type=F32
        )

    for s in range(RING):
        r = wrap((y - wrap(x - s * way)) * way)
        for m in range(RING):
            part = wrap(z - m * way)
            term = product(mine, 0, s, m) + product(
                theirs, 1, (RING - s) % RING, (RING - m) % RING
            )
            terms[r, :, lane_block(part, PIECE)] = term.astype(BF)
    count = pairs * slots // parts
    for r in range(RING):
        for c in range(parts):
            out_refs[r * parts + c][...] = terms[r, c * count : (c + 1) * count, :]


def attend(parts, place, lens, qkv, own, other):
    count, width = qkv[0].shape

    def kernel(*refs):
        attend_kernel(count // (2 * SAMPLE), parts, *refs)

    return pl.pallas_call(
        kernel,
        out_shape=(jax.ShapeDtypeStruct((count // parts, width), BF),) * (RING * parts),
        in_specs=[in_smem(), in_smem()] + [in_vmem()] * 3 + [anywhere()] * (2 * RING),
        out_specs=(in_vmem(),) * (RING * parts),
        scratch_shapes=[
            pltpu.VMEM((count, width), BF),
            pltpu.VMEM((RING, count, width), BF),
        ]
        + weight_space(RING, 2 * PIECE),
        compiler_params=params(),
        name="attend",
    )(place, lens, *qkv, *own, *other)


def finish_kernel(place_ref, gain_ref, b0, b1, b2, b3, *rest):
    out_ref = rest[-1]
    _, _, y, _, way = place_of(place_ref)
    values = [b[...].astype(F32) for b in (b0, b1, b2, b3)]
    squares = sum(jnp.sum(v * v, axis=-1, keepdims=True) for v in values)
    scale = lax.rsqrt(squares * (1.0 / (TENSOR * LANES)) + epsilon)
    for r in range(RING):
        lanes = lane_block(wrap(y - r * way), LANES)
        out_ref[:, lanes] = (values[r] * scale * gain_ref[:, lanes]).astype(BF)


def finish(place, gain, blocks, before, chunk, total):
    count, width = blocks[0].shape
    tile = 2 * SAMPLE
    steps = count // tile
    specs = [
        in_smem(),
        pl.BlockSpec((1, TENSOR * width), lambda i: (0, 0)),
    ] + [pl.BlockSpec((tile, width), lambda i: (i, 0))] * RING
    args = [place, gain, *blocks]
    aliases = {}
    if before is not None:
        specs.append(pl.BlockSpec(memory_space=pl.ANY))
        aliases = {len(args): 0}
        args.append(before)
    return pl.pallas_call(
        finish_kernel,
        grid=(steps,),
        out_shape=jax.ShapeDtypeStruct((total, TENSOR * width), BF),
        in_specs=specs,
        out_specs=pl.BlockSpec((tile, TENSOR * width), lambda i: (i + chunk * steps, 0)),
        input_output_aliases=aliases,
        compiler_params=params(),
        name="finish",
    )(*args)


def after(value, *others):
    return pl.pallas_call(
        lambda *refs: None,
        out_shape=jax.ShapeDtypeStruct(value.shape, value.dtype),
        in_specs=[anywhere()] * (1 + len(others)),
        out_specs=anywhere(),
        input_output_aliases={0: 0},
        name="after",
    )(value, *others)


def way_of(dp):
    return 1 - 2 * (dp % 2)


def along_y(values):
    pairs = [
        (dp * TENSOR + y, dp * TENSOR + (y + way_of(dp)) % TENSOR)
        for dp in range(4)
        for y in range(TENSOR)
    ]
    return lax.ppermute(values, ("dp", "tensor"), pairs)


def along_x(values):
    pairs = [
        (dp * 16 + x * 4 + z, dp * 16 + (x + way_of(dp)) % 4 * 4 + z)
        for dp in range(4)
        for x in range(4)
        for z in range(4)
    ]
    return lax.ppermute(values, ("dp", "fsdp"), pairs)


def along_z(values):
    pairs = [
        (dp * 16 + x * 4 + z, dp * 16 + x * 4 + (z + way_of(dp)) % 4)
        for dp in range(4)
        for x in range(4)
        for z in range(4)
    ]
    return lax.ppermute(values, ("dp", "fsdp"), pairs)


def other_core(values):
    return lax.ppermute(values, "dp", [(dp, dp ^ 1) for dp in range(4)])


def spread_x(piece):
    rounds = [piece]
    for _ in range(3):
        rounds.append(along_x(rounds[-1]))
    return rounds


def on_device(
    candidates, cand_lengths, pairing, attn_gain, w_query, w_key, w_value, w_out, ffn_gain
):
    me = lax.axis_index("fsdp")
    y = lax.axis_index("tensor")
    core = lax.rem(lax.axis_index("dp"), 2)
    place = jnp.stack([me // 4, lax.rem(me, 4), y, core]).astype(jnp.int32)
    cand_dev = candidates.shape[1]
    devices = lax.axis_size("fsdp")
    flat = pairing[0].reshape(devices, cand_dev)
    pick = jnp.sum(jnp.where(flat // cand_dev == me, lax.rem(flat, cand_dev), 0), axis=1)
    wanted = lax.dynamic_index_in_dim(flat, me, 0, keepdims=False)
    source = wanted // cand_dev

    half_cols = (w_query.shape[1] + w_key.shape[1] + w_value.shape[1]) // 2
    first = w_query[:, :half_cols]
    second = jnp.concatenate([w_query[:, half_cols:], w_key, w_value], axis=1)
    depth = w_out.shape[0] // 2
    third = jnp.where(core == 0, w_out[:depth], w_out[depth:])
    piece = jnp.concatenate(
        [jnp.where(core == 0, first, second), third[: depth // 2], third[depth // 2 :]], axis=1
    )
    rounds = [piece, along_z(piece)]

    spread = [spread_x(block) for block in rounds]
    rounds.append(along_z(after(rounds[1], spread[0][3], spread[1][3])))

    packed = pack(pick, cand_lengths[0], candidates[0], (rounds[1],), devices)
    incoming = lax.all_to_all(packed, "fsdp", split_axis=0, concat_axis=0, tiled=True)
    parts = 2
    local = unpack(source, incoming, (spread[0][3], spread[1][3]), parts)
    rings = [[rows] for rows in local]
    block = after(rounds[2], local[0])
    spread.append(spread_x(block))
    block = along_z(block)
    spread.append([])
    for step in range(RING):
        spread[3].append(block)
        if step < 3:
            for ring in rings:
                ring.append(along_y(ring[-1]))
            block = along_x(after(block, rings[0][-1], rings[1][-1]))
    own = [jnp.stack(blocks) for blocks in spread]
    other = [other_core(blocks) for blocks in own]
    sent = incoming[:, -1, 0].astype(F32)
    slots = jnp.arange(devices, dtype=jnp.int32)
    lens = jnp.sum(
        jnp.where(source[:, None] == slots[None, :], sent[None, :], 0.0), axis=1
    ).astype(jnp.int32)


    gain_in = attn_gain.reshape(1, -1)
    gain_out = ffn_gain.reshape(1, -1)
    freq = rope_base ** (-jnp.arange(HEAD // 2, dtype=F32) * 2.0 / HEAD)
    starts = jnp.where(jnp.arange(cand_dev) % 2 == 0, 0, jnp.roll(lens, 1))
    positions = starts[:, None] + jnp.arange(SAMPLE, dtype=jnp.int32)[None, :]
    angles = positions.reshape(-1, 1).astype(F32) * freq[None, :]
    cosine, sine = jnp.cos(angles), jnp.sin(angles)
    cosine = jnp.concatenate([cosine, cosine], axis=1)
    sine = jnp.concatenate([-sine, sine], axis=1)

    width = candidates.shape[3]
    total = cand_dev * SAMPLE
    own_main, own_last, other_main, other_last, scale = prepare(place, gain_in, rings)
    sums = partial(own_main, other_main, own[:3], other[:3], half_cols)
    qkv = project(
        place, scale, cosine, sine, (own_last, other_last), sums, own[3], other[3]
    )
    terms = attend(parts, place, lens, qkv, own, other)
    normed = None
    resids = []
    for c in range(parts):
        term = terms[c::parts]
        moving = along_y(term[1])
        for r in (2, 3):
            moving = along_y((moving.astype(F32) + term[r].astype(F32)).astype(BF))
        stream = local[c].astype(F32) + term[0].astype(F32) + moving.astype(F32)
        blocks = [stream.astype(BF)]
        for _ in range(3):
            blocks.append(along_y(blocks[-1]))
        resids.append(blocks[0])
        normed = finish(place, gain_out, blocks, normed, c, total)
    resid = jnp.concatenate(resids, axis=0)
    pair_dev = cand_dev // 2
    return (
        resid.reshape(1, pair_dev, 2 * SAMPLE, width),
        normed.reshape(1, pair_dev, 2 * SAMPLE, TENSOR * width),
    )


def solution(mesh):
    return jax.shard_map(
        on_device,
        mesh=mesh,
        in_specs=(
            P("dp", "fsdp", None, "tensor"),
            P("dp", "fsdp"),
            P("dp", None, None),
            P(),
            P("fsdp", "tensor"),
            P("fsdp", "tensor"),
            P("fsdp", "tensor"),
            P("tensor", "fsdp"),
            P(),
        ),
        out_specs=(P("dp", "fsdp", None, "tensor"), P("dp", "fsdp", None, None)),
        check_vma=False,
    )
```

```python
import jax
import jax.numpy as jnp
from jax import lax
from jax.experimental import pallas as pl
from jax.experimental.pallas import tpu as pltpu
from jax.sharding import PartitionSpec as P

HEAD = 128
SAMPLE = 64
TENSOR = 4
RING = 4
LANES = 1024
PIECE = 256
EXTRA = 16
epsilon = 1e-05
rope_base = 500000.0
BF = jnp.bfloat16
F32 = jnp.float32
VMEM_LIMIT = 40 * 1024 * 1024


def wrap(value):
    return lax.rem(value + 2 * RING, RING)


def in_vmem():
    return pl.BlockSpec(memory_space=pltpu.VMEM)


def in_smem():
    return pl.BlockSpec(memory_space=pltpu.SMEM)


def params(**kw):
    return pltpu.CompilerParams(vmem_limit_bytes=VMEM_LIMIT, **kw)


def pack_kernel(pick_ref, lens_ref, cand_ref, *refs):
    slots_ref = refs[-1]
    blocks = cand_ref.shape[2] // HEAD
    for slot in range(slots_ref.shape[0]):
        own = pick_ref[slot]
        for b in range(blocks):
            slots_ref[slot, b * SAMPLE : (b + 1) * SAMPLE, :] = cand_ref[
                own, :, b * HEAD : (b + 1) * HEAD
            ]
        length = jnp.full((EXTRA, HEAD), lens_ref[own], jnp.int32).astype(F32)
        slots_ref[slot, blocks * SAMPLE :, :] = length.astype(BF)


def pack(pick, lens, cands, earlier, slots):
    rows = cands.shape[2] // HEAD * SAMPLE + EXTRA
    return pl.pallas_call(
        pack_kernel,
        out_shape=jax.ShapeDtypeStruct((slots, rows, HEAD), BF),
        in_specs=[in_smem(), in_smem(), in_vmem()]
        + [pl.BlockSpec(memory_space=pl.ANY)] * len(earlier),
        out_specs=in_vmem(),
        compiler_params=params(),
        name="pack",
    )(pick, lens, cands, *earlier)


def unpack_kernel(earlier, source_ref, slots_ref, *refs):
    rows_refs = refs[earlier:]
    blocks = rows_refs[0].shape[1] // HEAD
    per = source_ref.shape[0] // len(rows_refs)
    for cand in range(source_ref.shape[0]):
        at = cand % per * SAMPLE
        for b in range(blocks):
            rows_refs[cand // per][at : at + SAMPLE, b * HEAD : (b + 1) * HEAD] = slots_ref[
                source_ref[cand], b * SAMPLE : (b + 1) * SAMPLE, :
            ]


def unpack(source, slots, earlier, parts):
    width = (slots.shape[1] - EXTRA) // SAMPLE * HEAD
    rows = source.shape[0] * SAMPLE // parts

    def kernel(*refs):
        unpack_kernel(len(earlier), *refs)

    return pl.pallas_call(
        kernel,
        out_shape=(jax.ShapeDtypeStruct((rows, width), BF),) * parts,
        in_specs=[in_smem(), in_vmem()] + [anywhere()] * len(earlier),
        out_specs=(in_vmem(),) * parts,
        compiler_params=params(),
        name="unpack",
    )(source, slots, *earlier)


def place_of(place_ref):
    x, z, y, core = place_ref[0], place_ref[1], place_ref[2], place_ref[3]
    return x, z, y, core, 1 - 2 * core


def lane_block(index, width):
    return pl.ds(pl.multiple_of(index * width, width), width)


def fetch(own_refs, other_refs, start, weights, sems):
    width = weights.shape[4]
    copies = []
    for side, blocks in enumerate((own_refs, other_refs)):
        copies.append([])
        for m, block in enumerate(blocks):
            copy = pltpu.make_async_copy(
                block.at[:, :, start : start + width], weights.at[side, m], sems.at[side, m]
            )
            copy.start()
            copies[side].append(copy)
    return copies


def weight_space(pieces, width):
    return [
        pltpu.VMEM((2, pieces, RING, PIECE, width), BF),
        pltpu.SemaphoreType.DMA((2, pieces)),
    ]


def anywhere():
    return pl.BlockSpec(memory_space=pl.ANY)


def prepare_kernel(parts, place_ref, gain_ref, *refs):
    rows_refs = [refs[RING * c : RING * c + RING] for c in range(parts)]
    own_main, own_last, other_main, other_last, scale_ref = refs[RING * parts :]
    x, z, y, _, way = place_of(place_ref)
    count = rows_refs[0][0].shape[0]
    squares = [jnp.zeros((count, 1), F32) for _ in range(parts)]
    for r in range(RING):
        block = wrap(y - r * way)
        s = wrap((x - block) * way)
        for m in range(RING):
            part = wrap(z - m * way)
            gain = gain_ref[:, lane_block(block * RING + part, PIECE)]
            target, base = (own_main, m * RING) if m < RING - 1 else (own_last, 0)
            for c in range(parts):
                piece = rows_refs[c][r][:, lane_block(part, PIECE)].astype(F32)
                squares[c] = squares[c] + jnp.sum(piece * piece, axis=-1, keepdims=True)
                target[c * count : (c + 1) * count, lane_block(base + s, PIECE)] = (
                    piece * gain
                ).astype(BF)

    def spot(m, s, main, last):
        if m < RING - 1:
            return main, slice((m * RING + s) * PIECE, (m * RING + s + 1) * PIECE)
        return last, slice(s * PIECE, (s + 1) * PIECE)

    for m in range(RING):
        for s in range(RING):
            to, lanes = spot(m, s, other_main, other_last)
            source, back = spot((RING - m) % RING, (RING - s) % RING, own_main, own_last)
            to[:, lanes] = source[:, back]
    mean = jnp.concatenate(squares, axis=0) * (1.0 / (TENSOR * LANES))
    scale_ref[...] = jnp.broadcast_to(lax.rsqrt(mean + epsilon), scale_ref.shape)


def prepare(place, gain, rings):
    width = rings[0][0].shape[1]
    count = rings[0][0].shape[0] * len(rings)

    def kernel(*refs):
        prepare_kernel(len(rings), *refs)

    main = jax.ShapeDtypeStruct((count, (RING - 1) * width), BF)
    last = jax.ShapeDtypeStruct((count, width), BF)
    return pl.pallas_call(
        kernel,
        out_shape=(main, last, main, last, jax.ShapeDtypeStruct((count, HEAD), F32)),
        in_specs=[in_smem()] + [in_vmem()] * (1 + RING * len(rings)),
        out_specs=(in_vmem(),) * 5,
        compiler_params=params(),
        name="prepare",
    )(place, gain, *[row for ring in rings for row in ring])


def partial_kernel(pieces, own_rows, other_rows, *refs):
    own_refs, other_refs = refs[:pieces], refs[pieces : 2 * pieces]
    own_out, other_out, weights, sems = refs[2 * pieces :]
    copies = fetch(own_refs, other_refs, 0, weights, sems)
    for side, (rows, out) in enumerate(((own_rows, own_out), (other_rows, other_out))):
        for copy in copies[side]:
            copy.wait()
        for at in range(0, rows.shape[0], PIECE):
            out[at : at + PIECE, :] = sum_over(pieces, side, rows, at, weights)


def sum_over(pieces, side, rows, at, weights):
    total = None
    for m in range(pieces):
        term = jnp.dot(
            rows[at : at + PIECE, m * LANES : (m + 1) * LANES],
            weights[side, m].reshape(LANES, weights.shape[4]),
            preferred_element_type=F32,
        )
        total = term if total is None else total + term
    return total


def partial(own_rows, other_rows, own, other, wide):
    count = own_rows.shape[0]
    pieces = len(own)

    def kernel(*refs):
        partial_kernel(pieces, *refs)

    return pl.pallas_call(
        kernel,
        out_shape=(jax.ShapeDtypeStruct((count, wide), F32),) * 2,
        in_specs=[in_vmem()] * 2 + [anywhere()] * (2 * pieces),
        out_specs=(in_vmem(),) * 2,
        scratch_shapes=weight_space(pieces, wide),
        compiler_params=params(),
        name="partial",
    )(own_rows, other_rows, *own, *other)


def project_kernel(place_ref, scale_ref, cos_ref, sin_ref, *refs):
    rows_refs, sums_refs = refs[:2], refs[2:4]
    own_ref, other_ref = refs[4:6]
    query_ref, key_ref, value_ref = refs[6:9]
    result, weights, sems = refs[9:12]
    core = place_ref[3]
    wide = weights.shape[4]
    copies = fetch((own_ref,), (other_ref,), 0, weights, sems)
    for side, at in enumerate((core, 1 - core)):
        copies[side][0].wait()
        lanes = pl.ds(pl.multiple_of(at * wide, HEAD), wide)
        for row in range(0, result.shape[0], PIECE):
            term = sum_over(1, side, rows_refs[side], row, weights)
            result[row : row + PIECE, lanes] = sums_refs[side][row : row + PIECE, :] + term
    scale, cosine, sine = scale_ref[...], cos_ref[...], sin_ref[...]
    cosine, sine = cosine * scale, sine * scale
    heads = query_ref.shape[1] // HEAD
    for h in range(heads + 1):
        values = result[:, h * HEAD : (h + 1) * HEAD]
        turned = (values * cosine + pltpu.roll(values, HEAD // 2, 1) * sine).astype(BF)
        if h < heads:
            query_ref[:, h * HEAD : (h + 1) * HEAD] = turned
        else:
            key_ref[...] = turned
    value_ref[...] = (result[:, (heads + 1) * HEAD :] * scale).astype(BF)


def project(place, scale, cosine, sine, rows, sums, own, other):
    count, width = rows[0].shape
    wide = sums[0].shape[1]
    return pl.pallas_call(
        project_kernel,
        out_shape=(
            jax.ShapeDtypeStruct((count, width), BF),
            jax.ShapeDtypeStruct((count, HEAD), BF),
            jax.ShapeDtypeStruct((count, HEAD), BF),
        ),
        in_specs=[in_smem()] + [in_vmem()] * 7 + [anywhere()] * 2,
        out_specs=(in_vmem(),) * 3,
        scratch_shapes=[pltpu.VMEM((count, 2 * wide), F32)] + weight_space(1, wide),
        compiler_params=params(),
        name="project",
    )(place, scale, cosine, sine, *rows, *sums, own, other)


def attend_kernel(pairs, parts, place_ref, lens_ref, q_ref, k_ref, v_ref, *refs):
    own_refs, other_refs = refs[:RING], refs[RING : 2 * RING]
    out_refs = refs[2 * RING : 2 * RING + RING * parts]
    mixed, terms, weights, sems = refs[2 * RING + RING * parts :]
    copies = fetch(own_refs, other_refs, (q_ref.shape[1] + 2 * HEAD) // 2, weights, sems)
    x, z, y, core, way = place_of(place_ref)
    slots = 2 * SAMPLE
    heads = q_ref.shape[1] // HEAD
    step_t = lax.broadcasted_iota(jnp.int32, (slots, slots), 0)
    step_u = lax.broadcasted_iota(jnp.int32, (slots, slots), 1)
    for p in range(pairs):
        at = slice(p * slots, (p + 1) * slots)
        stacked = jnp.concatenate(
            [q_ref[at, h * HEAD : (h + 1) * HEAD] for h in range(heads)], axis=0
        )
        scores = lax.dot_general(
            stacked, k_ref[at, :], (((1,), (1,)), ((), ())), preferred_element_type=F32
        ) * (HEAD**-0.5)
        len_a = lens_ref[2 * p]
        len_b = lens_ref[2 * p + 1]
        limit = jnp.where(step_u < SAMPLE, len_a, len_b + SAMPLE)
        limit = jnp.minimum(limit, step_t + 1)
        closed = jnp.where(step_u < limit, 0.0, -1e30).astype(F32)
        scores = scores.reshape(heads, slots, slots) + closed[None]
        peak = jnp.max(scores, axis=-1, keepdims=True)
        raised = jnp.exp(scores - peak)
        probs = raised / jnp.sum(raised, axis=-1, keepdims=True)
        out = jnp.dot(
            probs.astype(BF).reshape(heads * slots, slots),
            v_ref[at, :],
            preferred_element_type=F32,
        ).astype(BF)
        for h in range(heads):
            mixed[at, h * HEAD : (h + 1) * HEAD] = out[h * slots : (h + 1) * slots]
    depth = 2 * PIECE
    mine = mixed[:, lane_block(core, depth)]
    theirs = mixed[:, lane_block(1 - core, depth)]
    for side in copies:
        for copy in side:
            copy.wait()

    def product(values, side, s, m):
        block = weights[side, m, s]
        return jnp.dot(values[:, :PIECE], block[:, :PIECE], preferred_element_type=F32) + jnp.dot(
            values[:, PIECE:], block[:, PIECE:], preferred_element_type=F32
        )

    for s in range(RING):
        r = wrap((y - wrap(x - s * way)) * way)
        for m in range(RING):
            part = wrap(z - m * way)
            term = product(mine, 0, s, m) + product(
                theirs, 1, (RING - s) % RING, (RING - m) % RING
            )
            terms[r, :, lane_block(part, PIECE)] = term.astype(BF)
    count = pairs * slots // parts
    for r in range(RING):
        for c in range(parts):
            out_refs[r * parts + c][...] = terms[r, c * count : (c + 1) * count, :]


def attend(parts, place, lens, qkv, own, other):
    count, width = qkv[0].shape

    def kernel(*refs):
        attend_kernel(count // (2 * SAMPLE), parts, *refs)

    return pl.pallas_call(
        kernel,
        out_shape=(jax.ShapeDtypeStruct((count // parts, width), BF),) * (RING * parts),
        in_specs=[in_smem(), in_smem()] + [in_vmem()] * 3 + [anywhere()] * (2 * RING),
        out_specs=(in_vmem(),) * (RING * parts),
        scratch_shapes=[
            pltpu.VMEM((count, width), BF),
            pltpu.VMEM((RING, count, width), BF),
        ]
        + weight_space(RING, 2 * PIECE),
        compiler_params=params(),
        name="attend",
    )(place, lens, *qkv, *own, *other)


def finish_kernel(place_ref, gain_ref, b0, b1, b2, b3, *rest):
    out_ref = rest[-1]
    _, _, y, _, way = place_of(place_ref)
    values = [b[...].astype(F32) for b in (b0, b1, b2, b3)]
    squares = sum(jnp.sum(v * v, axis=-1, keepdims=True) for v in values)
    scale = lax.rsqrt(squares * (1.0 / (TENSOR * LANES)) + epsilon)
    for r in range(RING):
        lanes = lane_block(wrap(y - r * way), LANES)
        out_ref[:, lanes] = (values[r] * scale * gain_ref[:, lanes]).astype(BF)


def finish(place, gain, blocks, before, chunk, total):
    count, width = blocks[0].shape
    tile = 2 * SAMPLE
    steps = count // tile
    specs = [
        in_smem(),
        pl.BlockSpec((1, TENSOR * width), lambda i: (0, 0)),
    ] + [pl.BlockSpec((tile, width), lambda i: (i, 0))] * RING
    args = [place, gain, *blocks]
    aliases = {}
    if before is not None:
        specs.append(pl.BlockSpec(memory_space=pl.ANY))
        aliases = {len(args): 0}
        args.append(before)
    return pl.pallas_call(
        finish_kernel,
        grid=(steps,),
        out_shape=jax.ShapeDtypeStruct((total, TENSOR * width), BF),
        in_specs=specs,
        out_specs=pl.BlockSpec((tile, TENSOR * width), lambda i: (i + chunk * steps, 0)),
        input_output_aliases=aliases,
        compiler_params=params(),
        name="finish",
    )(*args)


def after(value, *others):
    return pl.pallas_call(
        lambda *refs: None,
        out_shape=jax.ShapeDtypeStruct(value.shape, value.dtype),
        in_specs=[anywhere()] * (1 + len(others)),
        out_specs=anywhere(),
        input_output_aliases={0: 0},
        name="after",
    )(value, *others)


def way_of(dp):
    return 1 - 2 * (dp % 2)


def along_y(values):
    pairs = [
        (dp * TENSOR + y, dp * TENSOR + (y + way_of(dp)) % TENSOR)
        for dp in range(4)
        for y in range(TENSOR)
    ]
    return lax.ppermute(values, ("dp", "tensor"), pairs)


def along_x(values):
    pairs = [
        (dp * 16 + x * 4 + z, dp * 16 + (x + way_of(dp)) % 4 * 4 + z)
        for dp in range(4)
        for x in range(4)
        for z in range(4)
    ]
    return lax.ppermute(values, ("dp", "fsdp"), pairs)


def along_z(values):
    pairs = [
        (dp * 16 + x * 4 + z, dp * 16 + x * 4 + (z + way_of(dp)) % 4)
        for dp in range(4)
        for x in range(4)
        for z in range(4)
    ]
    return lax.ppermute(values, ("dp", "fsdp"), pairs)


def other_core(values):
    return lax.ppermute(values, "dp", [(dp, dp ^ 1) for dp in range(4)])


def spread_x(piece):
    rounds = [piece]
    for _ in range(3):
        rounds.append(along_x(rounds[-1]))
    return rounds


def on_device(
    candidates, cand_lengths, pairing, attn_gain, w_query, w_key, w_value, w_out, ffn_gain
):
    me = lax.axis_index("fsdp")
    y = lax.axis_index("tensor")
    core = lax.rem(lax.axis_index("dp"), 2)
    place = jnp.stack([me // 4, lax.rem(me, 4), y, core]).astype(jnp.int32)
    cand_dev = candidates.shape[1]
    devices = lax.axis_size("fsdp")
    flat = pairing[0].reshape(devices, cand_dev)
    pick = jnp.sum(jnp.where(flat // cand_dev == me, lax.rem(flat, cand_dev), 0), axis=1)
    wanted = lax.dynamic_index_in_dim(flat, me, 0, keepdims=False)
    source = wanted // cand_dev

    half_cols = (w_query.shape[1] + w_key.shape[1] + w_value.shape[1]) // 2
    first = w_query[:, :half_cols]
    second = jnp.concatenate([w_query[:, half_cols:], w_key, w_value], axis=1)
    depth = w_out.shape[0] // 2
    third = jnp.where(core == 0, w_out[:depth], w_out[depth:])
    piece = jnp.concatenate(
        [jnp.where(core == 0, first, second), third[: depth // 2], third[depth // 2 :]], axis=1
    )
    rounds = [piece, along_z(piece)]

    spread = [spread_x(piece)]

    packed = pack(pick, cand_lengths[0], candidates[0], (), devices)
    incoming = lax.all_to_all(packed, "fsdp", split_axis=0, concat_axis=0, tiled=True)
    parts = 2
    local = unpack(source, incoming, (spread[0][3],), parts)
    rings = [[rows] for rows in local]
    first = after(rounds[1], local[0])
    spread.append(spread_x(first))
    second = along_z(first)
    block = None
    last = []
    for step in range(RING):
        if step < 3:
            for ring in rings:
                ring.append(along_y(ring[-1]))
            fresh = (rings[0][-1], rings[1][-1])
        if step == 0:
            second = after(second, *fresh, spread[1][1])
            spread.append(spread_x(second))
            block = along_z(second)
        else:
            last.append(block)
            block = along_x(after(block, *fresh))
    last.append(block)
    spread.append(last)
    own = [jnp.stack(blocks) for blocks in spread]
    other = [other_core(blocks) for blocks in own]
    sent = incoming[:, -1, 0].astype(F32)
    slots = jnp.arange(devices, dtype=jnp.int32)
    lens = jnp.sum(
        jnp.where(source[:, None] == slots[None, :], sent[None, :], 0.0), axis=1
    ).astype(jnp.int32)


    gain_in = attn_gain.reshape(1, -1)
    gain_out = ffn_gain.reshape(1, -1)
    freq = rope_base ** (-jnp.arange(HEAD // 2, dtype=F32) * 2.0 / HEAD)
    starts = jnp.where(jnp.arange(cand_dev) % 2 == 0, 0, jnp.roll(lens, 1))
    positions = starts[:, None] + jnp.arange(SAMPLE, dtype=jnp.int32)[None, :]
    angles = positions.reshape(-1, 1).astype(F32) * freq[None, :]
    cosine, sine = jnp.cos(angles), jnp.sin(angles)
    cosine = jnp.concatenate([cosine, cosine], axis=1)
    sine = jnp.concatenate([-sine, sine], axis=1)

    width = candidates.shape[3]
    total = cand_dev * SAMPLE
    own_main, own_last, other_main, other_last, scale = prepare(place, gain_in, rings)
    sums = partial(own_main, other_main, own[:3], other[:3], half_cols)
    qkv = project(
        place, scale, cosine, sine, (own_last, other_last), sums, own[3], other[3]
    )
    terms = attend(parts, place, lens, qkv, own, other)
    normed = None
    resids = []
    for c in range(parts):
        term = terms[c::parts]
        moving = along_y(term[1])
        for r in (2, 3):
            moving = along_y((moving.astype(F32) + term[r].astype(F32)).astype(BF))
        stream = local[c].astype(F32) + term[0].astype(F32) + moving.astype(F32)
        blocks = [stream.astype(BF)]
        for _ in range(3):
            blocks.append(along_y(blocks[-1]))
        resids.append(blocks[0])
        normed = finish(place, gain_out, blocks, normed, c, total)
    resid = jnp.concatenate(resids, axis=0)
    pair_dev = cand_dev // 2
    return (
        resid.reshape(1, pair_dev, 2 * SAMPLE, width),
        normed.reshape(1, pair_dev, 2 * SAMPLE, TENSOR * width),
    )


def solution(mesh):
    return jax.shard_map(
        on_device,
        mesh=mesh,
        in_specs=(
            P("dp", "fsdp", None, "tensor"),
            P("dp", "fsdp"),
            P("dp", None, None),
            P(),
            P("fsdp", "tensor"),
            P("fsdp", "tensor"),
            P("fsdp", "tensor"),
            P("tensor", "fsdp"),
            P(),
        ),
        out_specs=(P("dp", "fsdp", None, "tensor"), P("dp", "fsdp", None, None)),
        check_vma=False,
    )
```

```python
import jax
import jax.numpy as jnp
from jax import lax
from jax.experimental import pallas as pl
from jax.experimental.pallas import tpu as pltpu
from jax.sharding import PartitionSpec as P

HEAD = 128
SAMPLE = 64
TENSOR = 4
RING = 4
LANES = 1024
PIECE = 256
EXTRA = 16
GROUPS = ((0, 1), (1, 2), (2, 4))
epsilon = 1e-05
rope_base = 500000.0
BF = jnp.bfloat16
F32 = jnp.float32
VMEM_LIMIT = 40 * 1024 * 1024


def wrap(value):
    return lax.rem(value + 2 * RING, RING)


def in_vmem():
    return pl.BlockSpec(memory_space=pltpu.VMEM)


def in_smem():
    return pl.BlockSpec(memory_space=pltpu.SMEM)


def params(**kw):
    return pltpu.CompilerParams(vmem_limit_bytes=VMEM_LIMIT, **kw)


def pack_kernel(pick_ref, lens_ref, cand_ref, *refs):
    slots_ref = refs[-1]
    blocks = cand_ref.shape[2] // HEAD
    for slot in range(slots_ref.shape[0]):
        own = pick_ref[slot]
        for b in range(blocks):
            slots_ref[slot, b * SAMPLE : (b + 1) * SAMPLE, :] = cand_ref[
                own, :, b * HEAD : (b + 1) * HEAD
            ]
        length = jnp.full((EXTRA, HEAD), lens_ref[own], jnp.int32).astype(F32)
        slots_ref[slot, blocks * SAMPLE :, :] = length.astype(BF)


def pack(pick, lens, cands, earlier, slots):
    rows = cands.shape[2] // HEAD * SAMPLE + EXTRA
    return pl.pallas_call(
        pack_kernel,
        out_shape=jax.ShapeDtypeStruct((slots, rows, HEAD), BF),
        in_specs=[in_smem(), in_smem(), in_vmem()]
        + [pl.BlockSpec(memory_space=pl.ANY)] * len(earlier),
        out_specs=in_vmem(),
        compiler_params=params(),
        name="pack",
    )(pick, lens, cands, *earlier)


def unpack_kernel(earlier, source_ref, slots_ref, *refs):
    rows_refs = refs[earlier:]
    blocks = rows_refs[0].shape[1] // HEAD
    per = source_ref.shape[0] // len(rows_refs)
    for cand in range(source_ref.shape[0]):
        at = cand % per * SAMPLE
        for b in range(blocks):
            rows_refs[cand // per][at : at + SAMPLE, b * HEAD : (b + 1) * HEAD] = slots_ref[
                source_ref[cand], b * SAMPLE : (b + 1) * SAMPLE, :
            ]


def unpack(source, slots, earlier, parts):
    width = (slots.shape[1] - EXTRA) // SAMPLE * HEAD
    rows = source.shape[0] * SAMPLE // parts

    def kernel(*refs):
        unpack_kernel(len(earlier), *refs)

    return pl.pallas_call(
        kernel,
        out_shape=(jax.ShapeDtypeStruct((rows, width), BF),) * parts,
        in_specs=[in_smem(), in_vmem()] + [anywhere()] * len(earlier),
        out_specs=(in_vmem(),) * parts,
        compiler_params=params(),
        name="unpack",
    )(source, slots, *earlier)


def place_of(place_ref):
    x, z, y, core = place_ref[0], place_ref[1], place_ref[2], place_ref[3]
    return x, z, y, core, 1 - 2 * core


def lane_block(index, width):
    return pl.ds(pl.multiple_of(index * width, width), width)


def fetch(own_refs, other_refs, start, weights, sems):
    width = weights.shape[4]
    copies = []
    for side, blocks in enumerate((own_refs, other_refs)):
        copies.append([])
        for s in range(RING):
            copies[side].append([])
            for g, (lo, hi) in enumerate(GROUPS):
                copy = pltpu.make_async_copy(
                    blocks[3 * s + g].at[:, :, start : start + width],
                    weights.at[side, s, 2 * lo : 2 * hi],
                    sems.at[side, s, g],
                )
                copy.start()
                copies[side][s].append(copy)
    return copies


def weight_space(width):
    return [
        pltpu.VMEM((2, RING, 2 * RING, PIECE // 2, width), BF),
        pltpu.SemaphoreType.DMA((2, RING, len(GROUPS))),
    ]


def anywhere():
    return pl.BlockSpec(memory_space=pl.ANY)


def project_kernel(place_ref, *refs):
    rows_refs = refs[:4]
    gain_ref, cos_ref, sin_ref = refs[4:7]
    own_refs, other_refs = refs[7:19], refs[19:31]
    query_ref, key_ref, value_ref = refs[31:34]
    own_rows, other_rows, result, weights, sems = refs[34:39]
    wide = weights.shape[4]
    copies = fetch(own_refs, other_refs, 0, weights, sems)
    x, z, y, core, way = place_of(place_ref)
    squares = jnp.zeros((rows_refs[0].shape[0], 1), F32)
    for r in range(RING):
        block = wrap(y - r * way)
        s = wrap((x - block) * way)
        for m in range(RING):
            part = wrap(z - m * way)
            piece = rows_refs[r][:, lane_block(part, PIECE)].astype(F32)
            squares = squares + jnp.sum(piece * piece, axis=-1, keepdims=True)
            gain = gain_ref[:, lane_block(block * RING + part, PIECE)]
            own_rows[:, lane_block(s * RING + m, PIECE)] = (piece * gain).astype(BF)
    for s in range(RING):
        for m in range(RING):
            at = (s * RING + m) * PIECE
            back = ((RING - s) % RING * RING + (RING - m) % RING) * PIECE
            other_rows[:, at : at + PIECE] = own_rows[:, back : back + PIECE]
    for side, (rows, at) in enumerate(((own_rows, core), (other_rows, 1 - core))):
        total = None
        for s in range(RING):
            for copy in copies[side][s]:
                copy.wait()
            term = jnp.dot(
                rows[:, s * LANES : (s + 1) * LANES],
                weights[side, s].reshape(LANES, wide),
                preferred_element_type=F32,
            )
            total = term if total is None else total + term
        result[:, pl.ds(pl.multiple_of(at * wide, HEAD), wide)] = total
    scale = lax.rsqrt(squares * (1.0 / (TENSOR * LANES)) + epsilon)
    cosine, sine = cos_ref[...], sin_ref[...]
    heads = query_ref.shape[1] // HEAD
    for h in range(heads + 1):
        values = result[:, h * HEAD : (h + 1) * HEAD] * scale
        turned = (values * cosine + pltpu.roll(values, HEAD // 2, 1) * sine).astype(BF)
        if h < heads:
            query_ref[:, h * HEAD : (h + 1) * HEAD] = turned
        else:
            key_ref[...] = turned
    value_ref[...] = (result[:, (heads + 1) * HEAD :] * scale).astype(BF)


def project(place, rows, gain, cosine, sine, own, other):
    count = rows[0].shape[0]
    width = rows[0].shape[1]
    return pl.pallas_call(
        project_kernel,
        out_shape=(
            jax.ShapeDtypeStruct((count, width), BF),
            jax.ShapeDtypeStruct((count, HEAD), BF),
            jax.ShapeDtypeStruct((count, HEAD), BF),
        ),
        in_specs=[in_smem()] + [in_vmem()] * 7 + [anywhere()] * 24,
        out_specs=(in_vmem(),) * 3,
        scratch_shapes=[
            pltpu.VMEM((count, TENSOR * width), BF),
            pltpu.VMEM((count, TENSOR * width), BF),
            pltpu.VMEM((count, width + 2 * HEAD), F32),
        ]
        + weight_space((width + 2 * HEAD) // 2),
        compiler_params=params(),
        name="project",
    )(place, *rows, gain, cosine, sine, *own, *other)


def attend_kernel(first_pair, pairs, place_ref, lens_ref, q_ref, k_ref, v_ref, *refs):
    own_refs, other_refs = refs[:12], refs[12:24]
    out_refs = refs[24:28]
    mixed, terms, weights, sems = refs[28:32]
    copies = fetch(own_refs, other_refs, (q_ref.shape[1] + 2 * HEAD) // 2, weights, sems)
    x, z, y, core, way = place_of(place_ref)
    slots = 2 * SAMPLE
    heads = q_ref.shape[1] // HEAD
    step_t = lax.broadcasted_iota(jnp.int32, (slots, slots), 0)
    step_u = lax.broadcasted_iota(jnp.int32, (slots, slots), 1)
    for p in range(pairs):
        at = slice(p * slots, (p + 1) * slots)
        stacked = jnp.concatenate(
            [q_ref[at, h * HEAD : (h + 1) * HEAD] for h in range(heads)], axis=0
        )
        scores = lax.dot_general(
            stacked, k_ref[at, :], (((1,), (1,)), ((), ())), preferred_element_type=F32
        ) * (HEAD**-0.5)
        len_a = lens_ref[2 * (first_pair + p)]
        len_b = lens_ref[2 * (first_pair + p) + 1]
        limit = jnp.where(step_u < SAMPLE, len_a, len_b + SAMPLE)
        limit = jnp.minimum(limit, step_t + 1)
        closed = jnp.where(step_u < limit, 0.0, -1e30).astype(F32)
        scores = scores.reshape(heads, slots, slots) + closed[None]
        peak = jnp.max(scores, axis=-1, keepdims=True)
        raised = jnp.exp(scores - peak)
        probs = raised / jnp.sum(raised, axis=-1, keepdims=True)
        out = jnp.dot(
            probs.astype(BF).reshape(heads * slots, slots),
            v_ref[at, :],
            preferred_element_type=F32,
        ).astype(BF)
        for h in range(heads):
            mixed[at, h * HEAD : (h + 1) * HEAD] = out[h * slots : (h + 1) * slots]
    depth = 2 * PIECE
    mine = mixed[:, lane_block(core, depth)]
    theirs = mixed[:, lane_block(1 - core, depth)]
    for side in copies:
        for step in side:
            for copy in step:
                copy.wait()

    def product(values, side, s, m):
        block = weights[side, s, 2 * m : 2 * m + 2].reshape(PIECE, depth)
        return jnp.dot(values[:, :PIECE], block[:, :PIECE], preferred_element_type=F32) + jnp.dot(
            values[:, PIECE:], block[:, PIECE:], preferred_element_type=F32
        )

    for s in range(RING):
        r = wrap((y - wrap(x - s * way)) * way)
        for m in range(RING):
            part = wrap(z - m * way)
            term = product(mine, 0, s, m) + product(
                theirs, 1, (RING - s) % RING, (RING - m) % RING
            )
            terms[r, :, lane_block(part, PIECE)] = term.astype(BF)
    for r in range(RING):
        out_refs[r][...] = terms[r]


def attend(first_pair, pairs, place, lens, qkv, own, other, earlier):
    count = pairs * 2 * SAMPLE
    width = qkv[0].shape[1]

    inputs = 5 + 24

    def kernel(*refs):
        attend_kernel(first_pair, pairs, *refs[:inputs], *refs[inputs + len(earlier) :])

    return pl.pallas_call(
        kernel,
        out_shape=(jax.ShapeDtypeStruct((count, width), BF),) * RING,
        in_specs=[in_smem(), in_smem()]
        + [in_vmem()] * 3
        + [anywhere()] * (24 + len(earlier)),
        out_specs=(in_vmem(),) * RING,
        scratch_shapes=[
            pltpu.VMEM((count, width), BF),
            pltpu.VMEM((RING, count, width), BF),
        ]
        + weight_space(2 * PIECE),
        compiler_params=params(),
        name="attend",
    )(place, lens, *qkv, *own, *other, *earlier)


def finish_kernel(place_ref, gain_ref, b0, b1, b2, b3, *rest):
    out_ref = rest[-1]
    _, _, y, _, way = place_of(place_ref)
    values = [b[...].astype(F32) for b in (b0, b1, b2, b3)]
    squares = sum(jnp.sum(v * v, axis=-1, keepdims=True) for v in values)
    scale = lax.rsqrt(squares * (1.0 / (TENSOR * LANES)) + epsilon)
    for r in range(RING):
        lanes = lane_block(wrap(y - r * way), LANES)
        out_ref[:, lanes] = (values[r] * scale * gain_ref[:, lanes]).astype(BF)


def finish(place, gain, blocks, before, chunk, total):
    count, width = blocks[0].shape
    tile = 2 * SAMPLE
    steps = count // tile
    specs = [
        in_smem(),
        pl.BlockSpec((1, TENSOR * width), lambda i: (0, 0)),
    ] + [pl.BlockSpec((tile, width), lambda i: (i, 0))] * RING
    args = [place, gain, *blocks]
    aliases = {}
    if before is not None:
        specs.append(pl.BlockSpec(memory_space=pl.ANY))
        aliases = {len(args): 0}
        args.append(before)
    return pl.pallas_call(
        finish_kernel,
        grid=(steps,),
        out_shape=jax.ShapeDtypeStruct((total, TENSOR * width), BF),
        in_specs=specs,
        out_specs=pl.BlockSpec((tile, TENSOR * width), lambda i: (i + chunk * steps, 0)),
        input_output_aliases=aliases,
        compiler_params=params(),
        name="finish",
    )(*args)


def after(value, *others):
    return pl.pallas_call(
        lambda *refs: None,
        out_shape=jax.ShapeDtypeStruct(value.shape, value.dtype),
        in_specs=[anywhere()] * (1 + len(others)),
        out_specs=anywhere(),
        input_output_aliases={0: 0},
        name="after",
    )(value, *others)


def way_of(dp):
    return 1 - 2 * (dp % 2)


def along_y(values):
    pairs = [
        (dp * TENSOR + y, dp * TENSOR + (y + way_of(dp)) % TENSOR)
        for dp in range(4)
        for y in range(TENSOR)
    ]
    return lax.ppermute(values, ("dp", "tensor"), pairs)


def along_x(values):
    pairs = [
        (dp * 16 + x * 4 + z, dp * 16 + (x + way_of(dp)) % 4 * 4 + z)
        for dp in range(4)
        for x in range(4)
        for z in range(4)
    ]
    return lax.ppermute(values, ("dp", "fsdp"), pairs)


def along_z(values):
    pairs = [
        (dp * 16 + x * 4 + z, dp * 16 + x * 4 + (z + way_of(dp)) % 4)
        for dp in range(4)
        for x in range(4)
        for z in range(4)
    ]
    return lax.ppermute(values, ("dp", "fsdp"), pairs)


def other_core(values):
    return lax.ppermute(values, "dp", [(dp, dp ^ 1) for dp in range(4)])


def spread_x(rounds):
    own = [None] * 12
    for g, (start, stop) in enumerate(GROUPS):
        block = jnp.stack([half for step in rounds[start:stop] for half in step])
        for s in range(4):
            own[3 * s + g] = block
            if s < 3 and (s < 2 or g < 2):
                block = along_x(block)
    return own


def on_device(
    candidates, cand_lengths, pairing, attn_gain, w_query, w_key, w_value, w_out, ffn_gain
):
    me = lax.axis_index("fsdp")
    y = lax.axis_index("tensor")
    core = lax.rem(lax.axis_index("dp"), 2)
    place = jnp.stack([me // 4, lax.rem(me, 4), y, core]).astype(jnp.int32)
    cand_dev = candidates.shape[1]
    devices = lax.axis_size("fsdp")
    flat = pairing[0].reshape(devices, cand_dev)
    pick = jnp.sum(jnp.where(flat // cand_dev == me, lax.rem(flat, cand_dev), 0), axis=1)
    wanted = lax.dynamic_index_in_dim(flat, me, 0, keepdims=False)
    source = wanted // cand_dev

    half_cols = (w_query.shape[1] + w_key.shape[1] + w_value.shape[1]) // 2
    first = w_query[:, :half_cols]
    second = jnp.concatenate([w_query[:, half_cols:], w_key, w_value], axis=1)
    depth = w_out.shape[0] // 2
    third = jnp.where(core == 0, w_out[:depth], w_out[depth:])
    piece = jnp.concatenate(
        [jnp.where(core == 0, first, second), third[: depth // 2], third[depth // 2 :]], axis=1
    )
    rounds = [[piece[: PIECE // 2], piece[PIECE // 2 :]]]
    for _ in range(3):
        rounds.append([along_z(half) for half in rounds[-1]])
    own = spread_x(rounds)
    early = {i: other_core(own[i]) for i in (0, 1, 3, 4, 6, 7, 9)}

    packed = pack(pick, cand_lengths[0], candidates[0], (*rounds[3], own[7], own[9]), devices)
    incoming = lax.all_to_all(packed, "fsdp", split_axis=0, concat_axis=0, tiled=True)
    parts = 2
    pairs = cand_dev // 2 // parts
    local = unpack(source, incoming, (own[10], *early.values()), parts)
    rings = [[rows] for rows in local]
    for step in range(3):
        for ring in rings:
            ring.append(along_y(ring[-1]))
        if step == 1:
            own[8] = after(own[8], rings[0][2], rings[1][2])
            own[11] = along_x(own[8])
    other = [early[i] if i in early else other_core(own[i]) for i in range(12)]
    sent = incoming[:, -1, 0].astype(F32)
    slots = jnp.arange(devices, dtype=jnp.int32)
    lens = jnp.sum(
        jnp.where(source[:, None] == slots[None, :], sent[None, :], 0.0), axis=1
    ).astype(jnp.int32)


    gain_in = attn_gain.reshape(1, -1)
    gain_out = ffn_gain.reshape(1, -1)
    freq = rope_base ** (-jnp.arange(HEAD // 2, dtype=F32) * 2.0 / HEAD)
    starts = jnp.where(jnp.arange(cand_dev) % 2 == 0, 0, jnp.roll(lens, 1))
    positions = starts[:, None] + jnp.arange(SAMPLE, dtype=jnp.int32)[None, :]
    angles = positions.reshape(parts, -1, 1).astype(F32) * freq
    cosine, sine = jnp.cos(angles), jnp.sin(angles)
    cosine = jnp.concatenate([cosine, cosine], axis=2)
    sine = jnp.concatenate([-sine, sine], axis=2)

    width = candidates.shape[3]
    total = cand_dev * SAMPLE
    normed = None
    resids = []
    terms, moved = [], []
    for c in range(parts):
        qkv = project(place, rings[c], gain_in, cosine[c], sine[c], own, other)
        terms.append(attend(c * pairs, pairs, place, lens, qkv, own, other, moved))
        moving = along_y(terms[c][1])
        moved.append((moving.astype(F32) + terms[c][2].astype(F32)).astype(BF))
    for c in range(parts):
        moving = along_y(moved[c])
        moving = along_y((moving.astype(F32) + terms[c][3].astype(F32)).astype(BF))
        stream = local[c].astype(F32) + terms[c][0].astype(F32) + moving.astype(F32)
        blocks = [stream.astype(BF)]
        for _ in range(3):
            blocks.append(along_y(blocks[-1]))
        resids.append(blocks[0])
        normed = finish(place, gain_out, blocks, normed, c, total)
    resid = jnp.concatenate(resids, axis=0)
    pair_dev = cand_dev // 2
    return (
        resid.reshape(1, pair_dev, 2 * SAMPLE, width),
        normed.reshape(1, pair_dev, 2 * SAMPLE, TENSOR * width),
    )


def solution(mesh):
    return jax.shard_map(
        on_device,
        mesh=mesh,
        in_specs=(
            P("dp", "fsdp", None, "tensor"),
            P("dp", "fsdp"),
            P("dp", None, None),
            P(),
            P("fsdp", "tensor"),
            P("fsdp", "tensor"),
            P("fsdp", "tensor"),
            P("tensor", "fsdp"),
            P(),
        ),
        out_specs=(P("dp", "fsdp", None, "tensor"), P("dp", "fsdp", None, None)),
        check_vma=False,
    )
```

```python
import jax
import jax.numpy as jnp
from jax import lax
from jax.experimental import pallas as pl
from jax.experimental.pallas import tpu as pltpu
from jax.sharding import PartitionSpec as P

HEAD = 128
SAMPLE = 64
TENSOR = 4
RING = 4
LANES = 1024
PIECE = 256
EXTRA = 16
GROUPS = ((0, 1), (1, 2), (2, 4))
epsilon = 1e-05
rope_base = 500000.0
BF = jnp.bfloat16
F32 = jnp.float32
VMEM_LIMIT = 40 * 1024 * 1024


def wrap(value):
    return lax.rem(value + 2 * RING, RING)


def in_vmem():
    return pl.BlockSpec(memory_space=pltpu.VMEM)


def in_smem():
    return pl.BlockSpec(memory_space=pltpu.SMEM)


def params(**kw):
    return pltpu.CompilerParams(vmem_limit_bytes=VMEM_LIMIT, **kw)


def pack_kernel(pick_ref, lens_ref, cand_ref, *refs):
    slots_ref = refs[-1]
    blocks = cand_ref.shape[2] // HEAD
    for slot in range(slots_ref.shape[0]):
        own = pick_ref[slot]
        for b in range(blocks):
            slots_ref[slot, b * SAMPLE : (b + 1) * SAMPLE, :] = cand_ref[
                own, :, b * HEAD : (b + 1) * HEAD
            ]
        length = jnp.full((EXTRA, HEAD), lens_ref[own], jnp.int32).astype(F32)
        slots_ref[slot, blocks * SAMPLE :, :] = length.astype(BF)


def pack(pick, lens, cands, earlier, slots):
    rows = cands.shape[2] // HEAD * SAMPLE + EXTRA
    return pl.pallas_call(
        pack_kernel,
        out_shape=jax.ShapeDtypeStruct((slots, rows, HEAD), BF),
        in_specs=[in_smem(), in_smem(), in_vmem()]
        + [pl.BlockSpec(memory_space=pl.ANY)] * len(earlier),
        out_specs=in_vmem(),
        compiler_params=params(),
        name="pack",
    )(pick, lens, cands, *earlier)


def unpack_kernel(earlier, source_ref, slots_ref, *refs):
    rows_refs = refs[earlier:]
    blocks = rows_refs[0].shape[1] // HEAD
    per = source_ref.shape[0] // len(rows_refs)
    for cand in range(source_ref.shape[0]):
        at = cand % per * SAMPLE
        for b in range(blocks):
            rows_refs[cand // per][at : at + SAMPLE, b * HEAD : (b + 1) * HEAD] = slots_ref[
                source_ref[cand], b * SAMPLE : (b + 1) * SAMPLE, :
            ]


def unpack(source, slots, earlier, parts):
    width = (slots.shape[1] - EXTRA) // SAMPLE * HEAD
    rows = source.shape[0] * SAMPLE // parts

    def kernel(*refs):
        unpack_kernel(len(earlier), *refs)

    return pl.pallas_call(
        kernel,
        out_shape=(jax.ShapeDtypeStruct((rows, width), BF),) * parts,
        in_specs=[in_smem(), in_vmem()] + [anywhere()] * len(earlier),
        out_specs=(in_vmem(),) * parts,
        compiler_params=params(),
        name="unpack",
    )(source, slots, *earlier)


def place_of(place_ref):
    x, z, y, core = place_ref[0], place_ref[1], place_ref[2], place_ref[3]
    return x, z, y, core, 1 - 2 * core


def lane_block(index, width):
    return pl.ds(pl.multiple_of(index * width, width), width)


def fetch(own_refs, other_refs, start, weights, sems):
    width = weights.shape[4]
    copies = []
    for side, blocks in enumerate((own_refs, other_refs)):
        copies.append([])
        for s in range(RING):
            copies[side].append([])
            for g, (lo, hi) in enumerate(GROUPS):
                copy = pltpu.make_async_copy(
                    blocks[3 * s + g].at[:, :, start : start + width],
                    weights.at[side, s, 2 * lo : 2 * hi],
                    sems.at[side, s, g],
                )
                copy.start()
                copies[side][s].append(copy)
    return copies


def weight_space(width):
    return [
        pltpu.VMEM((2, RING, 2 * RING, PIECE // 2, width), BF),
        pltpu.SemaphoreType.DMA((2, RING, len(GROUPS))),
    ]


def anywhere():
    return pl.BlockSpec(memory_space=pl.ANY)


def project_kernel(place_ref, *refs):
    rows_refs = refs[:4]
    gain_ref, cos_ref, sin_ref = refs[4:7]
    own_refs, other_refs = refs[7:19], refs[19:31]
    query_ref, key_ref, value_ref = refs[31:34]
    own_rows, other_rows, result, weights, sems = refs[34:39]
    wide = weights.shape[4]
    copies = fetch(own_refs, other_refs, 0, weights, sems)
    x, z, y, core, way = place_of(place_ref)
    squares = jnp.zeros((rows_refs[0].shape[0], 1), F32)
    for r in range(RING):
        block = wrap(y - r * way)
        s = wrap((x - block) * way)
        for m in range(RING):
            part = wrap(z - m * way)
            piece = rows_refs[r][:, lane_block(part, PIECE)].astype(F32)
            squares = squares + jnp.sum(piece * piece, axis=-1, keepdims=True)
            gain = gain_ref[:, lane_block(block * RING + part, PIECE)]
            own_rows[:, lane_block(s * RING + m, PIECE)] = (piece * gain).astype(BF)
    for s in range(RING):
        for m in range(RING):
            at = (s * RING + m) * PIECE
            back = ((RING - s) % RING * RING + (RING - m) % RING) * PIECE
            other_rows[:, at : at + PIECE] = own_rows[:, back : back + PIECE]
    for side, (rows, at) in enumerate(((own_rows, core), (other_rows, 1 - core))):
        total = None
        for s in range(RING):
            for copy in copies[side][s]:
                copy.wait()
            term = jnp.dot(
                rows[:, s * LANES : (s + 1) * LANES],
                weights[side, s].reshape(LANES, wide),
                preferred_element_type=F32,
            )
            total = term if total is None else total + term
        result[:, pl.ds(pl.multiple_of(at * wide, HEAD), wide)] = total
    scale = lax.rsqrt(squares * (1.0 / (TENSOR * LANES)) + epsilon)
    cosine, sine = cos_ref[...], sin_ref[...]
    heads = query_ref.shape[1] // HEAD
    for h in range(heads + 1):
        values = result[:, h * HEAD : (h + 1) * HEAD] * scale
        turned = (values * cosine + pltpu.roll(values, HEAD // 2, 1) * sine).astype(BF)
        if h < heads:
            query_ref[:, h * HEAD : (h + 1) * HEAD] = turned
        else:
            key_ref[...] = turned
    value_ref[...] = (result[:, (heads + 1) * HEAD :] * scale).astype(BF)


def project(place, rows, gain, cosine, sine, own, other):
    count = rows[0].shape[0]
    width = rows[0].shape[1]
    return pl.pallas_call(
        project_kernel,
        out_shape=(
            jax.ShapeDtypeStruct((count, width), BF),
            jax.ShapeDtypeStruct((count, HEAD), BF),
            jax.ShapeDtypeStruct((count, HEAD), BF),
        ),
        in_specs=[in_smem()] + [in_vmem()] * 7 + [anywhere()] * 24,
        out_specs=(in_vmem(),) * 3,
        scratch_shapes=[
            pltpu.VMEM((count, TENSOR * width), BF),
            pltpu.VMEM((count, TENSOR * width), BF),
            pltpu.VMEM((count, width + 2 * HEAD), F32),
        ]
        + weight_space((width + 2 * HEAD) // 2),
        compiler_params=params(),
        name="project",
    )(place, *rows, gain, cosine, sine, *own, *other)


def attend_kernel(first_pair, pairs, place_ref, lens_ref, q_ref, k_ref, v_ref, *refs):
    own_refs, other_refs = refs[:12], refs[12:24]
    out_refs = refs[24:28]
    mixed, terms, weights, sems = refs[28:32]
    copies = fetch(own_refs, other_refs, (q_ref.shape[1] + 2 * HEAD) // 2, weights, sems)
    x, z, y, core, way = place_of(place_ref)
    slots = 2 * SAMPLE
    heads = q_ref.shape[1] // HEAD
    step_t = lax.broadcasted_iota(jnp.int32, (slots, slots), 0)
    step_u = lax.broadcasted_iota(jnp.int32, (slots, slots), 1)
    for p in range(pairs):
        at = slice(p * slots, (p + 1) * slots)
        stacked = jnp.concatenate(
            [q_ref[at, h * HEAD : (h + 1) * HEAD] for h in range(heads)], axis=0
        )
        scores = lax.dot_general(
            stacked, k_ref[at, :], (((1,), (1,)), ((), ())), preferred_element_type=F32
        ) * (HEAD**-0.5)
        len_a = lens_ref[2 * (first_pair + p)]
        len_b = lens_ref[2 * (first_pair + p) + 1]
        limit = jnp.where(step_u < SAMPLE, len_a, len_b + SAMPLE)
        limit = jnp.minimum(limit, step_t + 1)
        closed = jnp.where(step_u < limit, 0.0, -1e30).astype(F32)
        scores = scores.reshape(heads, slots, slots) + closed[None]
        peak = jnp.max(scores, axis=-1, keepdims=True)
        raised = jnp.exp(scores - peak)
        probs = raised / jnp.sum(raised, axis=-1, keepdims=True)
        out = jnp.dot(
            probs.astype(BF).reshape(heads * slots, slots),
            v_ref[at, :],
            preferred_element_type=F32,
        ).astype(BF)
        for h in range(heads):
            mixed[at, h * HEAD : (h + 1) * HEAD] = out[h * slots : (h + 1) * slots]
    depth = 2 * PIECE
    mine = mixed[:, lane_block(core, depth)]
    theirs = mixed[:, lane_block(1 - core, depth)]
    for side in copies:
        for step in side:
            for copy in step:
                copy.wait()

    def product(values, side, s, m):
        block = weights[side, s, 2 * m : 2 * m + 2].reshape(PIECE, depth)
        return jnp.dot(values[:, :PIECE], block[:, :PIECE], preferred_element_type=F32) + jnp.dot(
            values[:, PIECE:], block[:, PIECE:], preferred_element_type=F32
        )

    for s in range(RING):
        r = wrap((y - wrap(x - s * way)) * way)
        for m in range(RING):
            part = wrap(z - m * way)
            term = product(mine, 0, s, m) + product(
                theirs, 1, (RING - s) % RING, (RING - m) % RING
            )
            terms[r, :, lane_block(part, PIECE)] = term.astype(BF)
    for r in range(RING):
        out_refs[r][...] = terms[r]


def attend(first_pair, pairs, place, lens, qkv, own, other):
    count = pairs * 2 * SAMPLE
    width = qkv[0].shape[1]

    def kernel(*refs):
        attend_kernel(first_pair, pairs, *refs)

    return pl.pallas_call(
        kernel,
        out_shape=(jax.ShapeDtypeStruct((count, width), BF),) * RING,
        in_specs=[in_smem(), in_smem()] + [in_vmem()] * 3 + [anywhere()] * 24,
        out_specs=(in_vmem(),) * RING,
        scratch_shapes=[
            pltpu.VMEM((count, width), BF),
            pltpu.VMEM((RING, count, width), BF),
        ]
        + weight_space(2 * PIECE),
        compiler_params=params(),
        name="attend",
    )(place, lens, *qkv, *own, *other)


def finish_kernel(place_ref, gain_ref, b0, b1, b2, b3, *rest):
    out_ref = rest[-1]
    _, _, y, _, way = place_of(place_ref)
    values = [b[...].astype(F32) for b in (b0, b1, b2, b3)]
    squares = sum(jnp.sum(v * v, axis=-1, keepdims=True) for v in values)
    scale = lax.rsqrt(squares * (1.0 / (TENSOR * LANES)) + epsilon)
    for r in range(RING):
        lanes = lane_block(wrap(y - r * way), LANES)
        out_ref[:, lanes] = (values[r] * scale * gain_ref[:, lanes]).astype(BF)


def finish(place, gain, blocks, before, chunk, total):
    count, width = blocks[0].shape
    tile = 2 * SAMPLE
    steps = count // tile
    specs = [
        in_smem(),
        pl.BlockSpec((1, TENSOR * width), lambda i: (0, 0)),
    ] + [pl.BlockSpec((tile, width), lambda i: (i, 0))] * RING
    args = [place, gain, *blocks]
    aliases = {}
    if before is not None:
        specs.append(pl.BlockSpec(memory_space=pl.ANY))
        aliases = {len(args): 0}
        args.append(before)
    return pl.pallas_call(
        finish_kernel,
        grid=(steps,),
        out_shape=jax.ShapeDtypeStruct((total, TENSOR * width), BF),
        in_specs=specs,
        out_specs=pl.BlockSpec((tile, TENSOR * width), lambda i: (i + chunk * steps, 0)),
        input_output_aliases=aliases,
        compiler_params=params(),
        name="finish",
    )(*args)


def after(value, *others):
    return pl.pallas_call(
        lambda *refs: None,
        out_shape=jax.ShapeDtypeStruct(value.shape, value.dtype),
        in_specs=[anywhere()] * (1 + len(others)),
        out_specs=anywhere(),
        input_output_aliases={0: 0},
        name="after",
    )(value, *others)


def way_of(dp):
    return 1 - 2 * (dp % 2)


def along_y(values):
    pairs = [
        (dp * TENSOR + y, dp * TENSOR + (y + way_of(dp)) % TENSOR)
        for dp in range(4)
        for y in range(TENSOR)
    ]
    return lax.ppermute(values, ("dp", "tensor"), pairs)


def along_x(values):
    pairs = [
        (dp * 16 + x * 4 + z, dp * 16 + (x + way_of(dp)) % 4 * 4 + z)
        for dp in range(4)
        for x in range(4)
        for z in range(4)
    ]
    return lax.ppermute(values, ("dp", "fsdp"), pairs)


def along_z(values):
    pairs = [
        (dp * 16 + x * 4 + z, dp * 16 + x * 4 + (z + way_of(dp)) % 4)
        for dp in range(4)
        for x in range(4)
        for z in range(4)
    ]
    return lax.ppermute(values, ("dp", "fsdp"), pairs)


def other_core(values):
    return lax.ppermute(values, "dp", [(dp, dp ^ 1) for dp in range(4)])


def spread_x(rounds):
    own = [None] * 12
    for g, (start, stop) in enumerate(GROUPS):
        block = jnp.stack([half for step in rounds[start:stop] for half in step])
        for s in range(4):
            own[3 * s + g] = block
            if s < 3:
                block = along_x(block)
    return own


def on_device(
    candidates, cand_lengths, pairing, attn_gain, w_query, w_key, w_value, w_out, ffn_gain
):
    me = lax.axis_index("fsdp")
    y = lax.axis_index("tensor")
    core = lax.rem(lax.axis_index("dp"), 2)
    place = jnp.stack([me // 4, lax.rem(me, 4), y, core]).astype(jnp.int32)
    cand_dev = candidates.shape[1]
    devices = lax.axis_size("fsdp")
    flat = pairing[0].reshape(devices, cand_dev)
    pick = jnp.sum(jnp.where(flat // cand_dev == me, lax.rem(flat, cand_dev), 0), axis=1)
    wanted = lax.dynamic_index_in_dim(flat, me, 0, keepdims=False)
    source = wanted // cand_dev

    half_cols = (w_query.shape[1] + w_key.shape[1] + w_value.shape[1]) // 2
    first = w_query[:, :half_cols]
    second = jnp.concatenate([w_query[:, half_cols:], w_key, w_value], axis=1)
    depth = w_out.shape[0] // 2
    third = jnp.where(core == 0, w_out[:depth], w_out[depth:])
    piece = jnp.concatenate(
        [jnp.where(core == 0, first, second), third[: depth // 2], third[depth // 2 :]], axis=1
    )
    rounds = [[piece[: PIECE // 2], piece[PIECE // 2 :]]]
    for _ in range(3):
        rounds.append([along_z(half) for half in rounds[-1]])
    own = spread_x(rounds)

    packed = pack(pick, cand_lengths[0], candidates[0], (*rounds[3], own[7], own[9]), devices)
    incoming = lax.all_to_all(packed, "fsdp", split_axis=0, concat_axis=0, tiled=True)
    parts = 2
    pairs = cand_dev // 2 // parts
    local = unpack(source, incoming, (), parts)
    other = [other_core(block) for block in own]
    sent = incoming[:, -1, 0].astype(F32)
    slots = jnp.arange(devices, dtype=jnp.int32)
    lens = jnp.sum(
        jnp.where(source[:, None] == slots[None, :], sent[None, :], 0.0), axis=1
    ).astype(jnp.int32)


    gain_in = attn_gain.reshape(1, -1)
    gain_out = ffn_gain.reshape(1, -1)
    freq = rope_base ** (-jnp.arange(HEAD // 2, dtype=F32) * 2.0 / HEAD)
    starts = jnp.where(jnp.arange(cand_dev) % 2 == 0, 0, jnp.roll(lens, 1))
    positions = starts[:, None] + jnp.arange(SAMPLE, dtype=jnp.int32)[None, :]
    angles = positions.reshape(parts, -1, 1).astype(F32) * freq
    cosine, sine = jnp.cos(angles), jnp.sin(angles)
    cosine = jnp.concatenate([cosine, cosine], axis=2)
    sine = jnp.concatenate([-sine, sine], axis=2)

    width = candidates.shape[3]
    total = cand_dev * SAMPLE
    normed = None
    resids = []
    rings = [[rows] for rows in local]
    for _ in range(3):
        for ring in rings:
            ring.append(along_y(ring[-1]))
    for c in range(parts):
        ring = rings[c]
        qkv = project(place, ring, gain_in, cosine[c], sine[c], own, other)
        terms = attend(c * pairs, pairs, place, lens, qkv, own, other)
        moving = along_y(terms[1])
        for r in (2, 3):
            moving = along_y((moving.astype(F32) + terms[r].astype(F32)).astype(BF))
        stream = local[c].astype(F32) + terms[0].astype(F32) + moving.astype(F32)
        blocks = [stream.astype(BF)]
        for _ in range(3):
            blocks.append(along_y(blocks[-1]))
        resids.append(blocks[0])
        normed = finish(place, gain_out, blocks, normed, c, total)
    resid = jnp.concatenate(resids, axis=0)
    pair_dev = cand_dev // 2
    return (
        resid.reshape(1, pair_dev, 2 * SAMPLE, width),
        normed.reshape(1, pair_dev, 2 * SAMPLE, TENSOR * width),
    )


def solution(mesh):
    return jax.shard_map(
        on_device,
        mesh=mesh,
        in_specs=(
            P("dp", "fsdp", None, "tensor"),
            P("dp", "fsdp"),
            P("dp", None, None),
            P(),
            P("fsdp", "tensor"),
            P("fsdp", "tensor"),
            P("fsdp", "tensor"),
            P("tensor", "fsdp"),
            P(),
        ),
        out_specs=(P("dp", "fsdp", None, "tensor"), P("dp", "fsdp", None, None)),
        check_vma=False,
    )
```

```python
import jax
import jax.numpy as jnp
from jax import lax
from jax.experimental import pallas as pl
from jax.experimental.pallas import tpu as pltpu
from jax.sharding import PartitionSpec as P

HEAD = 128
SAMPLE = 64
TENSOR = 4
RING = 4
LANES = 1024
PIECE = 256
EXTRA = 16
GROUPS = ((0, 1), (1, 2), (2, 4))
epsilon = 1e-05
rope_base = 500000.0
BF = jnp.bfloat16
F32 = jnp.float32
VMEM_LIMIT = 58 * 1024 * 1024


def wrap(value):
    return lax.rem(value + 2 * RING, RING)


def in_vmem():
    return pl.BlockSpec(memory_space=pltpu.VMEM)


def in_smem():
    return pl.BlockSpec(memory_space=pltpu.SMEM)


def params(**kw):
    return pltpu.CompilerParams(vmem_limit_bytes=VMEM_LIMIT, **kw)


def pack_kernel(pick_ref, lens_ref, cand_ref, *refs):
    slots_ref = refs[-1]
    blocks = cand_ref.shape[2] // HEAD
    for slot in range(slots_ref.shape[0]):
        own = pick_ref[slot]
        for b in range(blocks):
            slots_ref[slot, b * SAMPLE : (b + 1) * SAMPLE, :] = cand_ref[
                own, :, b * HEAD : (b + 1) * HEAD
            ]
        length = jnp.full((EXTRA, HEAD), lens_ref[own], jnp.int32).astype(F32)
        slots_ref[slot, blocks * SAMPLE :, :] = length.astype(BF)


def pack(pick, lens, cands, earlier, slots):
    rows = cands.shape[2] // HEAD * SAMPLE + EXTRA
    return pl.pallas_call(
        pack_kernel,
        out_shape=jax.ShapeDtypeStruct((slots, rows, HEAD), BF),
        in_specs=[in_smem(), in_smem(), in_vmem()]
        + [pl.BlockSpec(memory_space=pl.ANY)] * len(earlier),
        out_specs=in_vmem(),
        compiler_params=params(),
        name="pack",
    )(pick, lens, cands, *earlier)


def unpack_kernel(earlier, source_ref, slots_ref, *refs):
    rows_refs = refs[earlier:]
    blocks = rows_refs[0].shape[1] // HEAD
    per = source_ref.shape[0] // len(rows_refs)
    for cand in range(source_ref.shape[0]):
        at = cand % per * SAMPLE
        for b in range(blocks):
            rows_refs[cand // per][at : at + SAMPLE, b * HEAD : (b + 1) * HEAD] = slots_ref[
                source_ref[cand], b * SAMPLE : (b + 1) * SAMPLE, :
            ]


def unpack(source, slots, earlier, parts):
    width = (slots.shape[1] - EXTRA) // SAMPLE * HEAD
    rows = source.shape[0] * SAMPLE // parts

    def kernel(*refs):
        unpack_kernel(len(earlier), *refs)

    return pl.pallas_call(
        kernel,
        out_shape=(jax.ShapeDtypeStruct((rows, width), BF),) * parts,
        in_specs=[in_smem(), in_vmem()] + [anywhere()] * len(earlier),
        out_specs=(in_vmem(),) * parts,
        compiler_params=params(),
        name="unpack",
    )(source, slots, *earlier)


def place_of(place_ref):
    x, z, y, core = place_ref[0], place_ref[1], place_ref[2], place_ref[3]
    return x, z, y, core, 1 - 2 * core


def lane_block(index, width):
    return pl.ds(pl.multiple_of(index * width, width), width)


def fetch(own_refs, other_refs, start, weights, sems):
    width = weights.shape[4]
    copies = []
    for side, blocks in enumerate((own_refs, other_refs)):
        copies.append([])
        for s in range(RING):
            copies[side].append([])
            for g, (lo, hi) in enumerate(GROUPS):
                copy = pltpu.make_async_copy(
                    blocks[3 * s + g].at[:, :, start : start + width],
                    weights.at[side, s, 2 * lo : 2 * hi],
                    sems.at[side, s, g],
                )
                copy.start()
                copies[side][s].append(copy)
    return copies


def weight_space(width):
    return [
        pltpu.VMEM((2, RING, 2 * RING, PIECE // 2, width), BF),
        pltpu.SemaphoreType.DMA((2, RING, len(GROUPS))),
    ]


def anywhere():
    return pl.BlockSpec(memory_space=pl.ANY)


def project_kernel(place_ref, *refs):
    rows_refs = refs[:4]
    gain_ref, cos_ref, sin_ref = refs[4:7]
    own_refs, other_refs = refs[7:19], refs[19:31]
    query_ref, key_ref, value_ref = refs[31:34]
    own_rows, other_rows, result, weights, sems = refs[34:39]
    wide = weights.shape[4]
    copies = fetch(own_refs, other_refs, 0, weights, sems)
    x, z, y, core, way = place_of(place_ref)
    squares = jnp.zeros((rows_refs[0].shape[0], 1), F32)
    for r in range(RING):
        block = wrap(y - r * way)
        s = wrap((x - block) * way)
        for m in range(RING):
            part = wrap(z - m * way)
            piece = rows_refs[r][:, lane_block(part, PIECE)].astype(F32)
            squares = squares + jnp.sum(piece * piece, axis=-1, keepdims=True)
            gain = gain_ref[:, lane_block(block * RING + part, PIECE)]
            own_rows[:, lane_block(s * RING + m, PIECE)] = (piece * gain).astype(BF)
    for s in range(RING):
        for m in range(RING):
            at = (s * RING + m) * PIECE
            back = ((RING - s) % RING * RING + (RING - m) % RING) * PIECE
            other_rows[:, at : at + PIECE] = own_rows[:, back : back + PIECE]
    for side, (rows, at) in enumerate(((own_rows, core), (other_rows, 1 - core))):
        total = None
        for s in range(RING):
            for copy in copies[side][s]:
                copy.wait()
            term = jnp.dot(
                rows[:, s * LANES : (s + 1) * LANES],
                weights[side, s].reshape(LANES, wide),
                preferred_element_type=F32,
            )
            total = term if total is None else total + term
        result[:, pl.ds(pl.multiple_of(at * wide, HEAD), wide)] = total
    scale = lax.rsqrt(squares * (1.0 / (TENSOR * LANES)) + epsilon)
    cosine, sine = cos_ref[...], sin_ref[...]
    heads = query_ref.shape[1] // HEAD
    for h in range(heads + 1):
        values = result[:, h * HEAD : (h + 1) * HEAD] * scale
        turned = (values * cosine + pltpu.roll(values, HEAD // 2, 1) * sine).astype(BF)
        if h < heads:
            query_ref[:, h * HEAD : (h + 1) * HEAD] = turned
        else:
            key_ref[...] = turned
    value_ref[...] = (result[:, (heads + 1) * HEAD :] * scale).astype(BF)


def project(place, rows, gain, cosine, sine, own, other):
    count = rows[0].shape[0]
    width = rows[0].shape[1]
    return pl.pallas_call(
        project_kernel,
        out_shape=(
            jax.ShapeDtypeStruct((count, width), BF),
            jax.ShapeDtypeStruct((count, HEAD), BF),
            jax.ShapeDtypeStruct((count, HEAD), BF),
        ),
        in_specs=[in_smem()] + [in_vmem()] * 7 + [anywhere()] * 24,
        out_specs=(in_vmem(),) * 3,
        scratch_shapes=[
            pltpu.VMEM((count, TENSOR * width), BF),
            pltpu.VMEM((count, TENSOR * width), BF),
            pltpu.VMEM((count, width + 2 * HEAD), F32),
        ]
        + weight_space((width + 2 * HEAD) // 2),
        compiler_params=params(),
        name="project",
    )(place, *rows, gain, cosine, sine, *own, *other)


def attend_kernel(first_pair, pairs, place_ref, lens_ref, q_ref, k_ref, v_ref, *refs):
    own_refs, other_refs = refs[:12], refs[12:24]
    out_refs = refs[24:28]
    mixed, terms, weights, sems = refs[28:32]
    copies = fetch(own_refs, other_refs, (q_ref.shape[1] + 2 * HEAD) // 2, weights, sems)
    x, z, y, core, way = place_of(place_ref)
    slots = 2 * SAMPLE
    heads = q_ref.shape[1] // HEAD
    step_t = lax.broadcasted_iota(jnp.int32, (slots, slots), 0)
    step_u = lax.broadcasted_iota(jnp.int32, (slots, slots), 1)
    for p in range(pairs):
        at = slice(p * slots, (p + 1) * slots)
        stacked = jnp.concatenate(
            [q_ref[at, h * HEAD : (h + 1) * HEAD] for h in range(heads)], axis=0
        )
        scores = lax.dot_general(
            stacked, k_ref[at, :], (((1,), (1,)), ((), ())), preferred_element_type=F32
        ) * (HEAD**-0.5)
        len_a = lens_ref[2 * (first_pair + p)]
        len_b = lens_ref[2 * (first_pair + p) + 1]
        limit = jnp.where(step_u < SAMPLE, len_a, len_b + SAMPLE)
        limit = jnp.minimum(limit, step_t + 1)
        closed = jnp.where(step_u < limit, 0.0, -1e30).astype(F32)
        scores = scores.reshape(heads, slots, slots) + closed[None]
        peak = jnp.max(scores, axis=-1, keepdims=True)
        raised = jnp.exp(scores - peak)
        probs = raised / jnp.sum(raised, axis=-1, keepdims=True)
        out = jnp.dot(
            probs.astype(BF).reshape(heads * slots, slots),
            v_ref[at, :],
            preferred_element_type=F32,
        ).astype(BF)
        for h in range(heads):
            mixed[at, h * HEAD : (h + 1) * HEAD] = out[h * slots : (h + 1) * slots]
    depth = 2 * PIECE
    mine = mixed[:, lane_block(core, depth)]
    theirs = mixed[:, lane_block(1 - core, depth)]
    for side in copies:
        for step in side:
            for copy in step:
                copy.wait()

    def product(values, side, s, m):
        block = weights[side, s, 2 * m : 2 * m + 2].reshape(PIECE, depth)
        return jnp.dot(values[:, :PIECE], block[:, :PIECE], preferred_element_type=F32) + jnp.dot(
            values[:, PIECE:], block[:, PIECE:], preferred_element_type=F32
        )

    for s in range(RING):
        r = wrap((y - wrap(x - s * way)) * way)
        for m in range(RING):
            part = wrap(z - m * way)
            term = product(mine, 0, s, m) + product(
                theirs, 1, (RING - s) % RING, (RING - m) % RING
            )
            terms[r, :, lane_block(part, PIECE)] = term.astype(BF)
    for r in range(RING):
        out_refs[r][...] = terms[r]


def attend(first_pair, pairs, place, lens, qkv, own, other):
    count = pairs * 2 * SAMPLE
    width = qkv[0].shape[1]

    def kernel(*refs):
        attend_kernel(first_pair, pairs, *refs)

    return pl.pallas_call(
        kernel,
        out_shape=(jax.ShapeDtypeStruct((count, width), BF),) * RING,
        in_specs=[in_smem(), in_smem()] + [in_vmem()] * 3 + [anywhere()] * 24,
        out_specs=(in_vmem(),) * RING,
        scratch_shapes=[
            pltpu.VMEM((count, width), BF),
            pltpu.VMEM((RING, count, width), BF),
        ]
        + weight_space(2 * PIECE),
        compiler_params=params(),
        name="attend",
    )(place, lens, *qkv, *own, *other)


def finish_kernel(place_ref, gain_ref, b0, b1, b2, b3, *rest):
    out_ref = rest[-1]
    _, _, y, _, way = place_of(place_ref)
    values = [b[...].astype(F32) for b in (b0, b1, b2, b3)]
    squares = sum(jnp.sum(v * v, axis=-1, keepdims=True) for v in values)
    scale = lax.rsqrt(squares * (1.0 / (TENSOR * LANES)) + epsilon)
    for r in range(RING):
        lanes = lane_block(wrap(y - r * way), LANES)
        out_ref[:, lanes] = (values[r] * scale * gain_ref[:, lanes]).astype(BF)


def finish(place, gain, blocks, before, chunk, total):
    count, width = blocks[0].shape
    tile = 2 * SAMPLE
    steps = count // tile
    specs = [
        in_smem(),
        pl.BlockSpec((1, TENSOR * width), lambda i: (0, 0)),
    ] + [pl.BlockSpec((tile, width), lambda i: (i, 0))] * RING
    args = [place, gain, *blocks]
    aliases = {}
    if before is not None:
        specs.append(pl.BlockSpec(memory_space=pl.ANY))
        aliases = {len(args): 0}
        args.append(before)
    return pl.pallas_call(
        finish_kernel,
        grid=(steps,),
        out_shape=jax.ShapeDtypeStruct((total, TENSOR * width), BF),
        in_specs=specs,
        out_specs=pl.BlockSpec((tile, TENSOR * width), lambda i: (i + chunk * steps, 0)),
        input_output_aliases=aliases,
        compiler_params=params(),
        name="finish",
    )(*args)


def after(value, *others):
    return pl.pallas_call(
        lambda *refs: None,
        out_shape=jax.ShapeDtypeStruct(value.shape, value.dtype),
        in_specs=[anywhere()] * (1 + len(others)),
        out_specs=anywhere(),
        input_output_aliases={0: 0},
        name="after",
    )(value, *others)


def way_of(dp):
    return 1 - 2 * (dp % 2)


def along_y(values):
    pairs = [
        (dp * TENSOR + y, dp * TENSOR + (y + way_of(dp)) % TENSOR)
        for dp in range(4)
        for y in range(TENSOR)
    ]
    return lax.ppermute(values, ("dp", "tensor"), pairs)


def along_x(values):
    pairs = [
        (dp * 16 + x * 4 + z, dp * 16 + (x + way_of(dp)) % 4 * 4 + z)
        for dp in range(4)
        for x in range(4)
        for z in range(4)
    ]
    return lax.ppermute(values, ("dp", "fsdp"), pairs)


def along_z(values):
    pairs = [
        (dp * 16 + x * 4 + z, dp * 16 + x * 4 + (z + way_of(dp)) % 4)
        for dp in range(4)
        for x in range(4)
        for z in range(4)
    ]
    return lax.ppermute(values, ("dp", "fsdp"), pairs)


def other_core(values):
    return lax.ppermute(values, "dp", [(dp, dp ^ 1) for dp in range(4)])


def spread_x(rounds):
    own = [None] * 12
    for g, (start, stop) in enumerate(GROUPS):
        block = jnp.stack([half for step in rounds[start:stop] for half in step])
        for s in range(4):
            own[3 * s + g] = block
            if s < 3:
                block = along_x(block)
    return own


def on_device(
    candidates, cand_lengths, pairing, attn_gain, w_query, w_key, w_value, w_out, ffn_gain
):
    me = lax.axis_index("fsdp")
    y = lax.axis_index("tensor")
    core = lax.rem(lax.axis_index("dp"), 2)
    place = jnp.stack([me // 4, lax.rem(me, 4), y, core]).astype(jnp.int32)
    cand_dev = candidates.shape[1]
    devices = lax.axis_size("fsdp")
    flat = pairing[0].reshape(devices, cand_dev)
    pick = jnp.sum(jnp.where(flat // cand_dev == me, lax.rem(flat, cand_dev), 0), axis=1)
    wanted = lax.dynamic_index_in_dim(flat, me, 0, keepdims=False)
    source = wanted // cand_dev

    half_cols = (w_query.shape[1] + w_key.shape[1] + w_value.shape[1]) // 2
    first = w_query[:, :half_cols]
    second = jnp.concatenate([w_query[:, half_cols:], w_key, w_value], axis=1)
    depth = w_out.shape[0] // 2
    third = jnp.where(core == 0, w_out[:depth], w_out[depth:])
    piece = jnp.concatenate(
        [jnp.where(core == 0, first, second), third[: depth // 2], third[depth // 2 :]], axis=1
    )
    rounds = [[piece[: PIECE // 2], piece[PIECE // 2 :]]]
    for _ in range(3):
        rounds.append([along_z(half) for half in rounds[-1]])
    own = spread_x(rounds)

    packed = pack(pick, cand_lengths[0], candidates[0], (*rounds[3], own[7], own[9]), devices)
    incoming = lax.all_to_all(packed, "fsdp", split_axis=0, concat_axis=0, tiled=True)
    parts = 2
    pairs = cand_dev // 2 // parts
    local = unpack(source, incoming, (), parts)
    other = [other_core(block) for block in own]
    sent = incoming[:, -1, 0].astype(F32)
    slots = jnp.arange(devices, dtype=jnp.int32)
    lens = jnp.sum(
        jnp.where(source[:, None] == slots[None, :], sent[None, :], 0.0), axis=1
    ).astype(jnp.int32)


    gain_in = attn_gain.reshape(1, -1)
    gain_out = ffn_gain.reshape(1, -1)
    freq = rope_base ** (-jnp.arange(HEAD // 2, dtype=F32) * 2.0 / HEAD)
    starts = jnp.where(jnp.arange(cand_dev) % 2 == 0, 0, jnp.roll(lens, 1))
    positions = starts[:, None] + jnp.arange(SAMPLE, dtype=jnp.int32)[None, :]
    angles = positions.reshape(parts, -1, 1).astype(F32) * freq
    cosine, sine = jnp.cos(angles), jnp.sin(angles)
    cosine = jnp.concatenate([cosine, cosine], axis=2)
    sine = jnp.concatenate([-sine, sine], axis=2)

    width = candidates.shape[3]
    total = cand_dev * SAMPLE
    normed = None
    resids = []
    rings = [[rows] for rows in local]
    for _ in range(3):
        for ring in rings:
            ring.append(along_y(ring[-1]))
    for c in range(parts):
        ring = rings[c]
        qkv = project(place, ring, gain_in, cosine[c], sine[c], own, other)
        terms = attend(c * pairs, pairs, place, lens, qkv, own, other)
        moving = along_y(terms[1])
        for r in (2, 3):
            moving = along_y((moving.astype(F32) + terms[r].astype(F32)).astype(BF))
        stream = local[c].astype(F32) + terms[0].astype(F32) + moving.astype(F32)
        blocks = [stream.astype(BF)]
        for _ in range(3):
            blocks.append(along_y(blocks[-1]))
        resids.append(blocks[0])
        normed = finish(place, gain_out, blocks, normed, c, total)
    resid = jnp.concatenate(resids, axis=0)
    pair_dev = cand_dev // 2
    return (
        resid.reshape(1, pair_dev, 2 * SAMPLE, width),
        normed.reshape(1, pair_dev, 2 * SAMPLE, TENSOR * width),
    )


def solution(mesh):
    return jax.shard_map(
        on_device,
        mesh=mesh,
        in_specs=(
            P("dp", "fsdp", None, "tensor"),
            P("dp", "fsdp"),
            P("dp", None, None),
            P(),
            P("fsdp", "tensor"),
            P("fsdp", "tensor"),
            P("fsdp", "tensor"),
            P("tensor", "fsdp"),
            P(),
        ),
        out_specs=(P("dp", "fsdp", None, "tensor"), P("dp", "fsdp", None, None)),
        check_vma=False,
    )
```
